32 devices in a mesh: grp: 2 (over x), tm: 8 (over z, y), bus: 2 (over core).
Axes of the slice: x: 2, y: 2, z: 4, core: 2. Of those that a mesh axis runs over, the one named last changes fastest.
Arguments:
- network: float32 [2048, 2048], P('bus'), may hold values from -0.125 to 0.125
- upper_bound: float32 [2048], P('bus'), may hold values from 0.5 to 2
- build_cost: float32 [2048], P('bus'), may hold values from 0.5 to 8
- unit_cost: float32 [512, 2048], P(('grp', 'tm'), 'bus'), parts along dimension 0, may hold values from -6 to 6
- demand: float32 [512, 2048], P(('grp', 'tm'), 'bus'), parts along dimension 0, may hold values from -6 to 6
- inflow: float32 [4096], P(('grp', 'bus')), parts along dimension 0, may hold values from 0.05 to 1
- primal_start: float32 [512, 2048], P(('grp', 'tm'), 'bus'), parts along dimension 0, may hold values from 0 to 1
- network_start: float32 [512, 2048], P(('grp', 'tm'), 'bus'), parts along dimension 0, may hold values from 0 to 1
- energy_start: float32 [512, 2048], P(('grp', 'tm'), 'bus'), parts along dimension 0, may hold values from 0 to 1
- build_start: float32 [4096], P(('grp', 'bus')), parts along dimension 0, may hold values from 0 to 2
- accepted: int32 [16], P('grp'), parts along dimension 0, may hold values from 0 to 1
- restarts: int32 [16], P('grp'), parts along dimension 0, may hold values from 0 to 1
Outputs:
- primal_final: float32 [512, 2048], P(('grp', 'tm'), 'bus'), parts along dimension 0
- network_final: float32 [512, 2048], P(('grp', 'tm'), 'bus'), parts along dimension 0
- energy_final: float32 [512, 2048], P(('grp', 'tm'), 'bus'), parts along dimension 0
- build_final: float32 [4096], P(('grp', 'bus')), parts along dimension 0
The draws below stay inside these ranges and needn't reach their ends.
There are 2 independent parts, one for each index of `grp`. The reference program is written for one: setup_inputs(seed, part) draws one part's arguments, and reference() takes and returns one part's arrays. A program takes and returns all parts, laid end to end along the dimension named above; an argument that names none is the same for every part. Nothing has to cross between parts.
Inputs may be any that keep to these rules, and one draw needn't show every extreme that they name: `accepted`: A flag, 0 or 1, for each iteration after the first. `restarts`: A flag, 0 or 1, for each iteration after the first.
All inputs are finite; a program needn't handle non-finite values.
Results may differ from the reference program's by a relative error of at most 0.00013.
Values sent between devices are 32-bit elements; how exact they have to be, the bound alone decides.
No kernel may reach another device: no remote copies, remote signals or barrier semaphores. Data moves between devices by JAX's collectives and lax.ppermute only.
A program may use at most 128 MiB of HBM per device.

```python
import math
import jax
import jax.numpy as jnp
from jax import lax

W = 2048
ITERS = 9
MEM = 5
HOURS = 256


def with_ends(values, stream_key, low, largest):
    index_at = [jax.random.randint(jax.random.fold_in(stream_key, axis), (), 0, length) for axis, length in enumerate(values.shape)]
    main_axis = values.shape.index(max(values.shape))
    neighbour = index_at[:main_axis] + [(index_at[main_axis] + 1) % values.shape[main_axis]] + index_at[main_axis + 1:]
    return values.at[tuple(index_at)].set(low).at[tuple(neighbour)].set(largest)


def steps_of(key, shape, pieces, low, high):
    gain, own = 1.0, jax.random.fold_in(key, 6)
    for position, parts in pieces:
        heights = jnp.exp(jax.random.uniform(jax.random.fold_in(own, position), (parts,), jnp.float32, low / len(pieces), high / len(pieces)))
        gain = gain * jnp.repeat(heights, shape[position] // parts).reshape([-1 if axis == position else 1 for axis in range(len(shape))])
    return gain


def gaussian(stream_key, extent, scale, most, cuts=(), kind=jnp.bfloat16):
    values = scale * jax.random.normal(stream_key, extent, jnp.float32)
    if cuts:
        values = values * steps_of(stream_key, extent, cuts, -0.22, 0.18)
    return jnp.clip(values, -most, most).astype(kind)


def setup_inputs(seed: int = 0, part: int = 0) -> dict:
    streams_of = jax.random.split(jax.random.key(seed), 13)
    part_keys = jax.random.split(jax.random.fold_in(streams_of[12], part), 13)
    network = gaussian(streams_of[0], (W, W), W ** -0.5, 0.125, ((0, 2),), jnp.float32)
    upper_bound = jnp.clip(0.5 + 1.5 * jax.random.uniform(streams_of[1], (W,), jnp.float32) ** steps_of(streams_of[1], (W,), ((0, 2),), -0.2, 0.2), 0.5, 2.0)
    build_cost = jnp.clip(jnp.exp(math.log(8.0) - 2.7725887 * jax.random.uniform(streams_of[2], (W,), jnp.float32) ** steps_of(streams_of[2], (W,), ((0, 2),), -0.2, 0.2)), 0.5, 8.0)
    unit_cost = gaussian(part_keys[3], (HOURS, W), 1.0, 6.0, ((0, 8), (1, 2)), jnp.float32)
    demand = gaussian(part_keys[4], (HOURS, W), 1.0, 6.0, ((0, 8), (1, 2)), jnp.float32)
    inflow = jnp.clip(0.05 + 0.95 * jax.random.uniform(part_keys[5], (W,), jnp.float32) ** steps_of(part_keys[5], (W,), ((0, 2),), -0.2, 0.2), 0.05, 1.0)
    primal_start = jnp.clip(1.0 * jax.random.uniform(part_keys[6], (HOURS, W), jnp.float32) ** steps_of(part_keys[6], (HOURS, W), ((0, 8), (1, 2)), -0.2, 0.2), 0.0, 1.0)
    network_start = jnp.clip(1.0 * jax.random.uniform(part_keys[7], (HOURS, W), jnp.float32) ** steps_of(part_keys[7], (HOURS, W), ((0, 8), (1, 2)), -0.2, 0.2), 0.0, 1.0)
    energy_start = jnp.clip(1.0 * jax.random.uniform(part_keys[8], (HOURS, W), jnp.float32) ** steps_of(part_keys[8], (HOURS, W), ((0, 8), (1, 2)), -0.2, 0.2), 0.0, 1.0)
    build_start = jnp.clip(2.0 * jax.random.uniform(part_keys[9], (W,), jnp.float32) ** steps_of(part_keys[9], (W,), ((0, 2),), -0.2, 0.2), 0.0, 2.0)
    accepted = with_ends(jax.random.randint(part_keys[10], (ITERS - 1,), 0, 2), jax.random.fold_in(part_keys[10], 1), 0, 1).astype(jnp.int32)
    restarts = with_ends(jax.random.randint(part_keys[11], (ITERS - 1,), 0, 2), jax.random.fold_in(part_keys[11], 1), 0, 1).astype(jnp.int32)
    return dict(network=network, upper_bound=upper_bound, build_cost=build_cost, unit_cost=unit_cost, demand=demand, inflow=inflow, primal_start=primal_start, network_start=network_start, energy_start=energy_start, build_start=build_start, accepted=accepted, restarts=restarts)


primal_step = 0.3
dual_step = 0.3
highest = lax.Precision.HIGHEST


def solve_small(matrix, vector):
    size_n = vector.shape[0]
    entries = [[matrix[i, j] for j in range(size_n)] for i in range(size_n)]
    values = [vector[i] for i in range(size_n)]
    for p in range(size_n):
        for i in range(p + 1, size_n):
            factor = entries[i][p] / entries[p][p]
            for j in range(p, size_n):
                entries[i][j] = entries[i][j] - factor * entries[p][j]
            values[i] = values[i] - factor * values[p]
    result = [values[0]] * size_n
    for i in range(size_n - 1, -1, -1):
        running_value = values[i]
        for j in range(i + 1, size_n):
            running_value = running_value - entries[i][j] * result[j]
        result[i] = running_value / entries[i][i]
    return jnp.stack(result)


def mixing_weights(gram_matrix, right_side, active):
    column_count = right_side.shape[0]
    active_pairs = active[:, None] * active[None, :]
    trace_sum = jnp.sum(jnp.diagonal(gram_matrix) * active)
    shift_amount = 0.001 * trace_sum / column_count + 1e-6
    system = gram_matrix * active_pairs + jnp.diag(1.0 - active) + shift_amount * jnp.eye(column_count, dtype=jnp.float32)
    return solve_small(system, right_side * active) * active


def pdhg_map(state, network, upper_bound, build_cost, unit_cost, demand, inflow):
    primal, net_dual, energy_dual, build_level = state
    hour_count = primal.shape[0]
    weight = (1.0 / (jnp.arange(hour_count) + 1).astype(jnp.float32))[:, None]
    scaled = energy_dual * weight
    remaining = jnp.cumsum(scaled[::-1], axis=0)[::-1]
    column_total = jnp.sum(scaled, axis=0)
    pulled = jnp.dot(net_dual, network, precision=highest)
    next_primal = jnp.clip(primal - primal_step * (unit_cost - pulled + remaining), 0.0, upper_bound)
    next_build = jnp.maximum(build_level - primal_step * (build_cost - column_total), 0.0)
    bar_primal = 2.0 * next_primal - primal
    bar_build = 2.0 * next_build - build_level
    pushed = lax.dot_general(bar_primal, network, (((1,), (1,)), ((), ())), precision=highest)
    running = jnp.cumsum(bar_primal, axis=0)
    next_net = jnp.maximum(net_dual + dual_step * (demand - pushed), 0.0)
    next_energy = jnp.maximum(energy_dual + dual_step * (-inflow - (bar_build - running) * weight), 0.0)
    return (next_primal, next_net, next_energy, next_build)


def inner_full(first, second):
    subtotal = jnp.sum(first[0] * second[0]) + jnp.sum(first[1] * second[1]) + jnp.sum(first[2] * second[2])
    return subtotal + jnp.sum(first[3] * second[3])


def reference(network, upper_bound, build_cost, unit_cost, demand, inflow, primal_start, network_start, energy_start, build_start, accepted, restarts):
    state = (primal_start, network_start, energy_start, build_start)
    totals = tuple(jnp.zeros_like(member) for member in state)
    counter = jnp.zeros((), jnp.float32)
    delta_maps = []
    delta_resid = []
    active = []
    last_map = state
    last_resid = state
    restart_flag = jnp.zeros((), jnp.float32)
    for iteration in range(ITERS):
        if iteration > 0:
            restart_flag = restarts[iteration - 1].astype(jnp.float32)
            state = tuple(restart_flag * (summed / counter) + (1.0 - restart_flag) * member for summed, member in zip(totals, state))
            totals = tuple((1.0 - restart_flag) * summed for summed in totals)
            counter = (1.0 - restart_flag) * counter
        mapped = pdhg_map(state, network, upper_bound, build_cost, unit_cost, demand, inflow)
        residual = tuple(m - z for m, z in zip(mapped, state))
        if iteration == 0:
            following = mapped
        else:
            keep_flag = 1.0 - restart_flag
            active = [old_flag * keep_flag for old_flag in active] + [keep_flag]
            delta_maps.append(tuple(m - z for m, z in zip(mapped, last_map)))
            delta_resid.append(tuple(m - z for m, z in zip(residual, last_resid)))
            if len(delta_resid) > MEM:
                delta_maps.pop(0)
                delta_resid.pop(0)
                active.pop(0)
            size_n = len(delta_resid)
            gram_matrix = jnp.stack([jnp.stack([inner_full(delta_resid[i], delta_resid[j]) for j in range(size_n)]) for i in range(size_n)])
            right_side = jnp.stack([inner_full(column, residual) for column in delta_resid])
            mix_weights = mixing_weights(gram_matrix, right_side, jnp.stack(active))
            accept_flag = accepted[iteration - 1].astype(jnp.float32)
            following = []
            for b in range(4):
                correction = jnp.zeros_like(mapped[b])
                for j in range(size_n):
                    correction = correction + mix_weights[j] * delta_maps[j][b]
                following.append(mapped[b] - accept_flag * correction)
            following = tuple(following)
        last_map = mapped
        last_resid = residual
        state = following
        totals = tuple(summed + member for summed, member in zip(totals, state))
        counter = counter + 1.0
    return state
```

```python
import jax
import jax.numpy as jnp
from jax import lax
from jax.experimental import pallas as pl
from jax.experimental.pallas import tpu as pltpu
from jax.sharding import PartitionSpec as P

ITERS = 9
MEM = 5
LANES = 128
ROWS = 16

primal_step = 0.3
dual_step = 0.3
f32 = jnp.float32
bf16 = jnp.bfloat16


def shape(*dims, dtype=f32):
    return jax.ShapeDtypeStruct(dims, dtype)


def run(name, body, ins, outs):
    keys = list(ins)
    out_keys = list(outs)

    def kernel(*refs):
        body(dict(zip(keys + out_keys, refs)))

    def space(key):
        return pl.BlockSpec(memory_space=pltpu.SMEM if key == "flags" else pltpu.VMEM)

    results = pl.pallas_call(
        kernel,
        out_shape=[outs[key] for key in out_keys],
        in_specs=[space(key) for key in keys],
        out_specs=[space(key) for key in out_keys],
        compiler_params=pltpu.CompilerParams(vmem_limit_bytes=40 * 1024 * 1024),
        name=name,
    )(*[ins[key] for key in keys])
    return dict(zip(out_keys, results))


def listed(prefix, arrays):
    return {f"{prefix}{i}": array for i, array in enumerate(arrays)}


def lane_blocks(width):
    return [slice(j * LANES, (j + 1) * LANES) for j in range(width // LANES)]


def row_iota(rows):
    return lax.broadcasted_iota(jnp.int32, (rows, LANES), 0)


def running_sum(block):
    rows = block.shape[0]
    at = row_iota(rows)
    step = 1
    while step < rows:
        block = block + jnp.where(at >= step, pltpu.roll(block, step, 0), 0.0)
        step *= 2
    return block


def tail_sum(block):
    rows = block.shape[0]
    at = row_iota(rows)
    step = 1
    while step < rows:
        block = block + jnp.where(at < rows - step, pltpu.roll(block, rows - step, 0), 0.0)
        step *= 2
    return block


def to_tile(block):
    rows = block.shape[0]
    total = block[0:8]
    for i in range(8, rows, 8):
        total = total + block[i : i + 8]
    return total


def product(left, high, low, transposed):
    rows = left.shape[0]
    dims = (((1,), (1 if transposed else 0,)), ((), ()))
    left_high = left.astype(bf16)
    left_low = (left - left_high.astype(f32)).astype(bf16)
    both = lax.dot_general(
        jnp.concatenate([left_high, left_low], axis=0), high, dims, preferred_element_type=f32
    )
    rest = lax.dot_general(left_high, low, dims, preferred_element_type=f32)
    return both[:rows] + (both[rows:] + rest)


def split_network(network, bus):
    rows, units = network.shape
    width = units // 2
    step = min(256, rows)

    def kernel(_, source, high, low):
        value = source[...]
        rounded = value.astype(bf16)
        high[0] = rounded
        low[0] = (value - rounded.astype(f32)).astype(bf16)

    part = pl.BlockSpec((1, step, width), lambda i, j, b: (j, i, 0))
    return pl.pallas_call(
        kernel,
        out_shape=[shape(2, rows, width, dtype=bf16)] * 2,
        grid_spec=pltpu.PrefetchScalarGridSpec(
            num_scalar_prefetch=1,
            grid=(rows // step, 2),
            in_specs=[pl.BlockSpec((step, width), lambda i, j, b: (i, (b[0] + j) % 2))],
            out_specs=[part, part],
        ),
        compiler_params=pltpu.CompilerParams(vmem_limit_bytes=40 * 1024 * 1024),
        name="split_network",
    )(bus, network)


def solve_rows(entries, values):
    size_n = len(values)
    entries = [list(row) for row in entries]
    values = list(values)
    for p in range(size_n):
        for i in range(p + 1, size_n):
            factor = entries[i][p] / entries[p][p]
            for j in range(p + 1, size_n):
                entries[i][j] = entries[i][j] - factor * entries[p][j]
            values[i] = values[i] - factor * values[p]
    result = [None] * size_n
    for i in range(size_n - 1, -1, -1):
        value = values[i]
        for j in range(i + 1, size_n):
            value = value - entries[i][j] * result[j]
        result[i] = value / entries[i][i]
    return result


def on_device(
    network,
    upper_bound,
    build_cost,
    unit_cost,
    demand,
    inflow,
    primal_start,
    network_start,
    energy_start,
    build_start,
    accepted,
    restarts,
):
    tm_count, bus_count = lax.axis_size("tm"), lax.axis_size("bus")
    tm, bus = lax.axis_index("tm"), lax.axis_index("bus")
    hours, width = primal_start.shape
    blocks = lane_blocks(width)
    block_count = len(blocks)
    steps = accepted.shape[0]
    everyone = tm_count * bus_count
    flags = jnp.concatenate(
        [accepted, restarts, jnp.stack([tm, bus]).astype(jnp.int32)]
    )
    AT_TM, AT_BUS = 2 * steps, 2 * steps + 1
    member = shape(hours, width)
    line = shape(1, width)
    tile = shape(ROWS, LANES)
    message = shape(everyone, block_count + ROWS, LANES)

    upper_bound, build_cost, inflow, build_start = (
        value.reshape(1, width) for value in (upper_bound, build_cost, inflow, build_start)
    )
    high, low = split_network(network, bus.astype(jnp.int32).reshape(1))
    own_parts = dict(high=high[0], low=low[0])
    other_parts = dict(high=high[1], low=low[1])

    def flag(ref, index):
        return ref[index].astype(f32)

    def restart_of(ref, iteration):
        return flag(ref, steps + iteration - 1)

    def counter_of(ref, iteration):
        count = jnp.float32(1.0)
        for k in range(1, iteration):
            count = (1.0 - restart_of(ref, k)) * count + 1.0
        return count

    def active_of(ref, column, iteration):
        value = jnp.float32(1.0)
        for k in range(column, iteration + 1):
            value = value * (1.0 - restart_of(ref, k))
        return value

    def columns_at(iteration):
        return list(range(max(1, iteration - MEM + 1), iteration + 1))

    def swap(value):
        return lax.ppermute(value, "bus", [(i, (i + 1) % bus_count) for i in range(bus_count)])

    def from_before(value):
        return [
            lax.ppermute(value, "tm", [(i, (i + s) % tm_count) for i in range(tm_count)])
            for s in range(1, tm_count)
        ]

    def to_all(value):
        return lax.all_to_all(value, ("tm", "bus"), 0, 0, tiled=True)


    def write_message(r, total_row, pairs):
        rows = [total_row[:, sl] for sl in blocks]
        for d in range(everyone):
            for j, row in enumerate(rows):
                r["message"][d, j : j + 1, :] = row
            r["message"][d, block_count:, :] = pairs

    def mixing(r, iteration):
        columns = columns_at(iteration)
        size_n = len(columns)
        summed = {}
        for k in columns[:-1]:
            summed[k] = r[f"pairs{k}"][...]
        newest = r["message"][0, block_count:, :]
        for d in range(1, everyone):
            newest = newest + r["message"][d, block_count:, :]
        newest = jnp.broadcast_to(jnp.sum(newest, axis=1, keepdims=True), (ROWS, LANES))
        r["pairs"][...] = newest
        summed[iteration] = newest
        active = [active_of(r["flags"], k, iteration) for k in columns]

        def entry(i, j):
            i, j = max(i, j), min(i, j)
            at = columns_at(columns[i]).index(columns[j])
            return summed[columns[i]][at : at + 1]

        gram = [[entry(i, j) for j in range(size_n)] for i in range(size_n)]
        trace = gram[0][0] * active[0]
        for i in range(1, size_n):
            trace = trace + gram[i][i] * active[i]
        shift = 0.001 * trace / size_n + 1e-06
        system = [
            [gram[i][j] * (active[i] * active[j]) for j in range(size_n)] for i in range(size_n)
        ]
        for i in range(size_n):
            system[i][i] = system[i][i] + (1.0 - active[i]) + shift
        right = [newest[8 + i : 9 + i] * active[i] for i in range(size_n)]
        mix = solve_rows(system, right)
        accept = flag(r["flags"], iteration - 1)
        return [accept * (value * a) for value, a in zip(mix, active)]

    def mixed(mapped, deltas, coefs):
        if not coefs:
            return mapped
        correction = coefs[0] * deltas[0]
        for coef, delta in zip(coefs[1:], deltas[1:]):
            correction = correction + coef * delta
        return mapped - correction

    def restarted(flags_ref, iteration, following, total):
        if iteration == 0:
            return following, jnp.zeros_like(following)
        restart = restart_of(flags_ref, iteration)
        total = following if total is None else total + following
        mean = total / counter_of(flags_ref, iteration)
        return jnp.where(restart > 0.5, mean, following), (1.0 - restart) * total


    def first_body(r):
        weight_at = tm_weight(r)
        totals = []
        for sl in blocks:
            tail = tail_sum(r["energy"][:, sl] * weight_at)
            r["tail"][:, sl] = tail
            totals.append(tail[0:1])
        write_message(r, jnp.concatenate(totals, axis=1), jnp.zeros((ROWS, LANES), f32))

    def tm_weight(r):
        at = r["flags"][AT_TM] * hours + row_iota(hours) + 1
        return 1.0 / at.astype(f32)

    def primal_body(k):
        olds = columns_at(k - 1)[:-1] if k >= 2 else []
        count = len(columns_at(k - 1)) if k >= 2 else 0

        def body(r):
            coefs = mixing(r, k - 1) if k >= 2 else []
            for i, coef in enumerate(coefs):
                r["coefs"][i : i + 1, :] = coef
            my_tm, my_bus = r["flags"][AT_TM], r["flags"][AT_BUS]
            later = jnp.zeros((block_count, LANES), f32)
            whole = jnp.zeros((block_count, LANES), f32)
            for s in range(tm_count):
                piece = r["message"][s * bus_count + my_bus, :block_count, :]
                whole = whole + piece
                later = later + jnp.where(s > my_tm, piece, 0.0)
            for j, sl in enumerate(blocks):

                def step(name, mapped, old_count, keep_delta):
                    deltas = [r[f"{name}_old{i}"][:, sl] for i in range(old_count)]
                    if keep_delta and count:
                        newest = mapped - r[f"{name}_last"][:, sl]
                        r[f"{name}_delta"][:, sl] = newest
                        deltas.append(newest)
                    following = mixed(mapped, deltas, coefs)
                    total = r[f"{name}_total"][:, sl] if k >= 2 else None
                    state, total = restarted(r["flags"], k, following, total)
                    if k >= 1:
                        r[f"{name}_sum"][:, sl] = total
                    return state

                slope = (r["pulled_own"][:, sl] + r["pulled_other"][:, sl]) - (
                    r["tail"][:, sl] + later[j : j + 1]
                )
                r["slope_map"][:, sl] = slope
                slope = step("slope", slope, len(olds), True)
                column = whole[j : j + 1]
                r["column_map"][:, sl] = column
                column = step("column", column, len(olds), True)
                primal = step("primal", r["primal_mapped"][:, sl], count, False)
                build = step("build", r["build_mapped"][:, sl], count, False)
                next_primal = jnp.clip(
                    primal - primal_step * (r["unit_cost"][:, sl] - slope),
                    0.0,
                    r["upper_bound"][:, sl],
                )
                next_build = jnp.maximum(
                    build - primal_step * (r["build_cost"][:, sl] - column), 0.0
                )
                bar = 2.0 * next_primal - primal
                r["primal"][:, sl] = primal
                r["build"][:, sl] = build
                r["next_primal"][:, sl] = next_primal
                r["next_build"][:, sl] = next_build
                r["bar"][:, sl] = bar
                r["block"][:, sl] = jnp.sum(bar, axis=0, keepdims=True)

        return body

    def pair_sums(pairs, olds, newest, residual):
        for i, column in enumerate(olds + [newest]):
            for row, other in ((i, newest), (8 + i, residual)):
                term = to_tile(column * other)
                pairs[row] = pairs[row] + term if row in pairs else term

    def pair_tile(pairs, before=None):
        rows = []
        for i in range(ROWS):
            if i in pairs:
                rows.append(jnp.sum(pairs[i], axis=0, keepdims=True))
            else:
                rows.append(jnp.zeros((1, LANES), f32))
        result = jnp.concatenate(rows, axis=0)
        return result if before is None else result + before

    def note(r, name, k, sl, mapped, state, pairs, scale=None):
        residual = mapped - state
        r[f"{name}_resid"][:, sl] = residual
        if k == 0:
            return
        r[f"{name}_delta"][:, sl] = mapped - r[f"{name}_last"][:, sl]
        newest = residual - r[f"{name}_resid_last"][:, sl]
        r[f"{name}_column"][:, sl] = newest
        olds = [r[f"{name}_column_old{i}"][:, sl] for i in range(len(columns_at(k)) - 1)]
        if scale is None:
            pair_sums(pairs, olds, newest, residual)
        else:
            for i, column in enumerate(olds + [newest]):
                for row, other in ((i, newest), (8 + i, residual)):
                    term = scale * (column * other)
                    key = ("line", row)
                    pairs[key] = pairs[key] + term if key in pairs else term

    def push_body(k):
        count = len(columns_at(k - 1)) if k >= 2 else 0

        def body(r):
            r["pushed"][...] = product(r["bar"][...], r["high"][...], r["low"][...], True)
            coefs = [r["coefs"][i : i + 1, :] for i in range(count)]
            pairs = {}
            for sl in blocks:
                for name in ("dual", "energy"):
                    deltas = [r[f"{name}_old{i}"][:, sl] for i in range(count)]
                    following = mixed(r[f"{name}_mapped"][:, sl], deltas, coefs)
                    total = r[f"{name}_total"][:, sl] if k >= 2 else None
                    state, total = restarted(r["flags"], k, following, total)
                    r[name][:, sl] = state
                    if k >= 1:
                        r[f"{name}_sum"][:, sl] = total
                r["running"][:, sl] = running_sum(r["bar"][:, sl])
                note(r, "primal", k, sl, r["next_primal"][:, sl], r["primal"][:, sl], pairs)
            r["pairs"][...] = pair_tile(pairs)

        return body

    def dual_body(k):
        def body(r):
            r["next_dual"][...] = r["pushed"][...] + product(
                r["bar_other"][...], r["high"][...], r["low"][...], True
            )
            pairs = {}
            for sl in blocks:
                dual = r["dual"][:, sl]
                next_dual = jnp.maximum(
                    dual + dual_step * (r["demand"][:, sl] - r["next_dual"][:, sl]), 0.0
                )
                r["next_dual"][:, sl] = next_dual
                note(r, "dual", k, sl, next_dual, dual, pairs)
            r["pairs"][...] = pair_tile(pairs, r["pairs_before"][...])

        return body

    def energy_body(k):
        def body(r):
            my_tm = r["flags"][AT_TM]
            weight_at = tm_weight(r)
            own_build = (my_tm == 0).astype(f32)
            pairs, totals = {}, []
            for sl in blocks:
                earlier = jnp.zeros((1, LANES), f32)
                for s in range(1, tm_count):
                    earlier = earlier + jnp.where(my_tm >= s, r[f"before{s - 1}"][:, sl], 0.0)
                running = r["running"][:, sl] + earlier
                energy = r["energy"][:, sl]
                build, next_build = r["build"][:, sl], r["next_build"][:, sl]
                bar_build = 2.0 * next_build - build
                next_energy = jnp.maximum(
                    energy
                    + dual_step * (-r["inflow"][:, sl] - (bar_build - running) * weight_at),
                    0.0,
                )
                r["next_energy"][:, sl] = next_energy
                tail = tail_sum(next_energy * weight_at)
                r["tail"][:, sl] = tail
                totals.append(tail[0:1])
                note(r, "energy", k, sl, next_energy, energy, pairs)
                note(r, "build", k, sl, next_build, build, pairs, own_build)
            lines = [
                pairs.get(("line", i), jnp.zeros((1, LANES), f32)) for i in range(ROWS)
            ]
            tile_here = pair_tile(pairs, r["pairs_before"][...]) + jnp.concatenate(lines, axis=0)
            write_message(r, jnp.concatenate(totals, axis=1), tile_here)

        return body

    def pull_body(r):
        r["pulled"][...] = product(r["dual"][...], r["high"][...], r["low"][...], False)

    def last_body(r):
        k = ITERS
        coefs = mixing(r, k - 1)
        for name in ("primal", "dual", "energy", "build"):
            for sl in blocks:
                deltas = [r[f"{name}_old{i}"][:, sl] for i in range(len(coefs))]
                r[name][:, sl] = mixed(r[f"{name}_mapped"][:, sl], deltas, coefs)


    names = ("primal", "dual", "energy", "build")
    kind = dict(primal=member, dual=member, energy=member, build=line, slope=member, column=line)
    mapped = dict(
        primal=primal_start, dual=network_start, energy=energy_start, build=build_start
    )
    deltas = {name: [] for name in kind}
    columns = {name: [] for name in names}
    totals, last_map, resid = {}, {}, {}
    pair_log = {}

    def pull(dual):
        out = run("pull_other", pull_body, dict(dual=dual, **other_parts), dict(pulled=member))
        arriving = swap(out["pulled"])
        out = run("pull_own", pull_body, dict(dual=dual, **own_parts), dict(pulled=member))
        return out["pulled"], arriving

    out = run(
        "first",
        first_body,
        dict(flags=flags, energy=energy_start),
        dict(tail=member, message=message),
    )
    tail = out["tail"]
    arrived = to_all(out["message"])
    pulled_own, pulled_other = pull(network_start)

    def column_inputs(name, k):
        if k == 0:
            return {}
        return {
            f"{name}_last": last_map[name],
            f"{name}_resid_last": resid[name],
            **listed(f"{name}_column_old", columns[name][-(MEM - 1) :]),
        }

    def column_outputs(name, k):
        outs = {f"{name}_resid": kind[name]}
        if k > 0:
            outs.update({f"{name}_delta": kind[name], f"{name}_column": kind[name]})
        return outs

    def take(name, k, out):
        resid[name] = out[f"{name}_resid"]
        if k > 0:
            deltas[name] = (deltas[name] + [out[f"{name}_delta"]])[-MEM:]
            columns[name] = (columns[name] + [out[f"{name}_column"]])[-MEM:]

    for k in range(ITERS):
        mixes = k >= 2
        ins = dict(
            flags=flags,
            message=arrived,
            pulled_own=pulled_own,
            pulled_other=pulled_other,
            tail=tail,
            primal_mapped=mapped["primal"],
            build_mapped=mapped["build"],
            unit_cost=unit_cost,
            upper_bound=upper_bound,
            build_cost=build_cost,
        )
        outs = dict(
            slope_map=member,
            column_map=line,
            primal=member,
            build=line,
            next_primal=member,
            next_build=line,
            bar=member,
            block=line,
        )
        if mixes:
            for j in columns_at(k - 1)[:-1]:
                ins[f"pairs{j}"] = pair_log[j]
            outs["pairs"] = tile
            outs["coefs"] = shape(8, LANES)
            for name in ("slope", "column"):
                ins[f"{name}_last"] = last_map[name]
                ins.update(listed(f"{name}_old", deltas[name][-(MEM - 1) :]))
                outs[f"{name}_delta"] = kind[name]
            for name in ("primal", "build"):
                ins.update(listed(f"{name}_old", deltas[name]))
            for name in ("slope", "column", "primal", "build"):
                ins[f"{name}_total"] = totals[name]
        if k >= 1:
            for name in ("slope", "column", "primal", "build"):
                outs[f"{name}_sum"] = kind[name]
        first = run(f"primal_{k}", primal_body(k), ins, outs)
        if mixes:
            pair_log[k - 1] = first["pairs"]
            for name in ("slope", "column"):
                deltas[name] = (deltas[name] + [first[f"{name}_delta"]])[-MEM:]
        last_map["slope"], last_map["column"] = first["slope_map"], first["column_map"]
        if k >= 1:
            for name in ("slope", "column", "primal", "build"):
                totals[name] = first[f"{name}_sum"]
        before = from_before(first["block"])
        bar_other = swap(first["bar"])

        ins = dict(
            flags=flags,
            bar=first["bar"],
            next_primal=first["next_primal"],
            primal=first["primal"],
            dual_mapped=mapped["dual"],
            energy_mapped=mapped["energy"],
            **own_parts,
            **column_inputs("primal", k),
        )
        outs = dict(
            pushed=member,
            dual=member,
            energy=member,
            running=member,
            pairs=tile,
            **column_outputs("primal", k),
        )
        if mixes:
            ins["coefs"] = first["coefs"]
            for name in ("dual", "energy"):
                ins.update(listed(f"{name}_old", deltas[name]))
                ins[f"{name}_total"] = totals[name]
        if k >= 1:
            for name in ("dual", "energy"):
                outs[f"{name}_sum"] = member
        second = run(f"push_{k}", push_body(k), ins, outs)
        if k >= 1:
            for name in ("dual", "energy"):
                totals[name] = second[f"{name}_sum"]

        third = run(
            f"dual_{k}",
            dual_body(k),
            dict(
                pushed=second["pushed"],
                bar_other=bar_other,
                dual=second["dual"],
                demand=demand,
                pairs_before=second["pairs"],
                **other_parts,
                **column_inputs("dual", k),
            ),
            dict(next_dual=member, pairs=tile, **column_outputs("dual", k)),
        )
        fourth = run(
            f"energy_{k}",
            energy_body(k),
            dict(
                flags=flags,
                running=second["running"],
                energy=second["energy"],
                build=first["build"],
                next_build=first["next_build"],
                inflow=inflow,
                pairs_before=third["pairs"],
                **listed("before", before),
                **column_inputs("energy", k),
                **column_inputs("build", k),
            ),
            dict(
                next_energy=member,
                tail=member,
                message=message,
                **column_outputs("energy", k),
                **column_outputs("build", k),
            ),
        )
        take("primal", k, second)
        take("dual", k, third)
        take("energy", k, fourth)
        take("build", k, fourth)
        mapped = dict(
            primal=first["next_primal"],
            dual=third["next_dual"],
            energy=fourth["next_energy"],
            build=first["next_build"],
        )
        last_map.update(mapped)
        tail = fourth["tail"]
        arrived = to_all(fourth["message"])
        if k < ITERS - 1:
            pulled_own, pulled_other = pull(mapped["dual"])

    ins = dict(flags=flags, message=arrived)
    for j in columns_at(ITERS - 1)[:-1]:
        ins[f"pairs{j}"] = pair_log[j]
    for name in names:
        ins[f"{name}_mapped"] = mapped[name]
        ins.update(listed(f"{name}_old", deltas[name]))
    out = run(
        "last", last_body, ins, dict(pairs=tile, **{name: kind[name] for name in names})
    )
    return out["primal"], out["dual"], out["energy"], out["build"].reshape(width)


def solution(mesh):
    hourly = P(("grp", "tm"), "bus")
    return jax.shard_map(
        on_device,
        mesh=mesh,
        in_specs=(
            P("bus", None),
            P("bus"),
            P("bus"),
            hourly,
            hourly,
            P(("grp", "bus")),
            hourly,
            hourly,
            hourly,
            P(("grp", "bus")),
            P("grp"),
            P("grp"),
        ),
        out_specs=(hourly, hourly, hourly, P(("grp", "bus"))),
        check_vma=False,
    )
```

```python
from types import SimpleNamespace as Space

import jax
import jax.numpy as jnp
from jax import lax
from jax.experimental import pallas as pl
from jax.experimental.pallas import tpu as pltpu
from jax.sharding import PartitionSpec as P

ITERS = 9
MEM = 5
LANES = 128
ROWS = 16
LIMIT = 10 * 1024 * 1024
X, Y, E, U, SLOPE, COLUMN = range(6)

primal_step = 0.3
dual_step = 0.3
f32 = jnp.float32
bf16 = jnp.bfloat16


def shape(*dims, dtype=f32):
    return jax.ShapeDtypeStruct(dims, dtype)


def run(body, ins, outs):
    in_leaves, in_tree = jax.tree.flatten(ins)
    out_leaves, out_tree = jax.tree.flatten(outs)

    def kernel(*refs):
        given = jax.tree.unflatten(in_tree, refs[: len(in_leaves)])
        made = jax.tree.unflatten(out_tree, refs[len(in_leaves) :])
        body(Space(**given), Space(**made))

    def place(leaf):
        return pl.BlockSpec(memory_space=pltpu.SMEM if leaf.dtype == jnp.int32 else pltpu.VMEM)

    results = pl.pallas_call(
        kernel,
        out_shape=out_leaves,
        in_specs=[place(leaf) for leaf in in_leaves],
        out_specs=[place(leaf) for leaf in out_leaves],
        compiler_params=pltpu.CompilerParams(vmem_limit_bytes=LIMIT),
        name=body.__name__,
    )(*in_leaves)
    return Space(**jax.tree.unflatten(out_tree, results))


def lane_blocks(width):
    return [slice(j * LANES, (j + 1) * LANES) for j in range(width // LANES)]


def row_iota(rows):
    return lax.broadcasted_iota(jnp.int32, (rows, LANES), 0)


def running_sum(block):
    rows = block.shape[0]
    at = row_iota(rows)
    step = 1
    while step < rows:
        block = block + jnp.where(at >= step, pltpu.roll(block, step, 0), 0.0)
        step *= 2
    return block


def tail_sum(block):
    rows = block.shape[0]
    at = row_iota(rows)
    step = 1
    while step < rows:
        block = block + jnp.where(at < rows - step, pltpu.roll(block, rows - step, 0), 0.0)
        step *= 2
    return block


def to_tile(block):
    rows = block.shape[0]
    total = block[0:8]
    for i in range(8, rows, 8):
        total = total + block[i : i + 8]
    return total


def product(left, high, low, transposed):
    rows = left.shape[0]
    dims = (((1,), (1 if transposed else 0,)), ((), ()))
    left_high = left.astype(bf16)
    left_low = (left - left_high.astype(f32)).astype(bf16)
    both = lax.dot_general(
        jnp.concatenate([left_high, left_low], axis=0), high, dims, preferred_element_type=f32
    )
    rest = lax.dot_general(left_high, low, dims, preferred_element_type=f32)
    return both[:rows] + (both[rows:] + rest)


def split_network(network, bus):
    rows, units = network.shape
    width = units // 2
    step = min(128, rows)

    def kernel(_, own, other, own_high, own_low, other_high, other_low):
        for source, high, low in ((own, own_high, own_low), (other, other_high, other_low)):
            value = source[...]
            rounded = value.astype(bf16)
            high[...] = rounded
            low[...] = (value - rounded.astype(f32)).astype(bf16)

    part = pl.BlockSpec((step, width), lambda i, b: (i, 0))
    return pl.pallas_call(
        kernel,
        out_shape=[shape(rows, width, dtype=bf16)] * 4,
        grid_spec=pltpu.PrefetchScalarGridSpec(
            num_scalar_prefetch=1,
            grid=(rows // step,),
            in_specs=[
                pl.BlockSpec((step, width), lambda i, b: (i, b[0])),
                pl.BlockSpec((step, width), lambda i, b: (i, 1 - b[0])),
            ],
            out_specs=[part] * 4,
        ),
        compiler_params=pltpu.CompilerParams(vmem_limit_bytes=LIMIT),
    )(bus, network, network)


def solve_rows(entries, values):
    size_n = len(values)
    entries = [list(row) for row in entries]
    values = list(values)
    for p in range(size_n):
        for i in range(p + 1, size_n):
            factor = entries[i][p] / entries[p][p]
            for j in range(p + 1, size_n):
                entries[i][j] = entries[i][j] - factor * entries[p][j]
            values[i] = values[i] - factor * values[p]
    result = [None] * size_n
    for i in range(size_n - 1, -1, -1):
        value = values[i]
        for j in range(i + 1, size_n):
            value = value - entries[i][j] * result[j]
        result[i] = value / entries[i][i]
    return result


def columns_at(iteration):
    return list(range(max(1, iteration - MEM + 1), iteration + 1))


def on_device(
    network,
    upper_bound,
    build_cost,
    unit_cost,
    demand,
    inflow,
    primal_start,
    network_start,
    energy_start,
    build_start,
    accepted,
    restarts,
):
    tm_count, bus_count = lax.axis_size("tm"), lax.axis_size("bus")
    tm, bus = lax.axis_index("tm"), lax.axis_index("bus")
    hours, width = primal_start.shape
    blocks = lane_blocks(width)
    flags = jnp.concatenate([accepted, restarts, tm.astype(jnp.int32).reshape(1)])
    first_restart, place_tm = accepted.shape[0], 2 * accepted.shape[0]
    member = shape(hours, width)
    line = shape(1, width)
    row = shape(1, LANES)
    tile = shape(ROWS, LANES)
    kind = {X: member, Y: member, E: member, U: line, SLOPE: member, COLUMN: line}

    upper_bound, build_cost, inflow, build_start = (
        value.reshape(1, width) for value in (upper_bound, build_cost, inflow, build_start)
    )
    own_high, own_low, other_high, other_low = split_network(
        network, bus.astype(jnp.int32).reshape(1)
    )


    def swap(value):
        return lax.ppermute(value, "bus", [(i, (i + 1) % bus_count) for i in range(bus_count)])

    def partner(value, distance):
        return lax.ppermute(value, "tm", [(i, i ^ distance) for i in range(tm_count)])

    def distances():
        return [1 << i for i in range(tm_count.bit_length() - 1)]

    def sums_of(value, backward, parts):
        beyond = jnp.zeros((1, parts), f32)
        for distance in distances():
            arrived = partner(value, distance)
            mine = (tm & distance) == 0
            take = mine if backward else ~mine
            beyond = beyond + jnp.where(take, arrived[:, :parts], 0.0)
            value = value + arrived
        return value, beyond


    def restart_of(ref, iteration):
        return ref[first_restart + iteration - 1].astype(f32)

    def counter_of(ref, iteration):
        count = jnp.float32(1.0)
        for k in range(1, iteration):
            count = (1.0 - restart_of(ref, k)) * count + 1.0
        return count

    def active_of(ref, column, iteration):
        value = jnp.float32(1.0)
        for k in range(column, iteration + 1):
            value = value * (1.0 - restart_of(ref, k))
        return value

    def weight_of(ref):
        at = ref[place_tm] * hours + row_iota(hours) + 1
        return 1.0 / at.astype(f32)

    def on_diagonal():
        lane = lax.broadcasted_iota(jnp.int32, (ROWS, LANES), 1)
        return lane == row_iota(ROWS)

    def mixing(i, iteration, products, log):
        columns = columns_at(iteration)
        size_n = len(columns)
        spread = jnp.where(on_diagonal(), jnp.broadcast_to(products, (ROWS, LANES)), 0.0)
        newest = jnp.broadcast_to(jnp.sum(spread, axis=1, keepdims=True), (ROWS, LANES))
        summed = dict(zip(columns[:-1], [ref[...] for ref in i.log]))
        summed[iteration] = newest
        log[...] = newest
        active = [active_of(i.flags, k, iteration) for k in columns]

        def entry(a, b):
            a, b = max(a, b), min(a, b)
            at = columns_at(columns[a]).index(columns[b])
            return summed[columns[a]][at : at + 1]

        gram = [[entry(a, b) for b in range(size_n)] for a in range(size_n)]
        trace = gram[0][0] * active[0]
        for a in range(1, size_n):
            trace = trace + gram[a][a] * active[a]
        shift = 0.001 * trace / size_n + 1e-06
        system = [
            [gram[a][b] * (active[a] * active[b]) for b in range(size_n)] for a in range(size_n)
        ]
        for a in range(size_n):
            system[a][a] = system[a][a] + (1.0 - active[a]) + shift
        right = [newest[8 + a : 9 + a] * active[a] for a in range(size_n)]
        mix = solve_rows(system, right)
        accept = i.flags[iteration - 1].astype(f32)
        return [accept * (value * a) for value, a in zip(mix, active)]

    def mixed(mapped, deltas, coefs):
        if not coefs:
            return mapped
        correction = coefs[0] * deltas[0]
        for coef, delta in zip(coefs[1:], deltas[1:]):
            correction = correction + coef * delta
        return mapped - correction

    def restarted(ref, iteration, following, total):
        if iteration == 0:
            return following, None
        restart = restart_of(ref, iteration)
        total = following if total is None else total + following
        mean = total / counter_of(ref, iteration)
        return jnp.where(restart > 0.5, mean, following), (1.0 - restart) * total

    def begin(i, o, k, at, name, mapped, deltas, coefs):
        following = mixed(mapped, deltas, coefs)
        total = i.totals[name][at] if k >= 2 else None
        state, total = restarted(i.flags, k, following, total)
        if k >= 1:
            o.totals[name][at] = total
        return state

    def note(i, o, k, at, name, mapped, state, pairs):
        residual = mapped - state
        o.resid[name][at] = residual
        if k == 0:
            return
        o.delta[name][at] = mapped - i.last_map[name][at]
        newest = residual - i.resid[name][at]
        o.column[name][at] = newest
        for j, column in enumerate([ref[at] for ref in i.columns[name]] + [newest]):
            for index, other in ((j, newest), (8 + j, residual)):
                term = column * other
                if name != U:
                    term = to_tile(term)
                key = (name == U, index)
                pairs[key] = pairs[key] + term if key in pairs else term

    def pair_tile(pairs, scale=1.0):
        rows = []
        for index in range(ROWS):
            total = jnp.zeros((1, LANES), f32)
            if (False, index) in pairs:
                total = jnp.sum(pairs[False, index], axis=0, keepdims=True)
            if (True, index) in pairs:
                total = total + scale * pairs[True, index]
            rows.append(total)
        return jnp.concatenate(rows, axis=0)


    def first_kernel(i, o):
        weight_at = weight_of(i.flags)
        for sl in blocks:
            tail = tail_sum(i.energy[:, sl] * weight_at)
            o.tail[:, sl] = tail
            o.message[:, sl] = tail[0:1]
        o.message[:, width:] = jnp.zeros((1, LANES), f32)

    def primal_kernel(k):
        count = len(columns_at(k - 1)) if k >= 2 else 0

        def primal(i, o):
            coefs = mixing(i, k - 1, i.message[:, width:], o.log) if k >= 2 else []
            for j, coef in enumerate(coefs):
                o.coefs[j : j + 1, :] = coef
            for sl in blocks:
                at = (slice(None), sl)
                slope = (i.pulled_own[at] + i.pulled_other[at]) - (i.tail[at] + i.later[at])
                column = i.message[at]
                state = {}
                for name, mapped in ((SLOPE, slope), (COLUMN, column)):
                    o.mapped[name][at] = mapped
                    deltas = [ref[at] for ref in i.deltas[name]] if count else []
                    if count:
                        newest = mapped - i.last_map[name][at]
                        o.delta[name][at] = newest
                        deltas.append(newest)
                    state[name] = begin(i, o, k, at, name, mapped, deltas, coefs)
                for name in (X, U):
                    deltas = [ref[at] for ref in i.deltas[name]] if count else []
                    state[name] = begin(i, o, k, at, name, i.mapped[name][at], deltas, coefs)
                    o.state[name][at] = state[name]
                next_primal = jnp.clip(
                    state[X] - primal_step * (i.unit_cost[at] - state[SLOPE]),
                    0.0,
                    i.upper_bound[at],
                )
                next_build = jnp.maximum(
                    state[U] - primal_step * (i.build_cost[at] - state[COLUMN]), 0.0
                )
                bar = 2.0 * next_primal - state[X]
                o.mapped[X][at] = next_primal
                o.mapped[U][at] = next_build
                o.bar[at] = bar
                o.block[at] = jnp.sum(bar, axis=0, keepdims=True)

        return primal

    def push_kernel(k):
        count = len(columns_at(k - 1)) if k >= 2 else 0

        def push(i, o):
            o.pushed[...] = product(i.bar[...], i.high[...], i.low[...], True)
            coefs = [i.coefs[j : j + 1, :] for j in range(count)]
            pairs = {}
            for sl in blocks:
                at = (slice(None), sl)
                for name in (Y, E):
                    deltas = [ref[at] for ref in i.deltas[name]] if count else []
                    o.state[name][at] = begin(
                        i, o, k, at, name, i.mapped[name][at], deltas, coefs
                    )
                o.running[at] = running_sum(i.bar[at])
                note(i, o, k, at, X, i.next_primal[at], i.primal[at], pairs)
            o.pairs[...] = pair_tile(pairs)

        return push

    def dual_kernel(k):
        def dual(i, o):
            o.mapped[...] = i.pushed[...] + product(
                i.bar_other[...], i.high[...], i.low[...], True
            )
            pairs = {}
            for sl in blocks:
                at = (slice(None), sl)
                state = i.state[at]
                mapped = jnp.maximum(state + dual_step * (i.demand[at] - o.mapped[at]), 0.0)
                o.mapped[at] = mapped
                note(i, o, k, at, Y, mapped, state, pairs)
            o.pairs[...] = i.pairs[...] + pair_tile(pairs)

        return dual

    def energy_kernel(k):
        def energy(i, o):
            weight_at = weight_of(i.flags)
            own_build = (i.flags[place_tm] == 0).astype(f32)
            pairs = {}
            for sl in blocks:
                at = (slice(None), sl)
                running = i.running[at] + i.earlier[at]
                state, build, next_build = i.state[E][at], i.state[U][at], i.mapped[at]
                bar_build = 2.0 * next_build - build
                mapped = jnp.maximum(
                    state + dual_step * (-i.inflow[at] - (bar_build - running) * weight_at), 0.0
                )
                o.mapped[at] = mapped
                tail = tail_sum(mapped * weight_at)
                o.tail[at] = tail
                o.block[at] = tail[0:1]
                note(i, o, k, at, E, mapped, state, pairs)
                note(i, o, k, at, U, next_build, build, pairs)
            if k >= 1:
                lines = i.pairs[...] + pair_tile(pairs, own_build)
                sums = jnp.broadcast_to(jnp.sum(lines, axis=1, keepdims=True), (ROWS, LANES))
                o.products[...] = jnp.sum(
                    jnp.where(on_diagonal(), sums, 0.0), axis=0, keepdims=True
                )
            else:
                o.products[...] = jnp.zeros((1, LANES), f32)

        return energy

    def pull_kernel(i, o):
        o.pulled[...] = product(i.dual[...], i.high[...], i.low[...], False)

    def last_kernel(i, o):
        coefs = mixing(i, ITERS - 1, i.message[...], o.log)
        for name in (X, Y, E, U):
            for sl in blocks:
                at = (slice(None), sl)
                deltas = [ref[at] for ref in i.deltas[name]]
                o.following[name][at] = mixed(i.mapped[name][at], deltas, coefs)


    mapped = {X: primal_start, Y: network_start, E: energy_start, U: build_start}
    deltas = {name: [] for name in kind}
    columns = {name: [] for name in (X, Y, E, U)}
    totals, last_map, resid, logs = {}, {}, {}, {}

    def pull(dual):
        out = run(pull_kernel, dict(dual=dual, high=other_high, low=other_low), dict(pulled=member))
        arriving = swap(out.pulled)
        out = run(pull_kernel, dict(dual=dual, high=own_high, low=own_low), dict(pulled=member))
        return out.pulled, arriving

    def picked(source, names):
        return {name: source[name] for name in names}

    def kinds(*names):
        return picked(kind, names)

    def note_ins(k, names):
        if k == 0:
            return {}
        return dict(
            last_map=picked(last_map, names),
            resid=picked(resid, names),
            columns={name: columns[name][-(MEM - 1) :] for name in names},
        )

    def note_outs(k, names):
        each = kinds(*names)
        return dict(resid=each, **(dict(delta=each, column=each) if k else {}))

    def take(k, out, names):
        for name in names:
            resid[name] = out.resid[name]
            if k:
                deltas[name] = (deltas[name] + [out.delta[name]])[-MEM:]
                columns[name] = (columns[name] + [out.column[name]])[-MEM:]

    def log_ins(iteration):
        return [logs[j] for j in columns_at(iteration)[:-1]]

    out = run(
        first_kernel,
        dict(flags=flags, energy=energy_start),
        dict(tail=member, message=shape(1, width + LANES)),
    )
    tail = out.tail
    message, later = sums_of(out.message, True, width)
    pulled_own, pulled_other = pull(network_start)

    for k in range(ITERS):
        mixes = k >= 2
        ins = dict(
            flags=flags,
            message=message,
            later=later,
            pulled_own=pulled_own,
            pulled_other=pulled_other,
            tail=tail,
            mapped=picked(mapped, (X, U)),
            unit_cost=unit_cost,
            upper_bound=upper_bound,
            build_cost=build_cost,
        )
        outs = dict(
            mapped=kinds(SLOPE, COLUMN, X, U),
            state=kinds(X, U),
            bar=member,
            block=line,
        )
        if mixes:
            ins.update(
                log=log_ins(k - 1),
                last_map=picked(last_map, (SLOPE, COLUMN)),
                totals=picked(totals, (SLOPE, COLUMN, X, U)),
                deltas={
                    SLOPE: deltas[SLOPE][-(MEM - 1) :],
                    COLUMN: deltas[COLUMN][-(MEM - 1) :],
                    X: deltas[X],
                    U: deltas[U],
                },
            )
            outs.update(log=tile, coefs=shape(8, LANES), delta=kinds(SLOPE, COLUMN))
        if k >= 1:
            outs.update(totals=kinds(SLOPE, COLUMN, X, U))
        one = run(primal_kernel(k), ins, outs)
        if mixes:
            logs[k - 1] = one.log
            for name in (SLOPE, COLUMN):
                deltas[name] = (deltas[name] + [one.delta[name]])[-MEM:]
        for name in (SLOPE, COLUMN):
            last_map[name] = one.mapped[name]
        if k >= 1:
            totals.update(one.totals)
        _, earlier = sums_of(one.block, False, width)
        bar_other = swap(one.bar)

        ins = dict(
            flags=flags,
            bar=one.bar,
            next_primal=one.mapped[X],
            primal=one.state[X],
            mapped=picked(mapped, (Y, E)),
            high=own_high,
            low=own_low,
            **note_ins(k, (X,)),
        )
        outs = dict(
            pushed=member,
            state=kinds(Y, E),
            running=member,
            pairs=tile,
            **note_outs(k, (X,)),
        )
        if mixes:
            ins.update(
                coefs=one.coefs, deltas=picked(deltas, (Y, E)), totals=picked(totals, (Y, E))
            )
        if k >= 1:
            outs.update(totals=kinds(Y, E))
        two = run(push_kernel(k), ins, outs)
        if k >= 1:
            totals.update(two.totals)

        three = run(
            dual_kernel(k),
            dict(
                pushed=two.pushed,
                bar_other=bar_other,
                state=two.state[Y],
                demand=demand,
                pairs=two.pairs,
                high=other_high,
                low=other_low,
                **note_ins(k, (Y,)),
            ),
            dict(mapped=member, pairs=tile, **note_outs(k, (Y,))),
        )
        four = run(
            energy_kernel(k),
            dict(
                flags=flags,
                running=two.running,
                earlier=earlier,
                state={E: two.state[E], U: one.state[U]},
                mapped=one.mapped[U],
                inflow=inflow,
                pairs=three.pairs,
                **note_ins(k, (E, U)),
            ),
            dict(mapped=member, tail=member, block=line, products=row, **note_outs(k, (E, U))),
        )
        take(k, two, (X,))
        take(k, three, (Y,))
        take(k, four, (E, U))
        mapped = {X: one.mapped[X], Y: three.mapped, E: four.mapped, U: one.mapped[U]}
        last_map.update(mapped)
        tail = four.tail
        products = four.products + swap(four.products) if k else four.products
        if k < ITERS - 1:
            message, later = sums_of(
                jnp.concatenate([four.block, products], axis=1), True, width
            )
            pulled_own, pulled_other = pull(mapped[Y])
        else:
            message, _ = sums_of(products, True, LANES)

    out = run(
        last_kernel,
        dict(
            flags=flags,
            message=message,
            log=log_ins(ITERS - 1),
            mapped=mapped,
            deltas=picked(deltas, (X, Y, E, U)),
        ),
        dict(log=tile, following=kinds(X, Y, E, U)),
    )
    final = out.following
    return final[X], final[Y], final[E], final[U].reshape(width)


def solution(mesh):
    hourly = P(("grp", "tm"), "bus")
    return jax.shard_map(
        on_device,
        mesh=mesh,
        in_specs=(
            P("bus", None),
            P("bus"),
            P("bus"),
            hourly,
            hourly,
            P(("grp", "bus")),
            hourly,
            hourly,
            hourly,
            P(("grp", "bus")),
            P("grp"),
            P("grp"),
        ),
        out_specs=(hourly, hourly, hourly, P(("grp", "bus"))),
        check_vma=False,
    )
```

```python
from types import SimpleNamespace as Space

import jax
import jax.numpy as jnp
from jax import lax
from jax.experimental import pallas as pl
from jax.experimental.pallas import tpu as pltpu
from jax.sharding import PartitionSpec as P

ITERS = 9
MEM = 5
LANES = 128
ROWS = 16
LIMIT = 10 * 1024 * 1024
X, Y, E, U, SLOPE, COLUMN = range(6)

primal_step = 0.3
dual_step = 0.3
f32 = jnp.float32
bf16 = jnp.bfloat16


def shape(*dims, dtype=f32):
    return jax.ShapeDtypeStruct(dims, dtype)


def run(body, ins, outs):
    in_leaves, in_tree = jax.tree.flatten(ins)
    out_leaves, out_tree = jax.tree.flatten(outs)

    def kernel(*refs):
        given = jax.tree.unflatten(in_tree, refs[: len(in_leaves)])
        made = jax.tree.unflatten(out_tree, refs[len(in_leaves) :])
        body(Space(**given), Space(**made))

    def place(leaf):
        return pl.BlockSpec(memory_space=pltpu.SMEM if leaf.dtype == jnp.int32 else pltpu.VMEM)

    results = pl.pallas_call(
        kernel,
        out_shape=out_leaves,
        in_specs=[place(leaf) for leaf in in_leaves],
        out_specs=[place(leaf) for leaf in out_leaves],
        compiler_params=pltpu.CompilerParams(vmem_limit_bytes=LIMIT),
        name=body.__name__,
    )(*in_leaves)
    return Space(**jax.tree.unflatten(out_tree, results))


def lane_blocks(width):
    return [slice(j * LANES, (j + 1) * LANES) for j in range(width // LANES)]


def row_iota(rows):
    return lax.broadcasted_iota(jnp.int32, (rows, LANES), 0)


def running_sum(block):
    rows = block.shape[0]
    at = row_iota(rows)
    step = 1
    while step < rows:
        block = block + jnp.where(at >= step, pltpu.roll(block, step, 0), 0.0)
        step *= 2
    return block


def tail_sum(block):
    rows = block.shape[0]
    at = row_iota(rows)
    step = 1
    while step < rows:
        block = block + jnp.where(at < rows - step, pltpu.roll(block, rows - step, 0), 0.0)
        step *= 2
    return block


def to_tile(block):
    rows = block.shape[0]
    total = block[0:8]
    for i in range(8, rows, 8):
        total = total + block[i : i + 8]
    return total


def product(left, high, low, transposed):
    rows = left.shape[0]
    dims = (((1,), (1 if transposed else 0,)), ((), ()))
    left_high = left.astype(bf16)
    left_low = (left - left_high.astype(f32)).astype(bf16)
    both = lax.dot_general(
        jnp.concatenate([left_high, left_low], axis=0), high, dims, preferred_element_type=f32
    )
    rest = lax.dot_general(left_high, low, dims, preferred_element_type=f32)
    return both[:rows] + (both[rows:] + rest)


def split_network(network, bus):
    rows, units = network.shape
    width = units // 2
    step = min(128, rows)

    def kernel(_, own, other, own_high, own_low, other_high, other_low):
        for source, high, low in ((own, own_high, own_low), (other, other_high, other_low)):
            value = source[...]
            rounded = value.astype(bf16)
            high[...] = rounded
            low[...] = (value - rounded.astype(f32)).astype(bf16)

    part = pl.BlockSpec((step, width), lambda i, b: (i, 0))
    return pl.pallas_call(
        kernel,
        out_shape=[shape(rows, width, dtype=bf16)] * 4,
        grid_spec=pltpu.PrefetchScalarGridSpec(
            num_scalar_prefetch=1,
            grid=(rows // step,),
            in_specs=[
                pl.BlockSpec((step, width), lambda i, b: (i, b[0])),
                pl.BlockSpec((step, width), lambda i, b: (i, 1 - b[0])),
            ],
            out_specs=[part] * 4,
        ),
        compiler_params=pltpu.CompilerParams(vmem_limit_bytes=LIMIT),
    )(bus, network, network)


def solve_rows(entries, values):
    size_n = len(values)
    entries = [list(row) for row in entries]
    values = list(values)
    for p in range(size_n):
        for i in range(p + 1, size_n):
            factor = entries[i][p] / entries[p][p]
            for j in range(p + 1, size_n):
                entries[i][j] = entries[i][j] - factor * entries[p][j]
            values[i] = values[i] - factor * values[p]
    result = [None] * size_n
    for i in range(size_n - 1, -1, -1):
        value = values[i]
        for j in range(i + 1, size_n):
            value = value - entries[i][j] * result[j]
        result[i] = value / entries[i][i]
    return result


def columns_at(iteration):
    return list(range(max(1, iteration - MEM + 1), iteration + 1))


def on_device(
    network,
    upper_bound,
    build_cost,
    unit_cost,
    demand,
    inflow,
    primal_start,
    network_start,
    energy_start,
    build_start,
    accepted,
    restarts,
):
    tm_count, bus_count = lax.axis_size("tm"), lax.axis_size("bus")
    tm, bus = lax.axis_index("tm"), lax.axis_index("bus")
    hours, width = primal_start.shape
    blocks = lane_blocks(width)
    everyone = tm_count * bus_count
    flags = jnp.concatenate([accepted, restarts, jnp.stack([tm, bus]).astype(jnp.int32)])
    first_restart = accepted.shape[0]
    place_tm, place_bus = 2 * first_restart, 2 * first_restart + 1
    member = shape(hours, width)
    line = shape(1, width)
    blocks_out = shape(tm_count, 1, width)
    message = shape(everyone, 1, width + LANES)
    tile = shape(ROWS, LANES)
    kind = {X: member, Y: member, E: member, U: line, SLOPE: member, COLUMN: line}

    upper_bound, build_cost, inflow, build_start = (
        value.reshape(1, width) for value in (upper_bound, build_cost, inflow, build_start)
    )
    own_high, own_low, other_high, other_low = split_network(
        network, bus.astype(jnp.int32).reshape(1)
    )


    def swap(value):
        return lax.ppermute(value, "bus", [(i, (i + 1) % bus_count) for i in range(bus_count)])

    def exchange(rows, axes):
        return lax.all_to_all(rows, axes, 0, 0, tiled=True)


    def restart_of(ref, iteration):
        return ref[first_restart + iteration - 1].astype(f32)

    def counter_of(ref, iteration):
        count = jnp.float32(1.0)
        for k in range(1, iteration):
            count = (1.0 - restart_of(ref, k)) * count + 1.0
        return count

    def active_of(ref, column, iteration):
        value = jnp.float32(1.0)
        for k in range(column, iteration + 1):
            value = value * (1.0 - restart_of(ref, k))
        return value

    def weight_of(ref):
        at = ref[place_tm] * hours + row_iota(hours) + 1
        return 1.0 / at.astype(f32)

    def on_diagonal():
        lane = lax.broadcasted_iota(jnp.int32, (ROWS, LANES), 1)
        return lane == row_iota(ROWS)

    def mixing(i, iteration, products, log):
        columns = columns_at(iteration)
        size_n = len(columns)
        spread = jnp.where(on_diagonal(), jnp.broadcast_to(products, (ROWS, LANES)), 0.0)
        newest = jnp.broadcast_to(jnp.sum(spread, axis=1, keepdims=True), (ROWS, LANES))
        summed = dict(zip(columns[:-1], [ref[...] for ref in i.log]))
        summed[iteration] = newest
        log[...] = newest
        active = [active_of(i.flags, k, iteration) for k in columns]

        def entry(a, b):
            a, b = max(a, b), min(a, b)
            at = columns_at(columns[a]).index(columns[b])
            return summed[columns[a]][at : at + 1]

        gram = [[entry(a, b) for b in range(size_n)] for a in range(size_n)]
        trace = gram[0][0] * active[0]
        for a in range(1, size_n):
            trace = trace + gram[a][a] * active[a]
        shift = 0.001 * trace / size_n + 1e-06
        system = [
            [gram[a][b] * (active[a] * active[b]) for b in range(size_n)] for a in range(size_n)
        ]
        for a in range(size_n):
            system[a][a] = system[a][a] + (1.0 - active[a]) + shift
        right = [newest[8 + a : 9 + a] * active[a] for a in range(size_n)]
        mix = solve_rows(system, right)
        accept = i.flags[iteration - 1].astype(f32)
        return [accept * (value * a) for value, a in zip(mix, active)]

    def mixed(mapped, deltas, coefs):
        if not coefs:
            return mapped
        correction = coefs[0] * deltas[0]
        for coef, delta in zip(coefs[1:], deltas[1:]):
            correction = correction + coef * delta
        return mapped - correction

    def restarted(ref, iteration, following, total):
        if iteration == 0:
            return following, None
        restart = restart_of(ref, iteration)
        total = following if total is None else total + following
        mean = total / counter_of(ref, iteration)
        return jnp.where(restart > 0.5, mean, following), (1.0 - restart) * total

    def begin(i, o, k, at, name, mapped, deltas, coefs):
        following = mixed(mapped, deltas, coefs)
        total = i.totals[name][at] if k >= 2 else None
        state, total = restarted(i.flags, k, following, total)
        if k >= 1:
            o.totals[name][at] = total
        return state

    def note(i, o, k, at, name, mapped, state, pairs):
        residual = mapped - state
        o.resid[name][at] = residual
        if k == 0:
            return
        o.delta[name][at] = mapped - i.last_map[name][at]
        newest = residual - i.resid[name][at]
        o.column[name][at] = newest
        for j, column in enumerate([ref[at] for ref in i.columns[name]] + [newest]):
            for index, other in ((j, newest), (8 + j, residual)):
                term = column * other
                if name != U:
                    term = to_tile(term)
                key = (name == U, index)
                pairs[key] = pairs[key] + term if key in pairs else term

    def pair_tile(pairs, scale=1.0):
        rows = []
        for index in range(ROWS):
            total = jnp.zeros((1, LANES), f32)
            if (False, index) in pairs:
                total = jnp.sum(pairs[False, index], axis=0, keepdims=True)
            if (True, index) in pairs:
                total = total + scale * pairs[True, index]
            rows.append(total)
        return jnp.concatenate(rows, axis=0)

    def send(ref, sl, value):
        for index in range(ref.shape[0]):
            ref[index, :, sl] = value

    def arrived_products(ref, sl):
        total = ref[0, :, sl]
        for index in range(1, everyone):
            total = total + ref[index, :, sl]
        return total


    def first_kernel(i, o):
        weight_at = weight_of(i.flags)
        for sl in blocks:
            tail = tail_sum(i.energy[:, sl] * weight_at)
            o.tail[:, sl] = tail
            send(o.message, sl, tail[0:1])
        send(o.message, slice(width, None), jnp.zeros((1, LANES), f32))

    def primal_kernel(k):
        count = len(columns_at(k - 1)) if k >= 2 else 0

        def primal(i, o):
            coefs = []
            if k >= 2:
                products = arrived_products(i.message, slice(width, None))
                coefs = mixing(i, k - 1, products, o.log)
            my_tm, my_bus = i.flags[place_tm], i.flags[place_bus]
            for j, coef in enumerate(coefs):
                o.coefs[j : j + 1, :] = coef
            for sl in blocks:
                at = (slice(None), sl)
                column = jnp.zeros((1, LANES), f32)
                later = jnp.zeros((1, LANES), f32)
                for s in range(tm_count):
                    piece = i.message[s * bus_count + my_bus, :, sl]
                    column = column + piece
                    later = later + jnp.where(s > my_tm, piece, 0.0)
                slope = (i.pulled_own[at] + i.pulled_other[at]) - (i.tail[at] + later)
                state = {}
                for name, mapped in ((SLOPE, slope), (COLUMN, column)):
                    o.mapped[name][at] = mapped
                    deltas = [ref[at] for ref in i.deltas[name]] if count else []
                    if count:
                        newest = mapped - i.last_map[name][at]
                        o.delta[name][at] = newest
                        deltas.append(newest)
                    state[name] = begin(i, o, k, at, name, mapped, deltas, coefs)
                for name in (X, U):
                    deltas = [ref[at] for ref in i.deltas[name]] if count else []
                    state[name] = begin(i, o, k, at, name, i.mapped[name][at], deltas, coefs)
                    o.state[name][at] = state[name]
                next_primal = jnp.clip(
                    state[X] - primal_step * (i.unit_cost[at] - state[SLOPE]),
                    0.0,
                    i.upper_bound[at],
                )
                next_build = jnp.maximum(
                    state[U] - primal_step * (i.build_cost[at] - state[COLUMN]), 0.0
                )
                bar = 2.0 * next_primal - state[X]
                o.mapped[X][at] = next_primal
                o.mapped[U][at] = next_build
                o.bar[at] = bar
                send(o.block, sl, jnp.sum(bar, axis=0, keepdims=True))

        return primal

    def push_kernel(k):
        count = len(columns_at(k - 1)) if k >= 2 else 0

        def push(i, o):
            o.pushed[...] = product(i.bar[...], i.high[...], i.low[...], True)
            coefs = [i.coefs[j : j + 1, :] for j in range(count)]
            pairs = {}
            for sl in blocks:
                at = (slice(None), sl)
                for name in (Y, E):
                    deltas = [ref[at] for ref in i.deltas[name]] if count else []
                    o.state[name][at] = begin(
                        i, o, k, at, name, i.mapped[name][at], deltas, coefs
                    )
                o.running[at] = running_sum(i.bar[at])
                note(i, o, k, at, X, i.next_primal[at], i.primal[at], pairs)
            o.pairs[...] = pair_tile(pairs)

        return push

    def dual_kernel(k):
        def dual(i, o):
            o.mapped[...] = i.pushed[...] + product(
                i.bar_other[...], i.high[...], i.low[...], True
            )
            pairs = {}
            for sl in blocks:
                at = (slice(None), sl)
                state = i.state[at]
                mapped = jnp.maximum(state + dual_step * (i.demand[at] - o.mapped[at]), 0.0)
                o.mapped[at] = mapped
                note(i, o, k, at, Y, mapped, state, pairs)
            o.pairs[...] = i.pairs[...] + pair_tile(pairs)

        return dual

    def energy_kernel(k):
        def energy(i, o):
            weight_at = weight_of(i.flags)
            my_tm = i.flags[place_tm]
            own_build = (my_tm == 0).astype(f32)
            pairs = {}
            for sl in blocks:
                at = (slice(None), sl)
                earlier = jnp.zeros((1, LANES), f32)
                for s in range(tm_count - 1):
                    earlier = earlier + jnp.where(s < my_tm, i.blocks[s, :, sl], 0.0)
                running = i.running[at] + earlier
                state, build, next_build = i.state[E][at], i.state[U][at], i.mapped[at]
                bar_build = 2.0 * next_build - build
                mapped = jnp.maximum(
                    state + dual_step * (-i.inflow[at] - (bar_build - running) * weight_at), 0.0
                )
                o.mapped[at] = mapped
                tail = tail_sum(mapped * weight_at)
                o.tail[at] = tail
                if k < ITERS - 1:
                    send(o.message, sl, tail[0:1])
                note(i, o, k, at, E, mapped, state, pairs)
                note(i, o, k, at, U, next_build, build, pairs)
            products = jnp.zeros((1, LANES), f32)
            if k >= 1:
                lines = i.pairs[...] + pair_tile(pairs, own_build)
                sums = jnp.broadcast_to(jnp.sum(lines, axis=1, keepdims=True), (ROWS, LANES))
                products = jnp.sum(jnp.where(on_diagonal(), sums, 0.0), axis=0, keepdims=True)
            send(o.message, slice(width if k < ITERS - 1 else 0, None), products)

        return energy

    def pull_kernel(i, o):
        o.pulled[...] = product(i.dual[...], i.high[...], i.low[...], False)

    def last_kernel(i, o):
        products = arrived_products(i.message, slice(None))
        coefs = mixing(i, ITERS - 1, products, o.log)
        for name in (X, Y, E, U):
            for sl in blocks:
                at = (slice(None), sl)
                deltas = [ref[at] for ref in i.deltas[name]]
                o.following[name][at] = mixed(i.mapped[name][at], deltas, coefs)


    mapped = {X: primal_start, Y: network_start, E: energy_start, U: build_start}
    deltas = {name: [] for name in kind}
    columns = {name: [] for name in (X, Y, E, U)}
    totals, last_map, resid, logs = {}, {}, {}, {}

    def pull(dual):
        out = run(pull_kernel, dict(dual=dual, high=other_high, low=other_low), dict(pulled=member))
        arriving = swap(out.pulled)
        own = run(
            pull_kernel,
            dict(dual=dual, high=own_high, low=own_low, after=out.pulled),
            dict(pulled=member),
        )
        return own.pulled, arriving

    def picked(source, names):
        return {name: source[name] for name in names}

    def kinds(*names):
        return picked(kind, names)

    def note_ins(k, names):
        if k == 0:
            return {}
        return dict(
            last_map=picked(last_map, names),
            resid=picked(resid, names),
            columns={name: columns[name][-(MEM - 1) :] for name in names},
        )

    def note_outs(k, names):
        each = kinds(*names)
        return dict(resid=each, **(dict(delta=each, column=each) if k else {}))

    def take(k, out, names):
        for name in names:
            resid[name] = out.resid[name]
            if k:
                deltas[name] = (deltas[name] + [out.delta[name]])[-MEM:]
                columns[name] = (columns[name] + [out.column[name]])[-MEM:]

    def log_ins(iteration):
        return [logs[j] for j in columns_at(iteration)[:-1]]

    out = run(
        first_kernel,
        dict(flags=flags, energy=energy_start),
        dict(tail=member, message=message),
    )
    tail = out.tail
    arrived = exchange(out.message, ("tm", "bus"))
    pulled_own, pulled_other = pull(network_start)

    for k in range(ITERS):
        mixes = k >= 2
        ins = dict(
            flags=flags,
            message=arrived,
            pulled_own=pulled_own,
            pulled_other=pulled_other,
            tail=tail,
            mapped=picked(mapped, (X, U)),
            unit_cost=unit_cost,
            upper_bound=upper_bound,
            build_cost=build_cost,
        )
        outs = dict(
            mapped=kinds(SLOPE, COLUMN, X, U),
            state=kinds(X, U),
            bar=member,
            block=blocks_out,
        )
        if mixes:
            ins.update(
                log=log_ins(k - 1),
                last_map=picked(last_map, (SLOPE, COLUMN)),
                totals=picked(totals, (SLOPE, COLUMN, X, U)),
                deltas={
                    SLOPE: deltas[SLOPE][-(MEM - 1) :],
                    COLUMN: deltas[COLUMN][-(MEM - 1) :],
                    X: deltas[X],
                    U: deltas[U],
                },
            )
            outs.update(log=tile, coefs=shape(8, LANES), delta=kinds(SLOPE, COLUMN))
        if k >= 1:
            outs.update(totals=kinds(SLOPE, COLUMN, X, U))
        one = run(primal_kernel(k), ins, outs)
        if mixes:
            logs[k - 1] = one.log
            for name in (SLOPE, COLUMN):
                deltas[name] = (deltas[name] + [one.delta[name]])[-MEM:]
        for name in (SLOPE, COLUMN):
            last_map[name] = one.mapped[name]
        if k >= 1:
            totals.update(one.totals)
        earlier = exchange(one.block, "tm")
        bar_other = swap(one.bar)

        ins = dict(
            flags=flags,
            bar=one.bar,
            next_primal=one.mapped[X],
            primal=one.state[X],
            mapped=picked(mapped, (Y, E)),
            high=own_high,
            low=own_low,
            **note_ins(k, (X,)),
        )
        outs = dict(
            pushed=member,
            state=kinds(Y, E),
            running=member,
            pairs=tile,
            **note_outs(k, (X,)),
        )
        if mixes:
            ins.update(
                coefs=one.coefs, deltas=picked(deltas, (Y, E)), totals=picked(totals, (Y, E))
            )
        if k >= 1:
            outs.update(totals=kinds(Y, E))
        two = run(push_kernel(k), ins, outs)
        if k >= 1:
            totals.update(two.totals)

        three = run(
            dual_kernel(k),
            dict(
                pushed=two.pushed,
                bar_other=bar_other,
                state=two.state[Y],
                demand=demand,
                pairs=two.pairs,
                high=other_high,
                low=other_low,
                **note_ins(k, (Y,)),
            ),
            dict(mapped=member, pairs=tile, **note_outs(k, (Y,))),
        )
        four = run(
            energy_kernel(k),
            dict(
                flags=flags,
                running=two.running,
                blocks=earlier,
                state={E: two.state[E], U: one.state[U]},
                mapped=one.mapped[U],
                inflow=inflow,
                pairs=three.pairs,
                **note_ins(k, (E, U)),
            ),
            dict(
                mapped=member,
                tail=member,
                message=message if k < ITERS - 1 else shape(everyone, 1, LANES),
                **note_outs(k, (E, U)),
            ),
        )
        take(k, two, (X,))
        take(k, three, (Y,))
        take(k, four, (E, U))
        mapped = {X: one.mapped[X], Y: three.mapped, E: four.mapped, U: one.mapped[U]}
        last_map.update(mapped)
        tail = four.tail
        arrived = exchange(four.message, ("tm", "bus"))
        if k < ITERS - 1:
            pulled_own, pulled_other = pull(mapped[Y])

    out = run(
        last_kernel,
        dict(
            flags=flags,
            message=arrived,
            log=log_ins(ITERS - 1),
            mapped=mapped,
            deltas=picked(deltas, (X, Y, E, U)),
        ),
        dict(log=tile, following=kinds(X, Y, E, U)),
    )
    final = out.following
    return final[X], final[Y], final[E], final[U].reshape(width)


def solution(mesh):
    hourly = P(("grp", "tm"), "bus")
    return jax.shard_map(
        on_device,
        mesh=mesh,
        in_specs=(
            P("bus", None),
            P("bus"),
            P("bus"),
            hourly,
            hourly,
            P(("grp", "bus")),
            hourly,
            hourly,
            hourly,
            P(("grp", "bus")),
            P("grp"),
            P("grp"),
        ),
        out_specs=(hourly, hourly, hourly, P(("grp", "bus"))),
        check_vma=False,
    )
```

```python
from types import SimpleNamespace as Space

import jax
import jax.numpy as jnp
from jax import lax
from jax.experimental import pallas as pl
from jax.experimental.pallas import tpu as pltpu
from jax.sharding import PartitionSpec as P

ITERS = 9
MEM = 5
LANES = 128
ROWS = 16
LIMIT = 10 * 1024 * 1024
X, Y, E, U, SLOPE, COLUMN = range(6)

primal_step = 0.3
dual_step = 0.3
f32 = jnp.float32
bf16 = jnp.bfloat16


def shape(*dims, dtype=f32):
    return jax.ShapeDtypeStruct(dims, dtype)


def run(body, ins, outs):
    in_leaves, in_tree = jax.tree.flatten(ins)
    out_leaves, out_tree = jax.tree.flatten(outs)

    def kernel(*refs):
        given = jax.tree.unflatten(in_tree, refs[: len(in_leaves)])
        made = jax.tree.unflatten(out_tree, refs[len(in_leaves) :])
        body(Space(**given), Space(**made))

    def place(leaf):
        return pl.BlockSpec(memory_space=pltpu.SMEM if leaf.dtype == jnp.int32 else pltpu.VMEM)

    results = pl.pallas_call(
        kernel,
        out_shape=out_leaves,
        in_specs=[place(leaf) for leaf in in_leaves],
        out_specs=[place(leaf) for leaf in out_leaves],
        compiler_params=pltpu.CompilerParams(vmem_limit_bytes=LIMIT),
        name=body.__name__,
    )(*in_leaves)
    return Space(**jax.tree.unflatten(out_tree, results))


def lane_blocks(width):
    return [slice(j * LANES, (j + 1) * LANES) for j in range(width // LANES)]


def row_iota(rows):
    return lax.broadcasted_iota(jnp.int32, (rows, LANES), 0)


def running_sum(block):
    rows = block.shape[0]
    at = row_iota(rows)
    step = 1
    while step < rows:
        block = block + jnp.where(at >= step, pltpu.roll(block, step, 0), 0.0)
        step *= 2
    return block


def tail_sum(block):
    rows = block.shape[0]
    at = row_iota(rows)
    step = 1
    while step < rows:
        block = block + jnp.where(at < rows - step, pltpu.roll(block, rows - step, 0), 0.0)
        step *= 2
    return block


def to_tile(block):
    rows = block.shape[0]
    total = block[0:8]
    for i in range(8, rows, 8):
        total = total + block[i : i + 8]
    return total


def product(left, high, low):
    rows = left.shape[0]
    left_high = left.astype(bf16)
    left_low = (left - left_high.astype(f32)).astype(bf16)
    both = jnp.dot(
        jnp.concatenate([left_high, left_low], axis=0), high, preferred_element_type=f32
    )
    rest = jnp.dot(left_high, low, preferred_element_type=f32)
    return both[:rows] + (both[rows:] + rest)


def split_network(network, bus):
    rows, units = network.shape
    width = units // 2
    step = min(256, rows)

    def halves(value, high, low):
        rounded = value.astype(bf16)
        high[...] = rounded
        low[...] = (value - rounded.astype(f32)).astype(bf16)

    def split(_, own, other, *parts):
        for at, source in ((0, own), (4, other)):
            value = source[...]
            halves(value, parts[at], parts[at + 1])
            halves(value.T, parts[at + 2], parts[at + 3])

    part = pl.BlockSpec((step, width), lambda i, b: (i, 0))
    turned = pl.BlockSpec((width, step), lambda i, b: (0, i))
    plain_shape, turned_shape = shape(rows, width, dtype=bf16), shape(width, rows, dtype=bf16)
    parts = pl.pallas_call(
        split,
        out_shape=([plain_shape] * 2 + [turned_shape] * 2) * 2,
        grid_spec=pltpu.PrefetchScalarGridSpec(
            num_scalar_prefetch=1,
            grid=(rows // step,),
            in_specs=[
                pl.BlockSpec((step, width), lambda i, b: (i, b[0])),
                pl.BlockSpec((step, width), lambda i, b: (i, 1 - b[0])),
            ],
            out_specs=([part] * 2 + [turned] * 2) * 2,
        ),
        compiler_params=pltpu.CompilerParams(vmem_limit_bytes=2 * LIMIT),
    )(bus, network, network)
    names = ("high", "low")
    return [dict(zip(names, parts[at : at + 2])) for at in (0, 2, 4, 6)]


def solve_rows(entries, values):
    size_n = len(values)
    entries = [list(row) for row in entries]
    values = list(values)
    for p in range(size_n):
        for i in range(p + 1, size_n):
            factor = entries[i][p] / entries[p][p]
            for j in range(p + 1, size_n):
                entries[i][j] = entries[i][j] - factor * entries[p][j]
            values[i] = values[i] - factor * values[p]
    result = [None] * size_n
    for i in range(size_n - 1, -1, -1):
        value = values[i]
        for j in range(i + 1, size_n):
            value = value - entries[i][j] * result[j]
        result[i] = value / entries[i][i]
    return result


def columns_at(iteration):
    return list(range(max(1, iteration - MEM + 1), iteration + 1))


def on_device(
    network,
    upper_bound,
    build_cost,
    unit_cost,
    demand,
    inflow,
    primal_start,
    network_start,
    energy_start,
    build_start,
    accepted,
    restarts,
):
    tm_count, bus_count = lax.axis_size("tm"), lax.axis_size("bus")
    tm, bus = lax.axis_index("tm"), lax.axis_index("bus")
    own_hours, width = primal_start.shape
    hours = 2 * own_hours
    blocks = lane_blocks(width)
    flags = jnp.concatenate([accepted, restarts, tm.astype(jnp.int32).reshape(1)])
    first_restart, place_tm = accepted.shape[0], 2 * accepted.shape[0]
    member = shape(hours, width)
    line = shape(1, width)
    row = shape(1, LANES)
    tile = shape(ROWS, LANES)
    kind = {X: member, Y: member, E: member, U: line, SLOPE: member, COLUMN: line}

    upper_bound, build_cost, inflow, build_start = (
        value.reshape(1, width) for value in (upper_bound, build_cost, inflow, build_start)
    )
    pull_own, push_own, pull_other, push_other = split_network(
        network, bus.astype(jnp.int32).reshape(1)
    )


    def swap(value):
        return lax.ppermute(value, "bus", [(i, (i + 1) % bus_count) for i in range(bus_count)])

    def partner(value, distance):
        return lax.ppermute(value, "tm", [(i, i ^ distance) for i in range(tm_count)])

    distances = [1 << i for i in range(1, tm_count.bit_length() - 1)]

    def gathered(value, first, carried):
        arrived = []
        for distance in distances:
            arrived.append(partner(value, distance) if arrived else first)
            if distance != distances[-1]:
                value = (value if len(arrived) > 1 else carried) + arrived[-1]
        return value if len(arrived) > 1 else carried, arrived


    def restart_of(ref, iteration):
        return ref[first_restart + iteration - 1].astype(f32)

    def counter_of(ref, iteration):
        count = jnp.float32(1.0)
        for k in range(1, iteration):
            count = (1.0 - restart_of(ref, k)) * count + 1.0
        return count

    def active_of(ref, column, iteration):
        value = jnp.float32(1.0)
        for k in range(column, iteration + 1):
            value = value * (1.0 - restart_of(ref, k))
        return value

    def weight_of(ref):
        at = (ref[place_tm] // 2) * hours + row_iota(hours) + 1
        return 1.0 / at.astype(f32)

    def on_diagonal():
        lane = lax.broadcasted_iota(jnp.int32, (ROWS, LANES), 1)
        return lane == row_iota(ROWS)

    def mixing(i, iteration, products, log):
        columns = columns_at(iteration)
        size_n = len(columns)
        spread = jnp.where(on_diagonal(), jnp.broadcast_to(products, (ROWS, LANES)), 0.0)
        newest = jnp.broadcast_to(jnp.sum(spread, axis=1, keepdims=True), (ROWS, LANES))
        summed = dict(zip(columns[:-1], [ref[...] for ref in i.log]))
        summed[iteration] = newest
        log[...] = newest
        active = [active_of(i.flags, k, iteration) for k in columns]

        def entry(a, b):
            a, b = max(a, b), min(a, b)
            at = columns_at(columns[a]).index(columns[b])
            return summed[columns[a]][at : at + 1]

        gram = [[entry(a, b) for b in range(size_n)] for a in range(size_n)]
        trace = gram[0][0] * active[0]
        for a in range(1, size_n):
            trace = trace + gram[a][a] * active[a]
        shift = 0.001 * trace / size_n + 1e-06
        system = [
            [gram[a][b] * (active[a] * active[b]) for b in range(size_n)] for a in range(size_n)
        ]
        for a in range(size_n):
            system[a][a] = system[a][a] + (1.0 - active[a]) + shift
        right = [newest[8 + a : 9 + a] * active[a] for a in range(size_n)]
        mix = solve_rows(system, right)
        accept = i.flags[iteration - 1].astype(f32)
        return [accept * (value * a) for value, a in zip(mix, active)]

    def mixed(mapped, deltas, coefs):
        if not coefs:
            return mapped
        correction = coefs[0] * deltas[0]
        for coef, delta in zip(coefs[1:], deltas[1:]):
            correction = correction + coef * delta
        return mapped - correction

    def restarted(ref, iteration, following, total):
        if iteration == 0:
            return following, None
        restart = restart_of(ref, iteration)
        total = following if total is None else total + following
        mean = total / counter_of(ref, iteration)
        return jnp.where(restart > 0.5, mean, following), (1.0 - restart) * total

    def begin(i, o, k, at, name, mapped, deltas, coefs):
        following = mixed(mapped, deltas, coefs)
        total = i.totals[name][at] if k >= 2 else None
        state, total = restarted(i.flags, k, following, total)
        if k >= 1:
            o.totals[name][at] = total
        return state

    def note(i, o, k, at, name, mapped, state, pairs):
        residual = mapped - state
        o.resid[name][at] = residual
        if k == 0:
            return
        o.delta[name][at] = mapped - i.last_map[name][at]
        newest = residual - i.resid[name][at]
        o.column[name][at] = newest
        for j, column in enumerate([ref[at] for ref in i.columns[name]] + [newest]):
            for index, other in ((j, newest), (8 + j, residual)):
                term = column * other
                if name != U:
                    term = to_tile(term)
                key = (name == U, index)
                pairs[key] = pairs[key] + term if key in pairs else term

    def pair_tile(pairs, scale=1.0):
        rows = []
        for index in range(ROWS):
            total = jnp.zeros((1, LANES), f32)
            if (False, index) in pairs:
                total = jnp.sum(pairs[False, index], axis=0, keepdims=True)
            if (True, index) in pairs:
                total = total + scale * pairs[True, index]
            rows.append(total)
        return jnp.concatenate(rows, axis=0)

    def beyond(ref, arrived, at, backward):
        total = jnp.zeros((1, LANES), f32)
        for distance, piece in zip(distances, arrived):
            first_half = (ref[place_tm] & distance) == 0
            take = first_half if backward else jnp.logical_not(first_half)
            total = total + jnp.where(take, piece[at], 0.0)
        return total

    def joined(ref, out, own, arrived):
        half = ref[place_tm] % 2
        out[pl.ds(pl.multiple_of(half * own_hours, own_hours), own_hours), :] = own
        out[pl.ds(pl.multiple_of((1 - half) * own_hours, own_hours), own_hours), :] = arrived


    def join(i, o):
        for index, (own, out) in enumerate(zip(i.own, o.out)):
            arrived = i.arrived[index * own_hours : (index + 1) * own_hours, :]
            joined(i.flags, out, own[...], arrived)

    def first(i, o):
        joined(i.flags, o.energy, i.own[...], i.arrived[...])
        weight_at = weight_of(i.flags)
        for sl in blocks:
            tail = tail_sum(o.energy[:, sl] * weight_at)
            o.tail[:, sl] = tail
            o.block[:, sl] = tail[0:1]

    def whole(i, sl):
        return i.message[:, sl] + i.arrived[-1][:, sl] if i.arrived else i.message[:, sl]

    def primal_kernel(k):
        count = len(columns_at(k - 1)) if k >= 2 else 0

        def primal(i, o):
            coefs = []
            if k >= 2:
                products = whole(i, slice(width, None))
                coefs = mixing(i, k - 1, products, o.log)
            for j, coef in enumerate(coefs):
                o.coefs[j : j + 1, :] = coef
            for sl in blocks:
                at = (slice(None), sl)
                later = beyond(i.flags, i.arrived, at, True)
                slope = (i.pulled_own[at] + i.pulled_other[at]) - (i.tail[at] + later)
                column = whole(i, sl)
                state = {}
                for name, mapped in ((SLOPE, slope), (COLUMN, column)):
                    o.mapped[name][at] = mapped
                    deltas = [ref[at] for ref in i.deltas[name]] if count else []
                    if count:
                        newest = mapped - i.last_map[name][at]
                        o.delta[name][at] = newest
                        deltas.append(newest)
                    state[name] = begin(i, o, k, at, name, mapped, deltas, coefs)
                for name in (X, U):
                    deltas = [ref[at] for ref in i.deltas[name]] if count else []
                    state[name] = begin(i, o, k, at, name, i.mapped[name][at], deltas, coefs)
                    o.state[name][at] = state[name]
                next_primal = jnp.clip(
                    state[X] - primal_step * (i.unit_cost[at] - state[SLOPE]),
                    0.0,
                    i.upper_bound[at],
                )
                next_build = jnp.maximum(
                    state[U] - primal_step * (i.build_cost[at] - state[COLUMN]), 0.0
                )
                bar = 2.0 * next_primal - state[X]
                o.mapped[X][at] = next_primal
                o.mapped[U][at] = next_build
                o.bar[at] = bar
                o.block[at] = jnp.sum(bar, axis=0, keepdims=True)

        return primal

    def push_kernel(k):
        count = len(columns_at(k - 1)) if k >= 2 else 0

        def push(i, o):
            o.block[...] = i.block[...]
            o.pushed[...] = product(i.bar[...], i.high[...], i.low[...])
            coefs = [i.coefs[j : j + 1, :] for j in range(count)]
            pairs = {}
            for sl in blocks:
                at = (slice(None), sl)
                for name in (Y, E):
                    deltas = [ref[at] for ref in i.deltas[name]] if count else []
                    o.state[name][at] = begin(
                        i, o, k, at, name, i.mapped[name][at], deltas, coefs
                    )
                o.running[at] = running_sum(i.bar[at])
                note(i, o, k, at, X, i.next_primal[at], i.primal[at], pairs)
            o.pairs[...] = pair_tile(pairs)

        return push

    def dual_kernel(k):
        def dual(i, o):
            o.mapped[...] = i.pushed[...] + product(i.bar_other[...], i.high[...], i.low[...])
            pairs = {}
            for sl in blocks:
                at = (slice(None), sl)
                state = i.state[at]
                mapped = jnp.maximum(state + dual_step * (i.demand[at] - o.mapped[at]), 0.0)
                o.mapped[at] = mapped
                note(i, o, k, at, Y, mapped, state, pairs)
            o.pairs[...] = i.pairs[...] + pair_tile(pairs)

        return dual

    def energy_kernel(k):
        def energy(i, o):
            weight_at = weight_of(i.flags)
            own_build = (i.flags[place_tm] < 2).astype(f32)
            pairs = {}
            for sl in blocks:
                at = (slice(None), sl)
                running = i.running[at] + beyond(i.flags, i.arrived, at, False)
                state, build, next_build = i.state[E][at], i.state[U][at], i.mapped[at]
                bar_build = 2.0 * next_build - build
                mapped = jnp.maximum(
                    state + dual_step * (-i.inflow[at] - (bar_build - running) * weight_at), 0.0
                )
                o.mapped[at] = mapped
                tail = tail_sum(mapped * weight_at)
                o.tail[at] = tail
                o.block[at] = tail[0:1]
                note(i, o, k, at, E, mapped, state, pairs)
                note(i, o, k, at, U, next_build, build, pairs)
            if k >= 1:
                lines = i.pairs[...] + pair_tile(pairs, own_build)
                sums = jnp.broadcast_to(jnp.sum(lines, axis=1, keepdims=True), (ROWS, LANES))
                o.products[...] = jnp.sum(
                    jnp.where(on_diagonal(), sums, 0.0), axis=0, keepdims=True
                )
            else:
                o.products[...] = jnp.zeros((1, LANES), f32)

        return energy

    def pull(i, o):
        o.carried[...] = i.carried[...]
        o.pulled[...] = product(i.dual[...], i.high[...], i.low[...])

    def last_kernel(i, o):
        half = i.flags[place_tm] % 2
        own = pl.ds(pl.multiple_of(half * own_hours, own_hours), own_hours)
        coefs = mixing(i, ITERS - 1, whole(i, slice(None)), o.log)
        for name in (X, Y, E, U):
            for sl in blocks:
                at = (slice(None) if name == U else own, sl)
                deltas = [ref[at] for ref in i.deltas[name]]
                o.following[name][:, sl] = mixed(i.mapped[name][at], deltas, coefs)


    deltas = {name: [] for name in kind}
    columns = {name: [] for name in (X, Y, E, U)}
    totals, last_map, resid, logs = {}, {}, {}, {}

    def pulled_by(dual, parts, carried):
        out = run(
            pull,
            dict(dual=dual, carried=carried, **parts),
            dict(pulled=member, carried=shape(*carried.shape)),
        )
        return out.pulled, out.carried

    def send_totals(block, products, dual):
        row = block
        if products is not None:
            row = jnp.concatenate([block, products + swap(products)], axis=1)
        first = partner(row, distances[0])
        other, row = pulled_by(dual, pull_other, row)
        pulled_other = swap(other)
        row, arrived = gathered(row, first, row)
        pulled_own, row = pulled_by(dual, pull_own, row)
        return dict(
            message=row, arrived=arrived, pulled_own=pulled_own, pulled_other=pulled_other
        )

    def picked(source, names):
        return {name: source[name] for name in names}

    def kinds(*names):
        return picked(kind, names)

    def note_ins(k, names):
        if k == 0:
            return {}
        return dict(
            last_map=picked(last_map, names),
            resid=picked(resid, names),
            columns={name: columns[name][-(MEM - 1) :] for name in names},
        )

    def note_outs(k, names):
        each = kinds(*names)
        return dict(resid=each, **(dict(delta=each, column=each) if k else {}))

    def take(k, out, names):
        for name in names:
            resid[name] = out.resid[name]
            if k:
                deltas[name] = (deltas[name] + [out.delta[name]])[-MEM:]
                columns[name] = (columns[name] + [out.column[name]])[-MEM:]

    def log_ins(iteration):
        return [logs[j] for j in columns_at(iteration)[:-1]]

    energy_arrived = partner(energy_start, 1)
    starts = [primal_start, network_start, unit_cost, demand]
    starts_arrived = partner(jnp.concatenate(starts, axis=0), 1)
    out = run(
        first,
        dict(flags=flags, own=energy_start, arrived=energy_arrived),
        dict(energy=member, tail=member, block=line),
    )
    energy, tail, block = out.energy, out.tail, out.block
    out = run(
        join, dict(flags=flags, own=starts, arrived=starts_arrived), dict(out=[member] * 4)
    )
    primal, dual, unit_cost, demand = out.out
    mapped = {X: primal, Y: dual, E: energy, U: build_start}
    totals_in = send_totals(block, None, dual)

    for k in range(ITERS):
        mixes = k >= 2
        ins = dict(
            flags=flags,
            **totals_in,
            tail=tail,
            mapped=picked(mapped, (X, U)),
            unit_cost=unit_cost,
            upper_bound=upper_bound,
            build_cost=build_cost,
        )
        outs = dict(
            mapped=kinds(SLOPE, COLUMN, X, U),
            state=kinds(X, U),
            bar=member,
            block=line,
        )
        if mixes:
            ins.update(
                log=log_ins(k - 1),
                last_map=picked(last_map, (SLOPE, COLUMN)),
                totals=picked(totals, (SLOPE, COLUMN, X, U)),
                deltas={
                    SLOPE: deltas[SLOPE][-(MEM - 1) :],
                    COLUMN: deltas[COLUMN][-(MEM - 1) :],
                    X: deltas[X],
                    U: deltas[U],
                },
            )
            outs.update(log=tile, coefs=shape(8, LANES), delta=kinds(SLOPE, COLUMN))
        if k >= 1:
            outs.update(totals=kinds(SLOPE, COLUMN, X, U))
        one = run(primal_kernel(k), ins, outs)
        if mixes:
            logs[k - 1] = one.log
            for name in (SLOPE, COLUMN):
                deltas[name] = (deltas[name] + [one.delta[name]])[-MEM:]
        for name in (SLOPE, COLUMN):
            last_map[name] = one.mapped[name]
        if k >= 1:
            totals.update(one.totals)
        first_arrived = partner(one.block, distances[0])
        bar_other = swap(one.bar)

        ins = dict(
            flags=flags,
            bar=one.bar,
            block=one.block,
            next_primal=one.mapped[X],
            primal=one.state[X],
            mapped=picked(mapped, (Y, E)),
            **push_own,
            **note_ins(k, (X,)),
        )
        outs = dict(
            pushed=member,
            block=line,
            state=kinds(Y, E),
            running=member,
            pairs=tile,
            **note_outs(k, (X,)),
        )
        if mixes:
            ins.update(
                coefs=one.coefs, deltas=picked(deltas, (Y, E)), totals=picked(totals, (Y, E))
            )
        if k >= 1:
            outs.update(totals=kinds(Y, E))
        two = run(push_kernel(k), ins, outs)
        if k >= 1:
            totals.update(two.totals)

        _, earlier = gathered(one.block, first_arrived, two.block)
        three = run(
            dual_kernel(k),
            dict(
                pushed=two.pushed,
                bar_other=bar_other,
                state=two.state[Y],
                demand=demand,
                pairs=two.pairs,
                **push_other,
                **note_ins(k, (Y,)),
            ),
            dict(mapped=member, pairs=tile, **note_outs(k, (Y,))),
        )
        four = run(
            energy_kernel(k),
            dict(
                flags=flags,
                running=two.running,
                arrived=earlier,
                state={E: two.state[E], U: one.state[U]},
                mapped=one.mapped[U],
                inflow=inflow,
                pairs=three.pairs,
                **note_ins(k, (E, U)),
            ),
            dict(mapped=member, tail=member, block=line, products=row, **note_outs(k, (E, U))),
        )
        take(k, two, (X,))
        take(k, three, (Y,))
        take(k, four, (E, U))
        mapped = {X: one.mapped[X], Y: three.mapped, E: four.mapped, U: one.mapped[U]}
        last_map.update(mapped)
        tail = four.tail
        if k < ITERS - 1:
            totals_in = send_totals(four.block, four.products, mapped[Y])

    products = four.products + swap(four.products)
    message, arrived = gathered(products, partner(products, distances[0]), products)
    out = run(
        last_kernel,
        dict(
            flags=flags,
            message=message,
            arrived=arrived,
            log=log_ins(ITERS - 1),
            mapped=mapped,
            deltas=picked(deltas, (X, Y, E, U)),
        ),
        dict(
            log=tile,
            following={name: line if name == U else shape(own_hours, width) for name in (X, Y, E, U)},
        ),
    )
    final = out.following
    return final[X], final[Y], final[E], final[U].reshape(width)


def solution(mesh):
    hourly = P(("grp", "tm"), "bus")
    return jax.shard_map(
        on_device,
        mesh=mesh,
        in_specs=(
            P("bus", None),
            P("bus"),
            P("bus"),
            hourly,
            hourly,
            P(("grp", "bus")),
            hourly,
            hourly,
            hourly,
            P(("grp", "bus")),
            P("grp"),
            P("grp"),
        ),
        out_specs=(hourly, hourly, hourly, P(("grp", "bus"))),
        check_vma=False,
    )
```

```python
from types import SimpleNamespace as Space

import jax
import jax.numpy as jnp
from jax import lax
from jax.experimental import pallas as pl
from jax.experimental.pallas import tpu as pltpu
from jax.sharding import PartitionSpec as P

ITERS = 9
MEM = 5
LANES = 128
ROWS = 16
LIMIT = 6 * 1024 * 1024
SPAN = 4
CHUNK = 32
X, Y, E, U, SLOPE, COLUMN = range(6)

primal_step = 0.3
dual_step = 0.3
f32 = jnp.float32
bf16 = jnp.bfloat16


def shape(*dims, dtype=f32):
    return jax.ShapeDtypeStruct(dims, dtype)


def run(body, ins, outs):
    in_leaves, in_tree = jax.tree.flatten(ins)
    out_leaves, out_tree = jax.tree.flatten(outs)

    def kernel(*refs):
        given = jax.tree.unflatten(in_tree, refs[: len(in_leaves)])
        made = jax.tree.unflatten(out_tree, refs[len(in_leaves) :])
        body(Space(**given), Space(**made))

    def place(leaf):
        return pl.BlockSpec(memory_space=pltpu.SMEM if leaf.dtype == jnp.int32 else pltpu.VMEM)

    results = pl.pallas_call(
        kernel,
        out_shape=out_leaves,
        in_specs=[place(leaf) for leaf in in_leaves],
        out_specs=[place(leaf) for leaf in out_leaves],
        compiler_params=pltpu.CompilerParams(vmem_limit_bytes=LIMIT),
        name=body.__name__,
    )(*in_leaves)
    return Space(**jax.tree.unflatten(out_tree, results))


def row_iota(rows):
    return lax.broadcasted_iota(jnp.int32, (rows, LANES), 0)


def running_sum(block):
    rows = block.shape[0]
    at = row_iota(rows)
    step = 1
    while step < rows:
        block = block + jnp.where(at >= step, pltpu.roll(block, step, 0), 0.0)
        step *= 2
    return block


def tail_sum(block):
    rows = block.shape[0]
    at = row_iota(rows)
    step = 1
    while step < rows:
        block = block + jnp.where(at < rows - step, pltpu.roll(block, rows - step, 0), 0.0)
        step *= 2
    return block


def to_tile(block):
    rows = block.shape[0]
    total = block[0:8]
    for i in range(8, rows, 8):
        total = total + block[i : i + 8]
    return total


def product(left, high, low):
    rows = left.shape[0]
    left_high = left.astype(bf16)
    left_low = (left - left_high.astype(f32)).astype(bf16)
    both = jnp.dot(
        jnp.concatenate([left_high, left_low], axis=0), high, preferred_element_type=f32
    )
    rest = jnp.dot(left_high, low, preferred_element_type=f32)
    return both[:rows] + (both[rows:] + rest)


def split_matrix(matrix, column, turns):
    rows = matrix.shape[0]
    width = rows
    step = min(256, rows)
    places = {
        False: (shape(rows, width, dtype=bf16), pl.BlockSpec((step, width), lambda i, b: (i, 0))),
        True: (shape(width, rows, dtype=bf16), pl.BlockSpec((width, step), lambda i, b: (0, i))),
    }

    def split(_, source, *parts):
        for index, turned in enumerate(turns):
            value = source[...].T if turned else source[...]
            rounded = value.astype(bf16)
            parts[2 * index][...] = rounded
            parts[2 * index + 1][...] = (value - rounded.astype(f32)).astype(bf16)

    parts = pl.pallas_call(
        split,
        out_shape=[places[turned][0] for turned in turns for _ in range(2)],
        grid_spec=pltpu.PrefetchScalarGridSpec(
            num_scalar_prefetch=1,
            grid=(rows // step,),
            in_specs=[pl.BlockSpec((step, width), lambda i, b: (i, b[0]))],
            out_specs=[places[turned][1] for turned in turns for _ in range(2)],
        ),
        compiler_params=pltpu.CompilerParams(vmem_limit_bytes=2 * LIMIT),
    )(column, matrix)
    return [dict(high=parts[2 * i], low=parts[2 * i + 1]) for i in range(len(turns))]


def solve_rows(entries, values):
    size_n = len(values)
    entries = [list(row) for row in entries]
    values = list(values)
    for p in range(size_n):
        for i in range(p + 1, size_n):
            factor = entries[i][p] / entries[p][p]
            for j in range(p + 1, size_n):
                entries[i][j] = entries[i][j] - factor * entries[p][j]
            values[i] = values[i] - factor * values[p]
    result = [None] * size_n
    for i in range(size_n - 1, -1, -1):
        value = values[i]
        for j in range(i + 1, size_n):
            value = value - entries[i][j] * result[j]
        result[i] = value / entries[i][i]
    return result


def columns_at(iteration):
    return list(range(max(1, iteration - MEM + 1), iteration + 1))


def on_device(
    network,
    upper_bound,
    build_cost,
    unit_cost,
    demand,
    inflow,
    primal_start,
    network_start,
    energy_start,
    build_start,
    accepted,
    restarts,
):
    tm_count, bus_count = lax.axis_size("tm"), lax.axis_size("bus")
    tm, bus = lax.axis_index("tm"), lax.axis_index("bus")
    own_hours, width = primal_start.shape
    hours = SPAN * own_hours
    chunks = [slice(at, at + CHUNK) for at in range(0, hours, CHUNK)]
    flags = jnp.concatenate([accepted, restarts, tm.astype(jnp.int32).reshape(1)])
    first_restart, place_tm = accepted.shape[0], 2 * accepted.shape[0]
    member = shape(hours, width)
    line = shape(1, width)
    row = shape(1, LANES)
    tile = shape(ROWS, LANES)
    kind = {X: member, Y: member, E: member, U: line, SLOPE: member, COLUMN: line}

    upper_bound, build_cost, inflow, build_start = (
        value.reshape(1, width) for value in (upper_bound, build_cost, inflow, build_start)
    )

    def swap(value):
        return lax.ppermute(value, "bus", [(i, (i + 1) % bus_count) for i in range(bus_count)])

    def partner(value, distance):
        return lax.ppermute(value, "tm", [(i, i ^ distance) for i in range(tm_count)])

    distances = [SPAN << i for i in range((tm_count // SPAN).bit_length() - 1)]

    def gathered(value):
        arrived = []
        for distance in distances:
            if arrived:
                value = value + arrived[-1]
            arrived.append(partner(value, distance))
        return value, arrived


    def restart_of(ref, iteration):
        return ref[first_restart + iteration - 1].astype(f32)

    def counter_of(ref, iteration):
        count = jnp.float32(1.0)
        for k in range(1, iteration):
            count = (1.0 - restart_of(ref, k)) * count + 1.0
        return count

    def active_of(ref, column, iteration):
        value = jnp.float32(1.0)
        for k in range(column, iteration + 1):
            value = value * (1.0 - restart_of(ref, k))
        return value

    def weight_of(ref, rows):
        at = (ref[place_tm] // SPAN) * hours + rows.start + row_iota(CHUNK) + 1
        return 1.0 / at.astype(f32)

    def over_lanes(step, carried=()):
        def one(j, values):
            return step(pl.ds(pl.multiple_of(j * LANES, LANES), LANES), values)

        return lax.fori_loop(0, width // LANES, one, carried)

    def pair_keys(k, with_line):
        if k == 0:
            return []
        count = len(columns_at(k))
        return [
            (line_too, base + j)
            for line_too in ((False, True) if with_line else (False,))
            for base in (0, 8)
            for j in range(count)
        ]

    def over_pairs(k, step, with_line=False):
        keys = pair_keys(k, with_line)

        def one(sl, values):
            pairs = dict(zip(keys, values))
            step(sl, pairs)
            return tuple(pairs[key] for key in keys)

        zeros = tuple(jnp.zeros((1 if key[0] else 8, LANES), f32) for key in keys)
        return dict(zip(keys, over_lanes(one, zeros)))

    def on_diagonal():
        lane = lax.broadcasted_iota(jnp.int32, (ROWS, LANES), 1)
        return lane == row_iota(ROWS)

    def mixing(i, iteration, products, log):
        columns = columns_at(iteration)
        size_n = len(columns)
        spread = jnp.where(on_diagonal(), jnp.broadcast_to(products, (ROWS, LANES)), 0.0)
        newest = jnp.broadcast_to(jnp.sum(spread, axis=1, keepdims=True), (ROWS, LANES))
        summed = dict(zip(columns[:-1], [ref[...] for ref in i.log]))
        summed[iteration] = newest
        log[...] = newest
        active = [active_of(i.flags, k, iteration) for k in columns]

        def entry(a, b):
            a, b = max(a, b), min(a, b)
            at = columns_at(columns[a]).index(columns[b])
            return summed[columns[a]][at : at + 1]

        gram = [[entry(a, b) for b in range(size_n)] for a in range(size_n)]
        trace = gram[0][0] * active[0]
        for a in range(1, size_n):
            trace = trace + gram[a][a] * active[a]
        shift = 0.001 * trace / size_n + 1e-06
        system = [
            [gram[a][b] * (active[a] * active[b]) for b in range(size_n)] for a in range(size_n)
        ]
        for a in range(size_n):
            system[a][a] = system[a][a] + (1.0 - active[a]) + shift
        right = [newest[8 + a : 9 + a] * active[a] for a in range(size_n)]
        mix = solve_rows(system, right)
        accept = i.flags[iteration - 1].astype(f32)
        return [accept * (value * a) for value, a in zip(mix, active)]

    def mixed(mapped, deltas, coefs):
        if not coefs:
            return mapped
        correction = coefs[0] * deltas[0]
        for coef, delta in zip(coefs[1:], deltas[1:]):
            correction = correction + coef * delta
        return mapped - correction

    def restarted(ref, iteration, following, total):
        if iteration == 0:
            return following, None
        restart = restart_of(ref, iteration)
        total = following if total is None else total + following
        mean = total / counter_of(ref, iteration)
        return jnp.where(restart > 0.5, mean, following), (1.0 - restart) * total

    def begin(i, o, k, at, name, mapped, deltas, coefs):
        following = mixed(mapped, deltas, coefs)
        total = i.totals[name][at] if k >= 2 else None
        state, total = restarted(i.flags, k, following, total)
        if k >= 1:
            o.totals[name][at] = total
        return state

    def note(i, o, k, at, name, mapped, state, pairs):
        residual = mapped - state
        o.resid[name][at] = residual
        if k == 0:
            return
        o.delta[name][at] = mapped - i.last_map[name][at]
        newest = residual - i.resid[name][at]
        o.column[name][at] = newest
        for j, column in enumerate([ref[at] for ref in i.columns[name]] + [newest]):
            for index, other in ((j, newest), (8 + j, residual)):
                term = column * other
                if name != U:
                    term = to_tile(term)
                pairs[name == U, index] += term

    def pair_tile(pairs, scale=1.0):
        rows = []
        for index in range(ROWS):
            total = jnp.zeros((1, LANES), f32)
            if (False, index) in pairs:
                total = jnp.sum(pairs[False, index], axis=0, keepdims=True)
            if (True, index) in pairs:
                total = total + scale * pairs[True, index]
            rows.append(total)
        return jnp.concatenate(rows, axis=0)

    def beyond(ref, arrived, at, backward):
        total = jnp.zeros((1, LANES), f32)
        for distance, piece in zip(distances, arrived):
            first_half = (ref[place_tm] & distance) == 0
            take = first_half if backward else jnp.logical_not(first_half)
            total = total + jnp.where(take, piece[at], 0.0)
        return total

    def join(i, o):
        place = i.flags[place_tm] % SPAN
        for index, (own, out) in enumerate(zip(i.own, o.out)):
            for distance in range(SPAN):
                rows = pl.ds(pl.multiple_of((place ^ distance) * own_hours, own_hours), own_hours)
                if distance:
                    source = i.arrived[distance - 1]
                    out[rows, :] = source[index * own_hours : (index + 1) * own_hours, :]
                else:
                    out[rows, :] = own[...]


    def tails(i, o, sl):
        carry = jnp.zeros((1, LANES), f32)
        for rows in reversed(chunks):
            tail = tail_sum(i[rows, sl] * weight_of(o.flags, rows)) + carry
            o.tail[rows, sl] = tail
            carry = tail[0:1]
        o.block[:, sl] = carry

    def first(i, o):
        def step(sl, _):
            tails(i.energy, Space(flags=i.flags, tail=o.tail, block=o.block), sl)
            return ()

        over_lanes(step)

    def whole(i, sl):
        return i.message[:, sl] + i.arrived[-1][:, sl] if i.arrived else i.message[:, sl]

    def primal_kernel(k):
        count = len(columns_at(k - 1)) if k >= 2 else 0

        def primal(i, o):
            coefs = []
            if k >= 2:
                products = whole(i, slice(width, None))
                coefs = mixing(i, k - 1, products, o.log)
            for j, coef in enumerate(coefs):
                o.coefs[j : j + 1, :] = coef

            def step(sl, _):
                line_at = (slice(None), sl)

                def start(name, at, value):
                    deltas = [ref[at] for ref in i.deltas[name]] if count else []
                    if name in (SLOPE, COLUMN):
                        o.mapped[name][at] = value
                        if count:
                            newest = value - i.last_map[name][at]
                            o.delta[name][at] = newest
                            deltas.append(newest)
                    return begin(i, o, k, at, name, value, deltas, coefs)

                later = beyond(i.flags, i.arrived, line_at, True)
                column = start(COLUMN, line_at, whole(i, sl))
                build = start(U, line_at, i.mapped[U][line_at])
                next_build = jnp.maximum(
                    build - primal_step * (i.build_cost[line_at] - column), 0.0
                )
                o.state[U][line_at] = build
                o.mapped[U][line_at] = next_build
                block = jnp.zeros((8, LANES), f32)
                for rows in chunks:
                    at = (rows, sl)
                    slope = i.pulled[at] - (i.tail[at] + later)
                    slope = start(SLOPE, at, slope)
                    primal = start(X, at, i.mapped[X][at])
                    next_primal = jnp.clip(
                        primal - primal_step * (i.unit_cost[at] - slope),
                        0.0,
                        i.upper_bound[line_at],
                    )
                    bar = 2.0 * next_primal - primal
                    o.state[X][at] = primal
                    o.mapped[X][at] = next_primal
                    o.bar[at] = bar
                    block = block + to_tile(bar)
                o.block[line_at] = jnp.sum(block, axis=0, keepdims=True)
                return ()

            over_lanes(step)

        return primal

    def push_kernel(k):
        count = len(columns_at(k - 1)) if k >= 2 else 0

        def push(i, o):
            o.pushed[...] = product(i.bar[...], i.high[...], i.low[...])
            coefs = [i.coefs[j : j + 1, :] for j in range(count)]

            def step(sl, pairs):
                carry = jnp.zeros((1, LANES), f32)
                for rows in chunks:
                    at = (rows, sl)
                    for name in (Y, E):
                        deltas = [ref[at] for ref in i.deltas[name]] if count else []
                        o.state[name][at] = begin(
                            i, o, k, at, name, i.mapped[name][at], deltas, coefs
                        )
                    running = running_sum(i.bar[at]) + carry
                    o.running[at] = running
                    carry = running[CHUNK - 1 :]
                    note(i, o, k, at, X, i.next_primal[at], i.primal[at], pairs)

            o.pairs[...] = pair_tile(over_pairs(k, step))

        return push

    def dual_kernel(k):
        def dual(i, o):
            o.mapped[...] = i.pushed[...] + product(i.bar_other[...], i.high[...], i.low[...])

            def step(sl, pairs):
                for rows in chunks:
                    at = (rows, sl)
                    state = i.state[at]
                    mapped = jnp.maximum(state + dual_step * (i.demand[at] - o.mapped[at]), 0.0)
                    o.mapped[at] = mapped
                    note(i, o, k, at, Y, mapped, state, pairs)

            o.pairs[...] = i.pairs[...] + pair_tile(over_pairs(k, step))

        return dual

    def energy_kernel(k):
        def energy(i, o):
            own_build = (i.flags[place_tm] < SPAN).astype(f32)

            def step(sl, pairs):
                line_at = (slice(None), sl)
                earlier = beyond(i.flags, i.arrived, line_at, False)
                build, next_build = i.state[U][line_at], i.mapped[line_at]
                bar_build = 2.0 * next_build - build
                note(i, o, k, line_at, U, next_build, build, pairs)
                for rows in chunks:
                    at = (rows, sl)
                    running = i.running[at] + earlier
                    state = i.state[E][at]
                    slack = (bar_build - running) * weight_of(i.flags, rows)
                    mapped = jnp.maximum(
                        state + dual_step * (-i.inflow[line_at] - slack), 0.0
                    )
                    o.mapped[at] = mapped
                    note(i, o, k, at, E, mapped, state, pairs)
                if k < ITERS - 1:
                    tails(o.mapped, Space(flags=i.flags, tail=o.tail, block=o.block), sl)

            pairs = over_pairs(k, step, True)
            if k >= 1:
                lines = i.pairs[...] + pair_tile(pairs, own_build)
                sums = jnp.broadcast_to(jnp.sum(lines, axis=1, keepdims=True), (ROWS, LANES))
                o.products[...] = jnp.sum(
                    jnp.where(on_diagonal(), sums, 0.0), axis=0, keepdims=True
                )
            else:
                o.products[...] = jnp.zeros((1, LANES), f32)

        return energy

    def pull(i, o):
        o.pulled[...] = product(i.dual[...], i.own[0][...], i.own[1][...])
        o.pulled[...] += product(i.dual_other[...], i.other[0][...], i.other[1][...])

    def last_kernel(i, o):
        place = i.flags[place_tm] % SPAN
        own = pl.ds(pl.multiple_of(place * own_hours, own_hours), own_hours)
        coefs = mixing(i, ITERS - 1, whole(i, slice(None)), o.log)

        def step(sl, _):
            for name in (X, Y, E, U):
                at = (slice(None) if name == U else own, sl)
                deltas = [ref[at] for ref in i.deltas[name]]
                o.following[name][:, sl] = mixed(i.mapped[name][at], deltas, coefs)
            return ()

        over_lanes(step)


    deltas = {name: [] for name in kind}
    columns = {name: [] for name in (X, Y, E, U)}
    totals, last_map, resid, logs = {}, {}, {}, {}

    def send_totals(block, products, dual, dual_other):
        row = block
        if products is not None:
            row = jnp.concatenate([block, products + swap(products)], axis=1)
        row, arrived = gathered(row)
        out = run(
            pull,
            dict(
                dual=dual,
                dual_other=dual_other,
                own=[pull_own[part] for part in sorted(pull_own)],
                other=[pull_other[part] for part in sorted(pull_other)],
            ),
            dict(pulled=member),
        )
        return dict(message=row, arrived=arrived, pulled=out.pulled)

    def picked(source, names):
        return {name: source[name] for name in names}

    def kinds(*names):
        return picked(kind, names)

    def note_ins(k, names):
        if k == 0:
            return {}
        return dict(
            last_map=picked(last_map, names),
            resid=picked(resid, names),
            columns={name: columns[name][-(MEM - 1) :] for name in names},
        )

    def note_outs(k, names):
        each = kinds(*names)
        return dict(resid=each, **(dict(delta=each, column=each) if k else {}))

    def take(k, out, names):
        for name in names:
            resid[name] = out.resid[name]
            if k:
                deltas[name] = (deltas[name] + [out.delta[name]])[-MEM:]
                columns[name] = (columns[name] + [out.column[name]])[-MEM:]

    def log_ins(iteration):
        return [logs[j] for j in columns_at(iteration)[:-1]]

    def from_neighbours(stack):
        return [partner(stack, distance) for distance in range(1, SPAN)]

    def with_neighbours(arrays, arrived):
        return run(
            join,
            dict(flags=flags, own=arrays, arrived=arrived),
            dict(out=[member] * len(arrays)),
        ).out

    starts = [primal_start, network_start, energy_start, unit_cost]
    stack, network = lax.optimization_barrier((jnp.concatenate(starts, axis=0), network))
    arrived = from_neighbours(stack)
    place = bus.astype(jnp.int32).reshape(1)
    pull_own, push_own = split_matrix(network, place, (False, True))
    (push_other,) = split_matrix(network, 1 - place, (True,))
    elsewhere = swap(lax.dynamic_slice(network, (0, (1 - bus) * width), (width, width)))
    (pull_other,) = split_matrix(elsewhere, jnp.zeros_like(place), (False,))
    arrived, pull_own, push_own, pull_other, push_other = lax.optimization_barrier(
        (arrived, pull_own, push_own, pull_other, push_other)
    )
    primal, dual, energy, unit_cost = with_neighbours(starts, arrived)
    (demand,) = with_neighbours([demand], from_neighbours(demand))
    out = run(first, dict(flags=flags, energy=energy), dict(tail=member, block=line))
    tail, block = out.tail, out.block
    mapped = {X: primal, Y: dual, E: energy, U: build_start}
    totals_in = send_totals(block, None, dual, swap(dual))

    for k in range(ITERS):
        mixes = k >= 2
        ins = dict(
            flags=flags,
            **totals_in,
            tail=tail,
            mapped=picked(mapped, (X, U)),
            unit_cost=unit_cost,
            upper_bound=upper_bound,
            build_cost=build_cost,
        )
        outs = dict(
            mapped=kinds(SLOPE, COLUMN, X, U),
            state=kinds(X, U),
            bar=member,
            block=line,
        )
        if mixes:
            ins.update(
                log=log_ins(k - 1),
                last_map=picked(last_map, (SLOPE, COLUMN)),
                totals=picked(totals, (SLOPE, COLUMN, X, U)),
                deltas={
                    SLOPE: deltas[SLOPE][-(MEM - 1) :],
                    COLUMN: deltas[COLUMN][-(MEM - 1) :],
                    X: deltas[X],
                    U: deltas[U],
                },
            )
            outs.update(log=tile, coefs=shape(8, LANES), delta=kinds(SLOPE, COLUMN))
        if k >= 1:
            outs.update(totals=kinds(SLOPE, COLUMN, X, U))
        one = run(primal_kernel(k), ins, outs)
        if mixes:
            logs[k - 1] = one.log
            for name in (SLOPE, COLUMN):
                deltas[name] = (deltas[name] + [one.delta[name]])[-MEM:]
        for name in (SLOPE, COLUMN):
            last_map[name] = one.mapped[name]
        if k >= 1:
            totals.update(one.totals)
        _, earlier = gathered(one.block)
        bar_other = swap(one.bar)

        ins = dict(
            flags=flags,
            bar=one.bar,
            next_primal=one.mapped[X],
            primal=one.state[X],
            mapped=picked(mapped, (Y, E)),
            **push_own,
            **note_ins(k, (X,)),
        )
        outs = dict(
            pushed=member,
            state=kinds(Y, E),
            running=member,
            pairs=tile,
            **note_outs(k, (X,)),
        )
        if mixes:
            ins.update(
                coefs=one.coefs, deltas=picked(deltas, (Y, E)), totals=picked(totals, (Y, E))
            )
        if k >= 1:
            outs.update(totals=kinds(Y, E))
        two = run(push_kernel(k), ins, outs)
        if k >= 1:
            totals.update(two.totals)

        three = run(
            dual_kernel(k),
            dict(
                pushed=two.pushed,
                bar_other=bar_other,
                state=two.state[Y],
                demand=demand,
                pairs=two.pairs,
                **push_other,
                **note_ins(k, (Y,)),
            ),
            dict(mapped=member, pairs=tile, **note_outs(k, (Y,))),
        )
        four = run(
            energy_kernel(k),
            dict(
                flags=flags,
                running=two.running,
                arrived=earlier,
                state={E: two.state[E], U: one.state[U]},
                mapped=one.mapped[U],
                inflow=inflow,
                pairs=three.pairs,
                **note_ins(k, (E, U)),
            ),
            dict(
                mapped=member,
                products=row,
                **(dict(tail=member, block=line) if k < ITERS - 1 else {}),
                **note_outs(k, (E, U)),
            ),
        )
        take(k, two, (X,))
        take(k, three, (Y,))
        take(k, four, (E, U))
        mapped = {X: one.mapped[X], Y: three.mapped, E: four.mapped, U: one.mapped[U]}
        last_map.update(mapped)
        if k < ITERS - 1:
            tail = four.tail
            dual, products = lax.optimization_barrier((mapped[Y], four.products))
            totals_in = send_totals(four.block, products, dual, swap(dual))

    products = four.products + swap(four.products)
    message, arrived = gathered(products)
    out = run(
        last_kernel,
        dict(
            flags=flags,
            message=message,
            arrived=arrived,
            log=log_ins(ITERS - 1),
            mapped=mapped,
            deltas=picked(deltas, (X, Y, E, U)),
        ),
        dict(
            log=tile,
            following={name: line if name == U else shape(own_hours, width) for name in (X, Y, E, U)},
        ),
    )
    final = out.following
    return final[X], final[Y], final[E], final[U].reshape(width)


def solution(mesh):
    hourly = P(("grp", "tm"), "bus")
    return jax.shard_map(
        on_device,
        mesh=mesh,
        in_specs=(
            P("bus", None),
            P("bus"),
            P("bus"),
            hourly,
            hourly,
            P(("grp", "bus")),
            hourly,
            hourly,
            hourly,
            P(("grp", "bus")),
            P("grp"),
            P("grp"),
        ),
        out_specs=(hourly, hourly, hourly, P(("grp", "bus"))),
        check_vma=False,
    )
```

```python
from types import SimpleNamespace as Space

import jax
import jax.numpy as jnp
from jax import lax
from jax.experimental import pallas as pl
from jax.experimental.pallas import tpu as pltpu
from jax.sharding import PartitionSpec as P

ITERS = 9
MEM = 5
LANES = 128
ROWS = 16
LIMIT = 6 * 1024 * 1024
SPAN = 4
CHUNK = 32
X, Y, E, U, SLOPE, COLUMN = range(6)

primal_step = 0.3
dual_step = 0.3
f32 = jnp.float32
bf16 = jnp.bfloat16


def shape(*dims, dtype=f32):
    return jax.ShapeDtypeStruct(dims, dtype)


def run(body, ins, outs):
    in_leaves, in_tree = jax.tree.flatten(ins)
    out_leaves, out_tree = jax.tree.flatten(outs)

    def kernel(*refs):
        given = jax.tree.unflatten(in_tree, refs[: len(in_leaves)])
        made = jax.tree.unflatten(out_tree, refs[len(in_leaves) :])
        body(Space(**given), Space(**made))

    def place(leaf):
        return pl.BlockSpec(memory_space=pltpu.SMEM if leaf.dtype == jnp.int32 else pltpu.VMEM)

    results = pl.pallas_call(
        kernel,
        out_shape=out_leaves,
        in_specs=[place(leaf) for leaf in in_leaves],
        out_specs=[place(leaf) for leaf in out_leaves],
        compiler_params=pltpu.CompilerParams(vmem_limit_bytes=LIMIT),
        name=body.__name__,
    )(*in_leaves)
    return Space(**jax.tree.unflatten(out_tree, results))


def row_iota(rows):
    return lax.broadcasted_iota(jnp.int32, (rows, LANES), 0)


def tail_sum(block):
    rows = block.shape[0]
    at = row_iota(rows)
    step = 1
    while step < rows:
        block = block + jnp.where(at < rows - step, pltpu.roll(block, rows - step, 0), 0.0)
        step *= 2
    return block


def to_tile(block):
    rows = block.shape[0]
    total = block[0:8]
    for i in range(8, rows, 8):
        total = total + block[i : i + 8]
    return total


def halves(value):
    high = value.astype(bf16)
    return high, (value - high.astype(f32)).astype(bf16)


def product(left, high, low):
    left_high, left_low = left
    rows = left_high.shape[0]
    both = jnp.dot(
        jnp.concatenate([left_high, left_low], axis=0), high, preferred_element_type=f32
    )
    rest = jnp.dot(left_high, low, preferred_element_type=f32)
    return both[:rows] + (both[rows:] + rest)


def running_sum(parts):
    rows = parts[0].shape[0]
    at = lax.broadcasted_iota(jnp.int32, (rows, rows), 0)
    ones = (at >= lax.broadcasted_iota(jnp.int32, (rows, rows), 1)).astype(f32).astype(bf16)
    high, low = (jnp.dot(ones, part, preferred_element_type=f32) for part in parts)
    return high + low


def split_matrix(matrix, column, turns):
    rows = matrix.shape[0]
    width = rows
    step = min(256, rows)
    places = {
        False: (shape(rows, width, dtype=bf16), pl.BlockSpec((step, width), lambda i, b: (i, 0))),
        True: (shape(width, rows, dtype=bf16), pl.BlockSpec((width, step), lambda i, b: (0, i))),
    }

    def split(_, source, *parts):
        for index, turned in enumerate(turns):
            value = source[...].T if turned else source[...]
            parts[2 * index][...], parts[2 * index + 1][...] = halves(value)

    parts = pl.pallas_call(
        split,
        out_shape=[places[turned][0] for turned in turns for _ in range(2)],
        grid_spec=pltpu.PrefetchScalarGridSpec(
            num_scalar_prefetch=1,
            grid=(rows // step,),
            in_specs=[pl.BlockSpec((step, width), lambda i, b: (i, b[0]))],
            out_specs=[places[turned][1] for turned in turns for _ in range(2)],
        ),
        compiler_params=pltpu.CompilerParams(vmem_limit_bytes=2 * LIMIT),
    )(column, matrix)
    return [dict(high=parts[2 * i], low=parts[2 * i + 1]) for i in range(len(turns))]


def solve_rows(entries, values):
    size_n = len(values)
    entries = [list(row) for row in entries]
    values = list(values)
    for p in range(size_n):
        for i in range(p + 1, size_n):
            factor = entries[i][p] / entries[p][p]
            for j in range(p + 1, size_n):
                entries[i][j] = entries[i][j] - factor * entries[p][j]
            values[i] = values[i] - factor * values[p]
    result = [None] * size_n
    for i in range(size_n - 1, -1, -1):
        value = values[i]
        for j in range(i + 1, size_n):
            value = value - entries[i][j] * result[j]
        result[i] = value / entries[i][i]
    return result


def columns_at(iteration):
    return list(range(max(1, iteration - MEM + 1), iteration + 1))


def on_device(
    network,
    upper_bound,
    build_cost,
    unit_cost,
    demand,
    inflow,
    primal_start,
    network_start,
    energy_start,
    build_start,
    accepted,
    restarts,
):
    tm_count, bus_count = lax.axis_size("tm"), lax.axis_size("bus")
    tm, bus = lax.axis_index("tm"), lax.axis_index("bus")
    own_hours, width = primal_start.shape
    hours = SPAN * own_hours
    chunks = [slice(at, at + CHUNK) for at in range(0, hours, CHUNK)]
    flags = jnp.concatenate([accepted, restarts, tm.astype(jnp.int32).reshape(1)])
    first_restart, place_tm = accepted.shape[0], 2 * accepted.shape[0]
    member = shape(hours, width)
    line = shape(1, width)
    row = shape(1, LANES)
    tile = shape(ROWS, LANES)
    kind = {X: member, Y: member, E: member, U: line, SLOPE: member, COLUMN: line}

    upper_bound, build_cost, inflow, build_start = (
        value.reshape(1, width) for value in (upper_bound, build_cost, inflow, build_start)
    )

    def swap(value):
        return lax.ppermute(value, "bus", [(i, (i + 1) % bus_count) for i in range(bus_count)])

    def partner(value, distance):
        return lax.ppermute(value, "tm", [(i, i ^ distance) for i in range(tm_count)])

    distances = [SPAN << i for i in range((tm_count // SPAN).bit_length() - 1)]

    def gathered(value):
        arrived = []
        for distance in distances:
            if arrived:
                value = value + arrived[-1]
            arrived.append(partner(value, distance))
        return value, arrived


    def restart_of(ref, iteration):
        return ref[first_restart + iteration - 1].astype(f32)

    def counter_of(ref, iteration):
        count = jnp.float32(1.0)
        for k in range(1, iteration):
            count = (1.0 - restart_of(ref, k)) * count + 1.0
        return count

    def active_of(ref, column, iteration):
        value = jnp.float32(1.0)
        for k in range(column, iteration + 1):
            value = value * (1.0 - restart_of(ref, k))
        return value

    def weight_of(ref, rows):
        at = (ref[place_tm] // SPAN) * hours + rows.start + row_iota(CHUNK) + 1
        return 1.0 / at.astype(f32)

    def over_lanes(step, carried=()):
        def one(j, values):
            return step(pl.ds(pl.multiple_of(j * LANES, LANES), LANES), values)

        return lax.fori_loop(0, width // LANES, one, carried)

    def pair_keys(k, with_line):
        if k == 0:
            return []
        count = len(columns_at(k))
        return [
            (line_too, base + j)
            for line_too in ((False, True) if with_line else (False,))
            for base in (0, 8)
            for j in range(count)
        ]

    def over_pairs(k, step, with_line=False):
        keys = pair_keys(k, with_line)

        def one(sl, values):
            pairs = dict(zip(keys, values))
            step(sl, pairs)
            return tuple(pairs[key] for key in keys)

        zeros = tuple(jnp.zeros((1 if key[0] else 8, LANES), f32) for key in keys)
        return dict(zip(keys, over_lanes(one, zeros)))

    def on_diagonal():
        lane = lax.broadcasted_iota(jnp.int32, (ROWS, LANES), 1)
        return lane == row_iota(ROWS)

    def mixing(i, iteration, products, log):
        columns = columns_at(iteration)
        size_n = len(columns)
        spread = jnp.where(on_diagonal(), jnp.broadcast_to(products, (ROWS, LANES)), 0.0)
        newest = jnp.broadcast_to(jnp.sum(spread, axis=1, keepdims=True), (ROWS, LANES))
        summed = dict(zip(columns[:-1], [ref[...] for ref in i.log]))
        summed[iteration] = newest
        log[...] = newest
        active = [active_of(i.flags, k, iteration) for k in columns]

        def entry(a, b):
            a, b = max(a, b), min(a, b)
            at = columns_at(columns[a]).index(columns[b])
            return summed[columns[a]][at : at + 1]

        gram = [[entry(a, b) for b in range(size_n)] for a in range(size_n)]
        trace = gram[0][0] * active[0]
        for a in range(1, size_n):
            trace = trace + gram[a][a] * active[a]
        shift = 0.001 * trace / size_n + 1e-06
        system = [
            [gram[a][b] * (active[a] * active[b]) for b in range(size_n)] for a in range(size_n)
        ]
        for a in range(size_n):
            system[a][a] = system[a][a] + (1.0 - active[a]) + shift
        right = [newest[8 + a : 9 + a] * active[a] for a in range(size_n)]
        mix = solve_rows(system, right)
        accept = i.flags[iteration - 1].astype(f32)
        return [accept * (value * a) for value, a in zip(mix, active)]

    def mixed(mapped, deltas, coefs):
        if not coefs:
            return mapped
        correction = coefs[0] * deltas[0]
        for coef, delta in zip(coefs[1:], deltas[1:]):
            correction = correction + coef * delta
        return mapped - correction

    def restarted(ref, iteration, following, total):
        if iteration == 0:
            return following, None
        restart = restart_of(ref, iteration)
        total = following if total is None else total + following
        mean = total / counter_of(ref, iteration)
        return jnp.where(restart > 0.5, mean, following), (1.0 - restart) * total

    def begin(i, o, k, at, name, mapped, deltas, coefs):
        following = mixed(mapped, deltas, coefs)
        total = i.totals[name][at] if k >= 2 else None
        state, total = restarted(i.flags, k, following, total)
        if 1 <= k < ITERS - 1:
            o.totals[name][at] = total
        return state

    def note(i, o, k, at, name, mapped, state, pairs):
        residual = mapped - state
        if k < ITERS - 1:
            o.resid[name][at] = residual
        if k == 0:
            return
        o.delta[name][at] = mapped - i.last_map[name][at]
        newest = residual - i.resid[name][at]
        o.column[name][at] = newest
        for j, column in enumerate([ref[at] for ref in i.columns[name]] + [newest]):
            for index, other in ((j, newest), (8 + j, residual)):
                term = column * other
                if name != U:
                    term = to_tile(term)
                pairs[name == U, index] += term

    def pair_tile(pairs, scale=1.0):
        rows = []
        for index in range(ROWS):
            total = jnp.zeros((1, LANES), f32)
            if (False, index) in pairs:
                total = jnp.sum(pairs[False, index], axis=0, keepdims=True)
            if (True, index) in pairs:
                total = total + scale * pairs[True, index]
            rows.append(total)
        return jnp.concatenate(rows, axis=0)

    def beyond(ref, arrived, at, backward):
        total = jnp.zeros((1, LANES), f32)
        for distance, piece in zip(distances, arrived):
            first_half = (ref[place_tm] & distance) == 0
            take = first_half if backward else jnp.logical_not(first_half)
            total = total + jnp.where(take, piece[at], 0.0)
        return total

    def join(i, o):
        place = i.flags[place_tm] % SPAN
        for index, (own, out) in enumerate(zip(i.own, o.out)):
            for distance in range(SPAN):
                rows = pl.ds(pl.multiple_of((place ^ distance) * own_hours, own_hours), own_hours)
                first = index * own_hours
                if distance == 0:
                    out[rows, :] = own[...]
                elif distance < 3:
                    out[rows, :] = i.arrived[distance - 1][first : first + own_hours, :]
                elif index < early:
                    out[rows, :] = i.arrived[2][first : first + own_hours, :]
                else:
                    first = first - early * own_hours
                    out[rows, :] = i.arrived[3][first : first + own_hours, :]


    def tails(i, o, sl):
        carry = jnp.zeros((1, LANES), f32)
        for rows in reversed(chunks):
            tail = tail_sum(i[rows, sl] * weight_of(o.flags, rows)) + carry
            o.tail[rows, sl] = tail
            carry = tail[0:1]
        o.block[:, sl] = carry

    def first(i, o):
        def step(sl, _):
            tails(i.energy, Space(flags=i.flags, tail=o.tail, block=o.block), sl)
            return ()

        over_lanes(step)

    def whole(i, sl):
        return i.message[:, sl] + i.arrived[-1][:, sl] if i.arrived else i.message[:, sl]

    def primal_kernel(k):
        count = len(columns_at(k - 1)) if k >= 2 else 0

        def primal(i, o):
            coefs = []
            if k >= 2:
                products = whole(i, slice(width, None))
                coefs = mixing(i, k - 1, products, o.log)
            for j, coef in enumerate(coefs):
                o.coefs[j : j + 1, :] = coef

            def step(sl, _):
                line_at = (slice(None), sl)

                def start(name, at, value):
                    deltas = [ref[at] for ref in i.deltas[name]] if count else []
                    if name in (SLOPE, COLUMN):
                        if k < ITERS - 1:
                            o.mapped[name][at] = value
                        if count:
                            newest = value - i.last_map[name][at]
                            if k < ITERS - 1:
                                o.delta[name][at] = newest
                            deltas.append(newest)
                    return begin(i, o, k, at, name, value, deltas, coefs)

                later = beyond(i.flags, i.arrived, line_at, True)
                column = start(COLUMN, line_at, whole(i, sl))
                build = start(U, line_at, i.mapped[U][line_at])
                next_build = jnp.maximum(
                    build - primal_step * (i.build_cost[line_at] - column), 0.0
                )
                o.state[U][line_at] = build
                o.mapped[U][line_at] = next_build
                block = jnp.zeros((8, LANES), f32)
                for rows in chunks:
                    at = (rows, sl)
                    slope = i.pulled[at] - (i.tail[at] + later)
                    slope = start(SLOPE, at, slope)
                    primal = start(X, at, i.mapped[X][at])
                    next_primal = jnp.clip(
                        primal - primal_step * (i.unit_cost[at] - slope),
                        0.0,
                        i.upper_bound[line_at],
                    )
                    bar = 2.0 * next_primal - primal
                    o.state[X][at] = primal
                    o.mapped[X][at] = next_primal
                    o.bar[at] = bar
                    block = block + to_tile(bar)
                o.block[line_at] = jnp.sum(block, axis=0, keepdims=True)
                return ()

            over_lanes(step)

        return primal

    def push_kernel(k):
        count = len(columns_at(k - 1)) if k >= 2 else 0

        def push(i, o):
            bar = halves(i.bar[...])
            o.pushed[...] = product(bar, i.high[...], i.low[...])
            o.running[...] = running_sum(bar)
            coefs = [i.coefs[j : j + 1, :] for j in range(count)]

            def step(sl, pairs):
                for rows in chunks:
                    at = (rows, sl)
                    for name in (Y, E):
                        deltas = [ref[at] for ref in i.deltas[name]] if count else []
                        o.state[name][at] = begin(
                            i, o, k, at, name, i.mapped[name][at], deltas, coefs
                        )
                    note(i, o, k, at, X, i.next_primal[at], i.primal[at], pairs)

            o.pairs[...] = pair_tile(over_pairs(k, step))

        return push

    def dual_kernel(k):
        def dual(i, o):
            o.mapped[...] = i.pushed[...] + product(halves(i.bar_other[...]), i.high[...], i.low[...])

            def step(sl, pairs):
                for rows in chunks:
                    at = (rows, sl)
                    state = i.state[at]
                    mapped = jnp.maximum(state + dual_step * (i.demand[at] - o.mapped[at]), 0.0)
                    o.mapped[at] = mapped
                    note(i, o, k, at, Y, mapped, state, pairs)

            o.pairs[...] = i.pairs[...] + pair_tile(over_pairs(k, step))

        return dual

    def energy_kernel(k):
        def energy(i, o):
            own_build = (i.flags[place_tm] < SPAN).astype(f32)

            def step(sl, pairs):
                line_at = (slice(None), sl)
                earlier = beyond(i.flags, i.arrived, line_at, False)
                build, next_build = i.state[U][line_at], i.mapped[line_at]
                bar_build = 2.0 * next_build - build
                note(i, o, k, line_at, U, next_build, build, pairs)
                for rows in chunks:
                    at = (rows, sl)
                    running = i.running[at] + earlier
                    state = i.state[E][at]
                    slack = (bar_build - running) * weight_of(i.flags, rows)
                    mapped = jnp.maximum(
                        state + dual_step * (-i.inflow[line_at] - slack), 0.0
                    )
                    o.mapped[at] = mapped
                    note(i, o, k, at, E, mapped, state, pairs)
                if k < ITERS - 1:
                    tails(o.mapped, Space(flags=i.flags, tail=o.tail, block=o.block), sl)

            pairs = over_pairs(k, step, True)
            if k >= 1:
                lines = i.pairs[...] + pair_tile(pairs, own_build)
                sums = jnp.broadcast_to(jnp.sum(lines, axis=1, keepdims=True), (ROWS, LANES))
                o.products[...] = jnp.sum(
                    jnp.where(on_diagonal(), sums, 0.0), axis=0, keepdims=True
                )
            else:
                o.products[...] = jnp.zeros((1, LANES), f32)

        return energy

    def pull(i, o):
        o.pulled[...] = product(halves(i.dual[...]), i.own[0][...], i.own[1][...])
        o.pulled[...] += product(halves(i.dual_other[...]), i.other[0][...], i.other[1][...])

    def last_kernel(i, o):
        place = i.flags[place_tm] % SPAN
        own = pl.ds(pl.multiple_of(place * own_hours, own_hours), own_hours)
        coefs = mixing(i, ITERS - 1, whole(i, slice(None)), o.log)

        def step(sl, _):
            for name in (X, Y, E, U):
                at = (slice(None) if name == U else own, sl)
                deltas = [ref[at] for ref in i.deltas[name]]
                o.following[name][:, sl] = mixed(i.mapped[name][at], deltas, coefs)
            return ()

        over_lanes(step)


    deltas = {name: [] for name in kind}
    columns = {name: [] for name in (X, Y, E, U)}
    totals, last_map, resid, logs = {}, {}, {}, {}

    def send_totals(block, products, dual, dual_other):
        row = block
        if products is not None:
            row = jnp.concatenate([block, products + swap(products)], axis=1)
        row, arrived = gathered(row)
        out = run(
            pull,
            dict(
                dual=dual,
                dual_other=dual_other,
                own=[pull_own[part] for part in sorted(pull_own)],
                other=[pull_other[part] for part in sorted(pull_other)],
            ),
            dict(pulled=member),
        )
        return dict(message=row, arrived=arrived, pulled=out.pulled)

    def picked(source, names):
        return {name: source[name] for name in names}

    def kinds(*names):
        return picked(kind, names)

    def note_ins(k, names):
        if k == 0:
            return {}
        return dict(
            last_map=picked(last_map, names),
            resid=picked(resid, names),
            columns={name: columns[name][-(MEM - 1) :] for name in names},
        )

    def note_outs(k, names):
        each = kinds(*names)
        return dict(
            **(dict(resid=each) if k < ITERS - 1 else {}),
            **(dict(delta=each, column=each) if k else {}),
        )

    def take(k, out, names):
        for name in names:
            if k < ITERS - 1:
                resid[name] = out.resid[name]
            if k:
                deltas[name] = (deltas[name] + [out.delta[name]])[-MEM:]
                columns[name] = (columns[name] + [out.column[name]])[-MEM:]

    def log_ins(iteration):
        return [logs[j] for j in columns_at(iteration)[:-1]]

    starts = [primal_start, network_start, energy_start, unit_cost, demand]
    early = 3
    stack = jnp.concatenate(starts, axis=0)
    near, far = partner(stack, 1), partner(stack, 2)
    place = bus.astype(jnp.int32).reshape(1)
    pull_own, push_own = split_matrix(network, place, (False, True))
    (push_other,) = split_matrix(network, 1 - place, (True,))
    (pull_other,) = split_matrix(swap(network), place, (False,))
    near, far, pull_own, push_own, push_other = lax.optimization_barrier(
        (near, far, pull_own, push_own, push_other)
    )
    across = [partner(near[: early * own_hours], 2), partner(far[early * own_hours :], 1)]
    across, pull_other = lax.optimization_barrier((across, pull_other))
    primal, dual, energy, unit_cost, demand = run(
        join,
        dict(flags=flags, own=starts, arrived=[near, far, *across]),
        dict(out=[member] * len(starts)),
    ).out
    out = run(first, dict(flags=flags, energy=energy), dict(tail=member, block=line))
    tail, block = out.tail, out.block
    mapped = {X: primal, Y: dual, E: energy, U: build_start}
    totals_in = send_totals(block, None, dual, swap(dual))

    for k in range(ITERS):
        mixes = k >= 2
        ins = dict(
            flags=flags,
            **totals_in,
            tail=tail,
            mapped=picked(mapped, (X, U)),
            unit_cost=unit_cost,
            upper_bound=upper_bound,
            build_cost=build_cost,
        )
        outs = dict(
            mapped=kinds(X, U) if k == ITERS - 1 else kinds(SLOPE, COLUMN, X, U),
            state=kinds(X, U),
            bar=member,
            block=line,
        )
        if mixes:
            ins.update(
                log=log_ins(k - 1),
                last_map=picked(last_map, (SLOPE, COLUMN)),
                totals=picked(totals, (SLOPE, COLUMN, X, U)),
                deltas={
                    SLOPE: deltas[SLOPE][-(MEM - 1) :],
                    COLUMN: deltas[COLUMN][-(MEM - 1) :],
                    X: deltas[X],
                    U: deltas[U],
                },
            )
            outs.update(log=tile, coefs=shape(8, LANES))
            if k < ITERS - 1:
                outs.update(delta=kinds(SLOPE, COLUMN))
        if 1 <= k < ITERS - 1:
            outs.update(totals=kinds(SLOPE, COLUMN, X, U))
        one = run(primal_kernel(k), ins, outs)
        if mixes:
            logs[k - 1] = one.log
        if mixes and k < ITERS - 1:
            for name in (SLOPE, COLUMN):
                deltas[name] = (deltas[name] + [one.delta[name]])[-MEM:]
        if k < ITERS - 1:
            last_map.update(picked(one.mapped, (SLOPE, COLUMN)))
        if 1 <= k < ITERS - 1:
            totals.update(one.totals)
        _, earlier = gathered(one.block)
        bar_other = swap(one.bar)

        ins = dict(
            flags=flags,
            bar=one.bar,
            next_primal=one.mapped[X],
            primal=one.state[X],
            mapped=picked(mapped, (Y, E)),
            **push_own,
            **note_ins(k, (X,)),
        )
        outs = dict(
            pushed=member,
            state=kinds(Y, E),
            running=member,
            pairs=tile,
            **note_outs(k, (X,)),
        )
        if mixes:
            ins.update(
                coefs=one.coefs, deltas=picked(deltas, (Y, E)), totals=picked(totals, (Y, E))
            )
        if 1 <= k < ITERS - 1:
            outs.update(totals=kinds(Y, E))
        two = run(push_kernel(k), ins, outs)
        if 1 <= k < ITERS - 1:
            totals.update(two.totals)

        three = run(
            dual_kernel(k),
            dict(
                pushed=two.pushed,
                bar_other=bar_other,
                state=two.state[Y],
                demand=demand,
                pairs=two.pairs,
                **push_other,
                **note_ins(k, (Y,)),
            ),
            dict(mapped=member, pairs=tile, **note_outs(k, (Y,))),
        )
        four = run(
            energy_kernel(k),
            dict(
                flags=flags,
                running=two.running,
                arrived=earlier,
                state={E: two.state[E], U: one.state[U]},
                mapped=one.mapped[U],
                inflow=inflow,
                pairs=three.pairs,
                **note_ins(k, (E, U)),
            ),
            dict(
                mapped=member,
                products=row,
                **(dict(tail=member, block=line) if k < ITERS - 1 else {}),
                **note_outs(k, (E, U)),
            ),
        )
        take(k, two, (X,))
        take(k, three, (Y,))
        take(k, four, (E, U))
        mapped = {X: one.mapped[X], Y: three.mapped, E: four.mapped, U: one.mapped[U]}
        last_map.update(mapped)
        if k < ITERS - 1:
            tail = four.tail
            dual, products = lax.optimization_barrier((mapped[Y], four.products))
            totals_in = send_totals(four.block, products, dual, swap(dual))

    products = four.products + swap(four.products)
    message, arrived = gathered(products)
    out = run(
        last_kernel,
        dict(
            flags=flags,
            message=message,
            arrived=arrived,
            log=log_ins(ITERS - 1),
            mapped=mapped,
            deltas=picked(deltas, (X, Y, E, U)),
        ),
        dict(
            log=tile,
            following={name: line if name == U else shape(own_hours, width) for name in (X, Y, E, U)},
        ),
    )
    final = out.following
    return final[X], final[Y], final[E], final[U].reshape(width)


def solution(mesh):
    hourly = P(("grp", "tm"), "bus")
    return jax.shard_map(
        on_device,
        mesh=mesh,
        in_specs=(
            P("bus", None),
            P("bus"),
            P("bus"),
            hourly,
            hourly,
            P(("grp", "bus")),
            hourly,
            hourly,
            hourly,
            P(("grp", "bus")),
            P("grp"),
            P("grp"),
        ),
        out_specs=(hourly, hourly, hourly, P(("grp", "bus"))),
        check_vma=False,
    )
```

```python
from types import SimpleNamespace as Space

import jax
import jax.numpy as jnp
from jax import lax
from jax.experimental import pallas as pl
from jax.experimental.pallas import tpu as pltpu
from jax.sharding import PartitionSpec as P

ITERS = 9
MEM = 5
LANES = 128
ROWS = 16
LIMIT = 6 * 1024 * 1024
SPAN = 4
CHUNK = 32
X, Y, E, U, SLOPE, COLUMN = range(6)

primal_step = 0.3
dual_step = 0.3
f32 = jnp.float32
bf16 = jnp.bfloat16


def shape(*dims, dtype=f32):
    return jax.ShapeDtypeStruct(dims, dtype)


def run(body, ins, outs):
    in_leaves, in_tree = jax.tree.flatten(ins)
    out_leaves, out_tree = jax.tree.flatten(outs)

    def kernel(*refs):
        given = jax.tree.unflatten(in_tree, refs[: len(in_leaves)])
        made = jax.tree.unflatten(out_tree, refs[len(in_leaves) :])
        body(Space(**given), Space(**made))

    def place(leaf):
        return pl.BlockSpec(memory_space=pltpu.SMEM if leaf.dtype == jnp.int32 else pltpu.VMEM)

    results = pl.pallas_call(
        kernel,
        out_shape=out_leaves,
        in_specs=[place(leaf) for leaf in in_leaves],
        out_specs=[place(leaf) for leaf in out_leaves],
        compiler_params=pltpu.CompilerParams(vmem_limit_bytes=LIMIT),
        name=body.__name__,
    )(*in_leaves)
    return Space(**jax.tree.unflatten(out_tree, results))


def row_iota(rows):
    return lax.broadcasted_iota(jnp.int32, (rows, LANES), 0)


def tail_sum(block):
    rows = block.shape[0]
    at = row_iota(rows)
    step = 1
    while step < rows:
        block = block + jnp.where(at < rows - step, pltpu.roll(block, rows - step, 0), 0.0)
        step *= 2
    return block


def to_tile(block):
    rows = block.shape[0]
    total = block[0:8]
    for i in range(8, rows, 8):
        total = total + block[i : i + 8]
    return total


def halves(value):
    high = value.astype(bf16)
    return high, (value - high.astype(f32)).astype(bf16)


def product(left, high, low):
    left_high, left_low = left
    rows = left_high.shape[0]
    both = jnp.dot(
        jnp.concatenate([left_high, left_low], axis=0), high, preferred_element_type=f32
    )
    rest = jnp.dot(left_high, low, preferred_element_type=f32)
    return both[:rows] + (both[rows:] + rest)


def running_sum(parts):
    rows = parts[0].shape[0]
    at = lax.broadcasted_iota(jnp.int32, (rows, rows), 0)
    ones = (at >= lax.broadcasted_iota(jnp.int32, (rows, rows), 1)).astype(f32).astype(bf16)
    high, low = (jnp.dot(ones, part, preferred_element_type=f32) for part in parts)
    return high + low


def split_matrix(matrix, column, turns):
    rows = matrix.shape[0]
    width = rows
    step = min(256, rows)
    places = {
        False: (shape(rows, width, dtype=bf16), pl.BlockSpec((step, width), lambda i, b: (i, 0))),
        True: (shape(width, rows, dtype=bf16), pl.BlockSpec((width, step), lambda i, b: (0, i))),
    }

    def split(_, source, *parts):
        for index, turned in enumerate(turns):
            value = source[...].T if turned else source[...]
            parts[2 * index][...], parts[2 * index + 1][...] = halves(value)

    parts = pl.pallas_call(
        split,
        out_shape=[places[turned][0] for turned in turns for _ in range(2)],
        grid_spec=pltpu.PrefetchScalarGridSpec(
            num_scalar_prefetch=1,
            grid=(rows // step,),
            in_specs=[pl.BlockSpec((step, width), lambda i, b: (i, b[0]))],
            out_specs=[places[turned][1] for turned in turns for _ in range(2)],
        ),
        compiler_params=pltpu.CompilerParams(vmem_limit_bytes=2 * LIMIT),
    )(column, matrix)
    return [dict(high=parts[2 * i], low=parts[2 * i + 1]) for i in range(len(turns))]


def solve_rows(entries, values):
    size_n = len(values)
    entries = [list(row) for row in entries]
    values = list(values)
    inverses = []
    for p in range(size_n):
        inverse = 1.0 / entries[p][p]
        inverses.append(inverse)
        for i in range(p + 1, size_n):
            factor = entries[i][p] * inverse
            for j in range(p + 1, size_n):
                entries[i][j] = entries[i][j] - factor * entries[p][j]
            values[i] = values[i] - factor * values[p]
    result = [None] * size_n
    for i in range(size_n - 1, -1, -1):
        value = values[i]
        for j in range(i + 1, size_n):
            value = value - entries[i][j] * result[j]
        result[i] = value * inverses[i]
    return result


def columns_at(iteration):
    return list(range(max(1, iteration - MEM + 1), iteration + 1))


def on_device(
    network,
    upper_bound,
    build_cost,
    unit_cost,
    demand,
    inflow,
    primal_start,
    network_start,
    energy_start,
    build_start,
    accepted,
    restarts,
):
    tm_count, bus_count = lax.axis_size("tm"), lax.axis_size("bus")
    tm, bus = lax.axis_index("tm"), lax.axis_index("bus")
    own_hours, width = primal_start.shape
    hours = SPAN * own_hours
    chunks = [slice(at, at + CHUNK) for at in range(0, hours, CHUNK)]
    flags = jnp.concatenate([accepted, restarts, tm.astype(jnp.int32).reshape(1)])
    first_restart, place_tm = accepted.shape[0], 2 * accepted.shape[0]
    member = shape(hours, width)
    line = shape(1, width)
    row = shape(1, LANES)
    tile = shape(ROWS, LANES)
    weights = shape(hours, LANES)
    kind = {X: member, Y: member, E: member, U: line, SLOPE: member, COLUMN: line}

    upper_bound, build_cost, inflow, build_start = (
        value.reshape(1, width) for value in (upper_bound, build_cost, inflow, build_start)
    )

    def swap(value):
        return lax.ppermute(value, "bus", [(i, (i + 1) % bus_count) for i in range(bus_count)])

    def partner(value, distance):
        return lax.ppermute(value, "tm", [(i, i ^ distance) for i in range(tm_count)])

    distances = [SPAN << i for i in range((tm_count // SPAN).bit_length() - 1)]

    def gathered(value):
        arrived = []
        for distance in distances:
            if arrived:
                value = value + arrived[-1]
            arrived.append(partner(value, distance))
        return value, arrived


    def restart_of(ref, iteration):
        return ref[first_restart + iteration - 1].astype(f32)

    def counter_of(ref, iteration):
        count = jnp.float32(1.0)
        for k in range(1, iteration):
            count = (1.0 - restart_of(ref, k)) * count + 1.0
        return count

    def active_of(ref, column, iteration):
        value = jnp.float32(1.0)
        for k in range(column, iteration + 1):
            value = value * (1.0 - restart_of(ref, k))
        return value

    def over_lanes(step, carried=()):
        def one(j, values):
            return step(pl.ds(pl.multiple_of(j * LANES, LANES), LANES), values)

        return lax.fori_loop(0, width // LANES, one, carried)

    def pair_keys(k, with_line):
        if k == 0:
            return []
        count = len(columns_at(k))
        return [
            (line_too, base + j)
            for line_too in ((False, True) if with_line else (False,))
            for base in (0, 8)
            for j in range(count)
        ]

    def over_pairs(k, step, with_line=False):
        keys = pair_keys(k, with_line)

        def one(sl, values):
            pairs = dict(zip(keys, values))
            step(sl, pairs)
            return tuple(pairs[key] for key in keys)

        zeros = tuple(jnp.zeros((1 if key[0] else 8, LANES), f32) for key in keys)
        return dict(zip(keys, over_lanes(one, zeros)))

    def on_diagonal():
        lane = lax.broadcasted_iota(jnp.int32, (ROWS, LANES), 1)
        return lane == row_iota(ROWS)

    def mixing(i, iteration, products, log):
        columns = columns_at(iteration)
        size_n = len(columns)
        spread = jnp.where(on_diagonal(), jnp.broadcast_to(products, (ROWS, LANES)), 0.0)
        newest = jnp.broadcast_to(jnp.sum(spread, axis=1, keepdims=True), (ROWS, LANES))
        summed = dict(zip(columns[:-1], [ref[...] for ref in i.log]))
        summed[iteration] = newest
        log[...] = newest
        active = [active_of(i.flags, k, iteration) for k in columns]

        def entry(a, b):
            a, b = max(a, b), min(a, b)
            at = columns_at(columns[a]).index(columns[b])
            return summed[columns[a]][at : at + 1]

        gram = [[entry(a, b) for b in range(size_n)] for a in range(size_n)]
        trace = gram[0][0] * active[0]
        for a in range(1, size_n):
            trace = trace + gram[a][a] * active[a]
        shift = 0.001 * trace / size_n + 1e-06
        system = [
            [gram[a][b] * (active[a] * active[b]) for b in range(size_n)] for a in range(size_n)
        ]
        for a in range(size_n):
            system[a][a] = system[a][a] + (1.0 - active[a]) + shift
        right = [newest[8 + a : 9 + a] * active[a] for a in range(size_n)]
        mix = solve_rows(system, right)
        accept = i.flags[iteration - 1].astype(f32)
        return [accept * (value * a) for value, a in zip(mix, active)]

    def mixed(mapped, deltas, coefs):
        if not coefs:
            return mapped
        correction = coefs[0] * deltas[0]
        for coef, delta in zip(coefs[1:], deltas[1:]):
            correction = correction + coef * delta
        return mapped - correction

    def restart_parts(ref, k):
        if k == 0:
            return None, None
        return restart_of(ref, k), 1.0 / jnp.full((1, LANES), counter_of(ref, k), f32)

    def begin(i, o, k, at, name, mapped, deltas, coefs, parts):
        following = mixed(mapped, deltas, coefs)
        if k == 0:
            return following
        restart, inverse = parts
        total = i.totals[name][at] + following if k >= 2 else following
        if k < ITERS - 1:
            o.totals[name][at] = (1.0 - restart) * total
        return jnp.where(restart > 0.5, total * inverse, following)

    def note(i, o, k, at, name, mapped, last, state, pairs):
        residual = mapped - state
        if k < ITERS - 1:
            o.resid[name][at] = residual
        if k == 0:
            return
        o.delta[name][at] = mapped - last
        newest = residual - i.resid[name][at]
        o.column[name][at] = newest
        for j, column in enumerate([ref[at] for ref in i.columns[name]] + [newest]):
            for index, other in ((j, newest), (8 + j, residual)):
                term = column * other
                if name != U:
                    term = to_tile(term)
                pairs[name == U, index] += term

    def pair_tile(pairs, scale=1.0):
        rows = []
        for index in range(ROWS):
            total = jnp.zeros((1, LANES), f32)
            if (False, index) in pairs:
                total = jnp.sum(pairs[False, index], axis=0, keepdims=True)
            if (True, index) in pairs:
                total = total + scale * pairs[True, index]
            rows.append(total)
        return jnp.concatenate(rows, axis=0)

    def beyond(ref, arrived, at, backward):
        total = jnp.zeros((1, LANES), f32)
        for distance, piece in zip(distances, arrived):
            first_half = (ref[place_tm] & distance) == 0
            take = first_half if backward else jnp.logical_not(first_half)
            total = total + jnp.where(take, piece[at], 0.0)
        return total

    def pile(i, o):
        for index, own in enumerate(i.own):
            o.out[index * own_hours : (index + 1) * own_hours, :] = own[...]

    def join(i, o):
        place = i.flags[place_tm] % SPAN
        for index, (own, out) in enumerate(zip(i.own, o.out)):
            for distance in range(SPAN):
                rows = pl.ds(pl.multiple_of((place ^ distance) * own_hours, own_hours), own_hours)
                first = index * own_hours
                if distance == 0:
                    out[rows, :] = own[...]
                elif distance < 3:
                    out[rows, :] = i.arrived[distance - 1][first : first + own_hours, :]
                elif index < early:
                    out[rows, :] = i.arrived[2][first : first + own_hours, :]
                else:
                    first = first - early * own_hours
                    out[rows, :] = i.arrived[3][first : first + own_hours, :]


    def tails(i, o, sl):
        carry = jnp.zeros((1, LANES), f32)
        for rows in reversed(chunks):
            tail = tail_sum(i[rows, sl] * o.weight[rows, :]) + carry
            o.tail[rows, sl] = tail
            carry = tail[0:1]
        o.block[:, sl] = carry

    def first(i, o):
        at = (i.flags[place_tm] // SPAN) * hours + row_iota(hours) + 1
        o.weight[...] = 1.0 / at.astype(f32)

        def step(sl, _):
            tails(i.energy, o, sl)
            return ()

        over_lanes(step)

    def whole(i, sl):
        return i.message[:, sl] + i.arrived[-1][:, sl] if i.arrived else i.message[:, sl]

    def primal_kernel(k):
        count = len(columns_at(k - 1)) if k >= 2 else 0

        def primal(i, o):
            coefs = []
            if k >= 2:
                products = whole(i, slice(width, None))
                coefs = mixing(i, k - 1, products, o.log)
            for j, coef in enumerate(coefs):
                o.coefs[j : j + 1, :] = coef

            parts = restart_parts(i.flags, k)

            def step(sl, pairs):
                line_at = (slice(None), sl)

                def start(name, at, value):
                    deltas = [ref[at] for ref in i.deltas[name]] if count else []
                    if name in (SLOPE, COLUMN):
                        if k < ITERS - 1:
                            o.mapped[name][at] = value
                        if count:
                            newest = value - i.last_map[name][at]
                            if k < ITERS - 1:
                                o.delta[name][at] = newest
                            deltas.append(newest)
                    return begin(i, o, k, at, name, value, deltas, coefs, parts)

                later = beyond(i.flags, i.arrived, line_at, True)
                column = start(COLUMN, line_at, whole(i, sl))
                build = start(U, line_at, i.mapped[U][line_at])
                next_build = jnp.maximum(
                    build - primal_step * (i.build_cost[line_at] - column), 0.0
                )
                o.state[line_at] = build
                o.mapped[U][line_at] = next_build
                block = jnp.zeros((8, LANES), f32)
                for rows in chunks:
                    at = (rows, sl)
                    slope = i.pulled[at] - (i.tail[at] + later)
                    slope = start(SLOPE, at, slope)
                    last = i.mapped[X][at]
                    primal = start(X, at, last)
                    next_primal = jnp.clip(
                        primal - primal_step * (i.unit_cost[at] - slope),
                        0.0,
                        i.upper_bound[line_at],
                    )
                    bar = 2.0 * next_primal - primal
                    o.mapped[X][at] = next_primal
                    o.bar[at] = bar
                    block = block + to_tile(bar)
                    note(i, o, k, at, X, next_primal, last, primal, pairs)
                o.block[line_at] = jnp.sum(block, axis=0, keepdims=True)

            o.pairs[...] = pair_tile(over_pairs(k, step))

        return primal

    def push(i, o):
        bar = halves(i.bar[...])
        o.pushed[...] = product(bar, i.high[...], i.low[...])
        o.running[...] = running_sum(bar)

    def coefs_of(i, k):
        return [i.coefs[j : j + 1, :] for j in range(len(columns_at(k - 1)) if k >= 2 else 0)]

    def deltas_of(i, name, at, coefs):
        return [ref[at] for ref in i.deltas[name]] if coefs else []

    def dual_kernel(k):
        def dual(i, o):
            o.mapped[...] = i.pushed[...] + product(halves(i.bar_other[...]), i.high[...], i.low[...])

            coefs, parts = coefs_of(i, k), restart_parts(i.flags, k)

            def step(sl, pairs):
                for rows in chunks:
                    at = (rows, sl)
                    last = i.last[Y][at]
                    deltas = deltas_of(i, Y, at, coefs)
                    state = begin(i, o, k, at, Y, last, deltas, coefs, parts)
                    mapped = jnp.maximum(state + dual_step * (i.demand[at] - o.mapped[at]), 0.0)
                    o.mapped[at] = mapped
                    note(i, o, k, at, Y, mapped, last, state, pairs)

            o.pairs[...] = i.pairs[...] + pair_tile(over_pairs(k, step))

        return dual

    def energy_kernel(k):
        def energy(i, o):
            own_build = (i.flags[place_tm] < SPAN).astype(f32)
            coefs, parts = coefs_of(i, k), restart_parts(i.flags, k)

            def step(sl, pairs):
                line_at = (slice(None), sl)
                earlier = beyond(i.flags, i.arrived, line_at, False)
                build, next_build = i.build[line_at], i.mapped[line_at]
                bar_build = 2.0 * next_build - build
                note(i, o, k, line_at, U, next_build, i.last[U][line_at], build, pairs)
                for rows in chunks:
                    at = (rows, sl)
                    running = i.running[at] + earlier
                    last = i.last[E][at]
                    deltas = deltas_of(i, E, at, coefs)
                    state = begin(i, o, k, at, E, last, deltas, coefs, parts)
                    slack = (bar_build - running) * i.weight[rows, :]
                    mapped = jnp.maximum(
                        state + dual_step * (-i.inflow[line_at] - slack), 0.0
                    )
                    o.mapped[at] = mapped
                    note(i, o, k, at, E, mapped, last, state, pairs)
                if k < ITERS - 1:
                    tails(o.mapped, Space(weight=i.weight, tail=o.tail, block=o.block), sl)

            pairs = over_pairs(k, step, True)
            if k >= 1:
                lines = i.pairs[...] + pair_tile(pairs, own_build)
                sums = jnp.broadcast_to(jnp.sum(lines, axis=1, keepdims=True), (ROWS, LANES))
                o.products[...] = jnp.sum(
                    jnp.where(on_diagonal(), sums, 0.0), axis=0, keepdims=True
                )
            else:
                o.products[...] = jnp.zeros((1, LANES), f32)

        return energy

    def pull(i, o):
        o.pulled[...] = product(halves(i.dual[...]), i.own[0][...], i.own[1][...])
        o.pulled[...] += product(halves(i.dual_other[...]), i.other[0][...], i.other[1][...])

    def last_kernel(i, o):
        place = i.flags[place_tm] % SPAN
        own = pl.ds(pl.multiple_of(place * own_hours, own_hours), own_hours)
        coefs = mixing(i, ITERS - 1, whole(i, slice(None)), o.log)

        def step(sl, _):
            for name in (X, Y, E, U):
                at = (slice(None) if name == U else own, sl)
                deltas = [ref[at] for ref in i.deltas[name]]
                o.following[name][:, sl] = mixed(i.mapped[name][at], deltas, coefs)
            return ()

        over_lanes(step)


    deltas = {name: [] for name in kind}
    columns = {name: [] for name in (X, Y, E, U)}
    totals, last_map, resid, logs = {}, {}, {}, {}

    def send_totals(block, products, dual, dual_other):
        row = block
        if products is not None:
            row = jnp.concatenate([block, products + swap(products)], axis=1)
        row, arrived = gathered(row)
        out = run(
            pull,
            dict(
                dual=dual,
                dual_other=dual_other,
                own=[pull_own[part] for part in sorted(pull_own)],
                other=[pull_other[part] for part in sorted(pull_other)],
            ),
            dict(pulled=member),
        )
        return dict(message=row, arrived=arrived, pulled=out.pulled)

    def picked(source, names):
        return {name: source[name] for name in names}

    def kinds(*names):
        return picked(kind, names)

    def note_ins(k, names):
        if k == 0:
            return {}
        return dict(
            resid=picked(resid, names),
            columns={name: columns[name][-(MEM - 1) :] for name in names},
        )

    def begin_ins(k, name):
        if k < 2:
            return {}
        return dict(coefs=one.coefs, deltas={name: deltas[name]}, totals={name: totals[name]})

    def begin_outs(k, name):
        return dict(totals=kinds(name)) if 1 <= k < ITERS - 1 else {}

    def note_outs(k, names):
        each = kinds(*names)
        return dict(
            **(dict(resid=each) if k < ITERS - 1 else {}),
            **(dict(delta=each, column=each) if k else {}),
        )

    def take(k, out, names):
        for name in names:
            if k < ITERS - 1:
                resid[name] = out.resid[name]
            if k:
                deltas[name] = (deltas[name] + [out.delta[name]])[-MEM:]
                columns[name] = (columns[name] + [out.column[name]])[-MEM:]

    def log_ins(iteration):
        return [logs[j] for j in columns_at(iteration)[:-1]]

    starts = [primal_start, network_start, energy_start, unit_cost, demand]
    early = 3
    stack = run(pile, dict(own=starts), dict(out=shape(len(starts) * own_hours, width))).out
    near, far = partner(stack, 1), partner(stack, 2)
    place = bus.astype(jnp.int32).reshape(1)
    pull_own, push_own = split_matrix(network, place, (False, True))
    (push_other,) = split_matrix(network, 1 - place, (True,))
    (pull_other,) = split_matrix(swap(network), place, (False,))
    near, far, pull_own, push_own, push_other = lax.optimization_barrier(
        (near, far, pull_own, push_own, push_other)
    )
    across = [partner(near[: early * own_hours], 2), partner(far[early * own_hours :], 1)]
    across, pull_other = lax.optimization_barrier((across, pull_other))
    primal, dual, energy, unit_cost, demand = run(
        join,
        dict(flags=flags, own=starts, arrived=[near, far, *across]),
        dict(out=[member] * len(starts)),
    ).out
    out = run(first, dict(flags=flags, energy=energy), dict(tail=member, block=line, weight=weights))
    tail, block, weight = out.tail, out.block, out.weight
    mapped = {X: primal, Y: dual, E: energy, U: build_start}
    totals_in = send_totals(block, None, dual, swap(dual))

    for k in range(ITERS):
        mixes = k >= 2
        keeps = k < ITERS - 1
        ins = dict(
            flags=flags,
            **totals_in,
            tail=tail,
            mapped=picked(mapped, (X, U)),
            unit_cost=unit_cost,
            upper_bound=upper_bound,
            build_cost=build_cost,
            **note_ins(k, (X,)),
        )
        outs = dict(
            mapped=kinds(SLOPE, COLUMN, X, U) if keeps else kinds(X, U),
            state=line,
            bar=member,
            block=line,
            pairs=tile,
            **note_outs(k, (X,)),
        )
        if mixes:
            ins.update(
                log=log_ins(k - 1),
                last_map=picked(last_map, (SLOPE, COLUMN)),
                totals=picked(totals, (SLOPE, COLUMN, X, U)),
                deltas={
                    SLOPE: deltas[SLOPE][-(MEM - 1) :],
                    COLUMN: deltas[COLUMN][-(MEM - 1) :],
                    X: deltas[X],
                    U: deltas[U],
                },
            )
            outs.update(log=tile, coefs=shape(8, LANES))
            if keeps:
                outs["delta"] = {**outs["delta"], **kinds(SLOPE, COLUMN)}
        if 1 <= k < ITERS - 1:
            outs.update(totals=kinds(SLOPE, COLUMN, X, U))
        one = run(primal_kernel(k), ins, outs)
        if mixes:
            logs[k - 1] = one.log
        if mixes and keeps:
            for name in (SLOPE, COLUMN):
                deltas[name] = (deltas[name] + [one.delta[name]])[-MEM:]
        if keeps:
            last_map.update(picked(one.mapped, (SLOPE, COLUMN)))
        if 1 <= k < ITERS - 1:
            totals.update(one.totals)
        _, earlier = gathered(one.block)
        bar_other = swap(one.bar)
        two = run(push, dict(bar=one.bar, **push_own), dict(pushed=member, running=member))
        three = run(
            dual_kernel(k),
            dict(
                flags=flags,
                pushed=two.pushed,
                bar_other=bar_other,
                last=picked(mapped, (Y,)),
                demand=demand,
                pairs=one.pairs,
                **push_other,
                **begin_ins(k, Y),
                **note_ins(k, (Y,)),
            ),
            dict(mapped=member, pairs=tile, **begin_outs(k, Y), **note_outs(k, (Y,))),
        )
        four = run(
            energy_kernel(k),
            dict(
                flags=flags,
                running=two.running,
                arrived=earlier,
                last=picked(mapped, (E, U)),
                build=one.state,
                mapped=one.mapped[U],
                inflow=inflow,
                weight=weight,
                pairs=three.pairs,
                **begin_ins(k, E),
                **note_ins(k, (E, U)),
            ),
            dict(
                mapped=member,
                products=row,
                **(dict(tail=member, block=line) if keeps else {}),
                **begin_outs(k, E),
                **note_outs(k, (E, U)),
            ),
        )
        if 1 <= k < ITERS - 1:
            totals.update(three.totals)
            totals.update(four.totals)
        take(k, one, (X,))
        take(k, three, (Y,))
        take(k, four, (E, U))
        mapped = {X: one.mapped[X], Y: three.mapped, E: four.mapped, U: one.mapped[U]}
        if keeps:
            tail = four.tail
            dual, products = lax.optimization_barrier((mapped[Y], four.products))
            totals_in = send_totals(four.block, products, dual, swap(dual))

    products = four.products + swap(four.products)
    message, arrived = gathered(products)
    out = run(
        last_kernel,
        dict(
            flags=flags,
            message=message,
            arrived=arrived,
            log=log_ins(ITERS - 1),
            mapped=mapped,
            deltas=picked(deltas, (X, Y, E, U)),
        ),
        dict(
            log=tile,
            following={name: line if name == U else shape(own_hours, width) for name in (X, Y, E, U)},
        ),
    )
    final = out.following
    return final[X], final[Y], final[E], final[U].reshape(width)


def solution(mesh):
    hourly = P(("grp", "tm"), "bus")
    return jax.shard_map(
        on_device,
        mesh=mesh,
        in_specs=(
            P("bus", None),
            P("bus"),
            P("bus"),
            hourly,
            hourly,
            P(("grp", "bus")),
            hourly,
            hourly,
            hourly,
            P(("grp", "bus")),
            P("grp"),
            P("grp"),
        ),
        out_specs=(hourly, hourly, hourly, P(("grp", "bus"))),
        check_vma=False,
    )
```

```python
from types import SimpleNamespace as Space

import jax
import jax.numpy as jnp
from jax import lax
from jax.experimental import pallas as pl
from jax.experimental.pallas import tpu as pltpu
from jax.sharding import PartitionSpec as P

ITERS = 9
MEM = 5
LANES = 128
ROWS = 16
LIMIT = 6 * 1024 * 1024
SPAN = 4
CHUNK = 32
X, Y, E, U, SLOPE, COLUMN = range(6)

primal_step = 0.3
dual_step = 0.3
f32 = jnp.float32
bf16 = jnp.bfloat16


def shape(*dims, dtype=f32):
    return jax.ShapeDtypeStruct(dims, dtype)


def run(body, ins, outs):
    in_leaves, in_tree = jax.tree.flatten(ins)
    out_leaves, out_tree = jax.tree.flatten(outs)

    def kernel(*refs):
        given = jax.tree.unflatten(in_tree, refs[: len(in_leaves)])
        made = jax.tree.unflatten(out_tree, refs[len(in_leaves) :])
        body(Space(**given), Space(**made))

    def place(leaf):
        return pl.BlockSpec(memory_space=pltpu.SMEM if leaf.dtype == jnp.int32 else pltpu.VMEM)

    results = pl.pallas_call(
        kernel,
        out_shape=out_leaves,
        in_specs=[place(leaf) for leaf in in_leaves],
        out_specs=[place(leaf) for leaf in out_leaves],
        compiler_params=pltpu.CompilerParams(vmem_limit_bytes=LIMIT),
        name=body.__name__,
    )(*in_leaves)
    return Space(**jax.tree.unflatten(out_tree, results))


def row_iota(rows):
    return lax.broadcasted_iota(jnp.int32, (rows, LANES), 0)


def tail_sum(block):
    rows = block.shape[0]
    at = row_iota(rows)
    step = 1
    while step < rows:
        block = block + jnp.where(at < rows - step, pltpu.roll(block, rows - step, 0), 0.0)
        step *= 2
    return block


def to_tile(block):
    rows = block.shape[0]
    total = block[0:8]
    for i in range(8, rows, 8):
        total = total + block[i : i + 8]
    return total


def halves(value):
    high = value.astype(bf16)
    return high, (value - high.astype(f32)).astype(bf16)


def product(left, high, low):
    left_high, left_low = left
    rows = left_high.shape[0]
    both = jnp.dot(
        jnp.concatenate([left_high, left_low], axis=0), high, preferred_element_type=f32
    )
    rest = jnp.dot(left_high, low, preferred_element_type=f32)
    return both[:rows] + (both[rows:] + rest)


def running_sum(parts):
    rows = parts[0].shape[0]
    at = lax.broadcasted_iota(jnp.int32, (rows, rows), 0)
    ones = (at >= lax.broadcasted_iota(jnp.int32, (rows, rows), 1)).astype(f32).astype(bf16)
    high, low = (jnp.dot(ones, part, preferred_element_type=f32) for part in parts)
    return high + low


def split_matrix(matrix, column, turns):
    rows = matrix.shape[0]
    width = rows
    step = min(256, rows)
    places = {
        False: (shape(rows, width, dtype=bf16), pl.BlockSpec((step, width), lambda i, b: (i, 0))),
        True: (shape(width, rows, dtype=bf16), pl.BlockSpec((width, step), lambda i, b: (0, i))),
    }

    def split(_, source, *parts):
        for index, turned in enumerate(turns):
            value = source[...].T if turned else source[...]
            parts[2 * index][...], parts[2 * index + 1][...] = halves(value)

    parts = pl.pallas_call(
        split,
        out_shape=[places[turned][0] for turned in turns for _ in range(2)],
        grid_spec=pltpu.PrefetchScalarGridSpec(
            num_scalar_prefetch=1,
            grid=(rows // step,),
            in_specs=[pl.BlockSpec((step, width), lambda i, b: (i, b[0]))],
            out_specs=[places[turned][1] for turned in turns for _ in range(2)],
        ),
        compiler_params=pltpu.CompilerParams(vmem_limit_bytes=2 * LIMIT),
    )(column, matrix)
    return [dict(high=parts[2 * i], low=parts[2 * i + 1]) for i in range(len(turns))]


def solve_rows(entries, values):
    size_n = len(values)
    entries = [list(row) for row in entries]
    values = list(values)
    inverses = []
    for p in range(size_n):
        inverse = 1.0 / entries[p][p]
        inverses.append(inverse)
        for i in range(p + 1, size_n):
            factor = entries[i][p] * inverse
            for j in range(p + 1, size_n):
                entries[i][j] = entries[i][j] - factor * entries[p][j]
            values[i] = values[i] - factor * values[p]
    result = [None] * size_n
    for i in range(size_n - 1, -1, -1):
        value = values[i]
        for j in range(i + 1, size_n):
            value = value - entries[i][j] * result[j]
        result[i] = value * inverses[i]
    return result


def columns_at(iteration):
    return list(range(max(1, iteration - MEM + 1), iteration + 1))


def on_device(
    network,
    upper_bound,
    build_cost,
    unit_cost,
    demand,
    inflow,
    primal_start,
    network_start,
    energy_start,
    build_start,
    accepted,
    restarts,
):
    tm_count, bus_count = lax.axis_size("tm"), lax.axis_size("bus")
    tm, bus = lax.axis_index("tm"), lax.axis_index("bus")
    own_hours, width = primal_start.shape
    hours = SPAN * own_hours
    chunks = [slice(at, at + CHUNK) for at in range(0, hours, CHUNK)]
    flags = jnp.concatenate([accepted, restarts, tm.astype(jnp.int32).reshape(1)])
    first_restart, place_tm = accepted.shape[0], 2 * accepted.shape[0]
    member = shape(hours, width)
    line = shape(1, width)
    row = shape(1, LANES)
    tile = shape(ROWS, LANES)
    weights = shape(hours, LANES)
    kind = {X: member, Y: member, E: member, U: line, SLOPE: member, COLUMN: line}

    upper_bound, build_cost, inflow, build_start = (
        value.reshape(1, width) for value in (upper_bound, build_cost, inflow, build_start)
    )

    def swap(value):
        return lax.ppermute(value, "bus", [(i, (i + 1) % bus_count) for i in range(bus_count)])

    def partner(value, distance):
        return lax.ppermute(value, "tm", [(i, i ^ distance) for i in range(tm_count)])

    distances = [SPAN << i for i in range((tm_count // SPAN).bit_length() - 1)]

    def gathered(value):
        arrived = []
        for distance in distances:
            if arrived:
                value = value + arrived[-1]
            arrived.append(partner(value, distance))
        return value, arrived


    def restart_of(ref, iteration):
        return ref[first_restart + iteration - 1].astype(f32)

    def counter_of(ref, iteration):
        count = jnp.float32(1.0)
        for k in range(1, iteration):
            count = (1.0 - restart_of(ref, k)) * count + 1.0
        return count

    def active_of(ref, column, iteration):
        value = jnp.float32(1.0)
        for k in range(column, iteration + 1):
            value = value * (1.0 - restart_of(ref, k))
        return value

    def over_lanes(step, carried=()):
        def one(j, values):
            return step(pl.ds(pl.multiple_of(j * LANES, LANES), LANES), values)

        return lax.fori_loop(0, width // LANES, one, carried, unroll=2)

    def pair_keys(k, with_line):
        if k == 0:
            return []
        count = len(columns_at(k))
        return [
            (line_too, base + j)
            for line_too in ((False, True) if with_line else (False,))
            for base in (0, 8)
            for j in range(count)
        ]

    def over_pairs(k, step, with_line=False):
        keys = pair_keys(k, with_line)

        def one(sl, values):
            pairs = dict(zip(keys, values))
            step(sl, pairs)
            return tuple(pairs[key] for key in keys)

        zeros = tuple(jnp.zeros((1 if key[0] else 8, LANES), f32) for key in keys)
        return dict(zip(keys, over_lanes(one, zeros)))

    def on_diagonal():
        lane = lax.broadcasted_iota(jnp.int32, (ROWS, LANES), 1)
        return lane == row_iota(ROWS)

    def mixing(i, iteration, products, log):
        columns = columns_at(iteration)
        size_n = len(columns)
        spread = jnp.where(on_diagonal(), jnp.broadcast_to(products, (ROWS, LANES)), 0.0)
        newest = jnp.broadcast_to(jnp.sum(spread, axis=1, keepdims=True), (ROWS, LANES))
        summed = dict(zip(columns[:-1], [ref[...] for ref in i.log]))
        summed[iteration] = newest
        log[...] = newest
        active = [active_of(i.flags, k, iteration) for k in columns]

        def entry(a, b):
            a, b = max(a, b), min(a, b)
            at = columns_at(columns[a]).index(columns[b])
            return summed[columns[a]][at : at + 1]

        gram = [[entry(a, b) for b in range(size_n)] for a in range(size_n)]
        trace = gram[0][0] * active[0]
        for a in range(1, size_n):
            trace = trace + gram[a][a] * active[a]
        shift = 0.001 * trace / size_n + 1e-06
        system = [
            [gram[a][b] * (active[a] * active[b]) for b in range(size_n)] for a in range(size_n)
        ]
        for a in range(size_n):
            system[a][a] = system[a][a] + (1.0 - active[a]) + shift
        right = [newest[8 + a : 9 + a] * active[a] for a in range(size_n)]
        mix = solve_rows(system, right)
        accept = i.flags[iteration - 1].astype(f32)
        return [accept * (value * a) for value, a in zip(mix, active)]

    def mixed(mapped, deltas, coefs):
        if not coefs:
            return mapped
        correction = coefs[0] * deltas[0]
        for coef, delta in zip(coefs[1:], deltas[1:]):
            correction = correction + coef * delta
        return mapped - correction

    def restart_parts(ref, k):
        if k == 0:
            return None, None
        return restart_of(ref, k), 1.0 / jnp.full((1, LANES), counter_of(ref, k), f32)

    def begin(i, o, k, at, name, mapped, deltas, coefs, parts):
        following = mixed(mapped, deltas, coefs)
        if k == 0:
            return following
        restart, inverse = parts
        total = i.totals[name][at] + following if k >= 2 else following
        if k < ITERS - 1:
            o.totals[name][at] = (1.0 - restart) * total
        return jnp.where(restart > 0.5, total * inverse, following)

    def note(i, o, k, at, name, mapped, last, state, pairs):
        residual = mapped - state
        if k < ITERS - 1:
            o.resid[name][at] = residual
        if k == 0:
            return
        o.delta[name][at] = mapped - last
        newest = residual - i.resid[name][at]
        o.column[name][at] = newest
        for j, column in enumerate([ref[at] for ref in i.columns[name]] + [newest]):
            for index, other in ((j, newest), (8 + j, residual)):
                term = column * other
                if name != U:
                    term = to_tile(term)
                pairs[name == U, index] += term

    def pair_tile(pairs, scale=1.0):
        rows = []
        for index in range(ROWS):
            total = jnp.zeros((1, LANES), f32)
            if (False, index) in pairs:
                total = jnp.sum(pairs[False, index], axis=0, keepdims=True)
            if (True, index) in pairs:
                total = total + scale * pairs[True, index]
            rows.append(total)
        return jnp.concatenate(rows, axis=0)

    def beyond(ref, arrived, at, backward):
        total = jnp.zeros((1, LANES), f32)
        for distance, piece in zip(distances, arrived):
            first_half = (ref[place_tm] & distance) == 0
            take = first_half if backward else jnp.logical_not(first_half)
            total = total + jnp.where(take, piece[at], 0.0)
        return total

    def pile(i, o):
        for index, own in enumerate(i.own):
            group = int(index >= early)
            at = (index - group * early) * own_hours
            o.out[group][at : at + own_hours, :] = own[...]

    def join(i, o):
        place = i.flags[place_tm] % SPAN
        for index, out in enumerate(o.out):
            group = int(index >= early)
            at = (index - group * early) * own_hours
            for distance in range(SPAN):
                rows = pl.ds(pl.multiple_of((place ^ distance) * own_hours, own_hours), own_hours)
                out[rows, :] = i.stacks[distance][group][at : at + own_hours, :]


    def tails(i, o, sl):
        carry = jnp.zeros((1, LANES), f32)
        for rows in reversed(chunks):
            tail = tail_sum(i[rows, sl] * o.weight[rows, :]) + carry
            o.tail[rows, sl] = tail
            carry = tail[0:1]
        o.block[:, sl] = carry

    def first(i, o):
        at = (i.flags[place_tm] // SPAN) * hours + row_iota(hours) + 1
        o.weight[...] = 1.0 / at.astype(f32)

        def step(sl, _):
            tails(i.energy, o, sl)
            return ()

        over_lanes(step)

    def whole(i, sl):
        return i.message[:, sl] + i.arrived[-1][:, sl] if i.arrived else i.message[:, sl]

    def primal_kernel(k):
        count = len(columns_at(k - 1)) if k >= 2 else 0

        def primal(i, o):
            coefs = []
            if k >= 2:
                products = whole(i, slice(width, None))
                coefs = mixing(i, k - 1, products, o.log)
            for j, coef in enumerate(coefs):
                o.coefs[j : j + 1, :] = coef

            parts = restart_parts(i.flags, k)

            def step(sl, pairs):
                line_at = (slice(None), sl)

                def start(name, at, value):
                    deltas = [ref[at] for ref in i.deltas[name]] if count else []
                    if name in (SLOPE, COLUMN):
                        if k < ITERS - 1:
                            o.mapped[name][at] = value
                        if count:
                            newest = value - i.last_map[name][at]
                            if k < ITERS - 1:
                                o.delta[name][at] = newest
                            deltas.append(newest)
                    return begin(i, o, k, at, name, value, deltas, coefs, parts)

                later = beyond(i.flags, i.arrived, line_at, True)
                column = start(COLUMN, line_at, whole(i, sl))
                build = start(U, line_at, i.mapped[U][line_at])
                next_build = jnp.maximum(
                    build - primal_step * (i.build_cost[line_at] - column), 0.0
                )
                o.state[line_at] = build
                o.mapped[U][line_at] = next_build
                block = jnp.zeros((8, LANES), f32)
                for rows in chunks:
                    at = (rows, sl)
                    slope = i.pulled[at] - (i.tail[at] + later)
                    slope = start(SLOPE, at, slope)
                    last = i.mapped[X][at]
                    primal = start(X, at, last)
                    next_primal = jnp.clip(
                        primal - primal_step * (i.unit_cost[at] - slope),
                        0.0,
                        i.upper_bound[line_at],
                    )
                    bar = 2.0 * next_primal - primal
                    o.mapped[X][at] = next_primal
                    o.bar[at] = bar
                    block = block + to_tile(bar)
                    note(i, o, k, at, X, next_primal, last, primal, pairs)
                o.block[line_at] = jnp.sum(block, axis=0, keepdims=True)

            o.pairs[...] = pair_tile(over_pairs(k, step))

        return primal

    def push(i, o):
        bar = halves(i.bar[...])
        o.pushed[...] = product(bar, i.high[...], i.low[...])
        o.running[...] = running_sum(bar)

    def coefs_of(i, k):
        return [i.coefs[j : j + 1, :] for j in range(len(columns_at(k - 1)) if k >= 2 else 0)]

    def deltas_of(i, name, at, coefs):
        return [ref[at] for ref in i.deltas[name]] if coefs else []

    def dual_kernel(k):
        def dual(i, o):
            o.mapped[...] = i.pushed[...] + product(halves(i.bar_other[...]), i.high[...], i.low[...])

            coefs, parts = coefs_of(i, k), restart_parts(i.flags, k)

            def step(sl, pairs):
                for rows in chunks:
                    at = (rows, sl)
                    last = i.last[Y][at]
                    deltas = deltas_of(i, Y, at, coefs)
                    state = begin(i, o, k, at, Y, last, deltas, coefs, parts)
                    mapped = jnp.maximum(state + dual_step * (i.demand[at] - o.mapped[at]), 0.0)
                    o.mapped[at] = mapped
                    note(i, o, k, at, Y, mapped, last, state, pairs)

            o.pairs[...] = i.pairs[...] + pair_tile(over_pairs(k, step))

        return dual

    def energy_kernel(k):
        def energy(i, o):
            own_build = (i.flags[place_tm] < SPAN).astype(f32)
            coefs, parts = coefs_of(i, k), restart_parts(i.flags, k)

            def step(sl, pairs):
                line_at = (slice(None), sl)
                earlier = beyond(i.flags, i.arrived, line_at, False)
                build, next_build = i.build[line_at], i.mapped[line_at]
                bar_build = 2.0 * next_build - build
                note(i, o, k, line_at, U, next_build, i.last[U][line_at], build, pairs)
                for rows in chunks:
                    at = (rows, sl)
                    running = i.running[at] + earlier
                    last = i.last[E][at]
                    deltas = deltas_of(i, E, at, coefs)
                    state = begin(i, o, k, at, E, last, deltas, coefs, parts)
                    slack = (bar_build - running) * i.weight[rows, :]
                    mapped = jnp.maximum(
                        state + dual_step * (-i.inflow[line_at] - slack), 0.0
                    )
                    o.mapped[at] = mapped
                    note(i, o, k, at, E, mapped, last, state, pairs)
                if k < ITERS - 1:
                    tails(o.mapped, Space(weight=i.weight, tail=o.tail, block=o.block), sl)

            pairs = over_pairs(k, step, True)
            if k >= 1:
                lines = i.pairs[...] + pair_tile(pairs, own_build)
                sums = jnp.broadcast_to(jnp.sum(lines, axis=1, keepdims=True), (ROWS, LANES))
                o.products[...] = jnp.sum(
                    jnp.where(on_diagonal(), sums, 0.0), axis=0, keepdims=True
                )
            else:
                o.products[...] = jnp.zeros((1, LANES), f32)

        return energy

    def pull(i, o):
        o.pulled[...] = product(halves(i.dual[...]), i.own[0][...], i.own[1][...])
        o.pulled[...] += product(halves(i.dual_other[...]), i.other[0][...], i.other[1][...])

    def last_kernel(i, o):
        place = i.flags[place_tm] % SPAN
        own = pl.ds(pl.multiple_of(place * own_hours, own_hours), own_hours)
        coefs = mixing(i, ITERS - 1, whole(i, slice(None)), o.log)

        def step(sl, _):
            for name in (X, Y, E, U):
                at = (slice(None) if name == U else own, sl)
                deltas = [ref[at] for ref in i.deltas[name]]
                o.following[name][:, sl] = mixed(i.mapped[name][at], deltas, coefs)
            return ()

        over_lanes(step)


    deltas = {name: [] for name in kind}
    columns = {name: [] for name in (X, Y, E, U)}
    totals, last_map, resid, logs = {}, {}, {}, {}

    def send_totals(block, products, dual, dual_other):
        row = block
        if products is not None:
            row = jnp.concatenate([block, products + swap(products)], axis=1)
        row, arrived = gathered(row)
        out = run(
            pull,
            dict(
                dual=dual,
                dual_other=dual_other,
                own=[pull_own[part] for part in sorted(pull_own)],
                other=[pull_other[part] for part in sorted(pull_other)],
            ),
            dict(pulled=member),
        )
        return dict(message=row, arrived=arrived, pulled=out.pulled)

    def picked(source, names):
        return {name: source[name] for name in names}

    def kinds(*names):
        return picked(kind, names)

    def note_ins(k, names):
        if k == 0:
            return {}
        return dict(
            resid=picked(resid, names),
            columns={name: columns[name][-(MEM - 1) :] for name in names},
        )

    def begin_ins(k, name):
        if k < 2:
            return {}
        return dict(coefs=one.coefs, deltas={name: deltas[name]}, totals={name: totals[name]})

    def begin_outs(k, name):
        return dict(totals=kinds(name)) if 1 <= k < ITERS - 1 else {}

    def note_outs(k, names):
        each = kinds(*names)
        return dict(
            **(dict(resid=each) if k < ITERS - 1 else {}),
            **(dict(delta=each, column=each) if k else {}),
        )

    def take(k, out, names):
        for name in names:
            if k < ITERS - 1:
                resid[name] = out.resid[name]
            if k:
                deltas[name] = (deltas[name] + [out.delta[name]])[-MEM:]
                columns[name] = (columns[name] + [out.column[name]])[-MEM:]

    def log_ins(iteration):
        return [logs[j] for j in columns_at(iteration)[:-1]]

    starts = [primal_start, network_start, energy_start, unit_cost, demand]
    early = 3
    stacks = run(
        pile,
        dict(own=starts),
        dict(out=[shape(count * own_hours, width) for count in (early, len(starts) - early)]),
    ).out
    near = [partner(stack, 1) for stack in stacks]
    far = [partner(stack, 2) for stack in stacks]
    place = bus.astype(jnp.int32).reshape(1)
    pull_own, push_own = split_matrix(network, place, (False, True))
    (push_other,) = split_matrix(network, 1 - place, (True,))
    (pull_other,) = split_matrix(swap(network), place, (False,))
    near[0], far[1], pull_own, push_own = lax.optimization_barrier(
        (near[0], far[1], pull_own, push_own)
    )
    across = [partner(near[0], 2), partner(far[1], 1)]
    across, pull_other, push_other = lax.optimization_barrier((across, pull_other, push_other))
    primal, dual, energy, unit_cost, demand = run(
        join,
        dict(flags=flags, stacks=[list(stacks), near, far, across]),
        dict(out=[member] * len(starts)),
    ).out
    out = run(first, dict(flags=flags, energy=energy), dict(tail=member, block=line, weight=weights))
    tail, block, weight = out.tail, out.block, out.weight
    mapped = {X: primal, Y: dual, E: energy, U: build_start}
    totals_in = send_totals(block, None, dual, swap(dual))

    for k in range(ITERS):
        mixes = k >= 2
        keeps = k < ITERS - 1
        ins = dict(
            flags=flags,
            **totals_in,
            tail=tail,
            mapped=picked(mapped, (X, U)),
            unit_cost=unit_cost,
            upper_bound=upper_bound,
            build_cost=build_cost,
            **note_ins(k, (X,)),
        )
        outs = dict(
            mapped=kinds(SLOPE, COLUMN, X, U) if keeps else kinds(X, U),
            state=line,
            bar=member,
            block=line,
            pairs=tile,
            **note_outs(k, (X,)),
        )
        if mixes:
            ins.update(
                log=log_ins(k - 1),
                last_map=picked(last_map, (SLOPE, COLUMN)),
                totals=picked(totals, (SLOPE, COLUMN, X, U)),
                deltas={
                    SLOPE: deltas[SLOPE][-(MEM - 1) :],
                    COLUMN: deltas[COLUMN][-(MEM - 1) :],
                    X: deltas[X],
                    U: deltas[U],
                },
            )
            outs.update(log=tile, coefs=shape(8, LANES))
            if keeps:
                outs["delta"] = {**outs["delta"], **kinds(SLOPE, COLUMN)}
        if 1 <= k < ITERS - 1:
            outs.update(totals=kinds(SLOPE, COLUMN, X, U))
        one = run(primal_kernel(k), ins, outs)
        if mixes:
            logs[k - 1] = one.log
        if mixes and keeps:
            for name in (SLOPE, COLUMN):
                deltas[name] = (deltas[name] + [one.delta[name]])[-MEM:]
        if keeps:
            last_map.update(picked(one.mapped, (SLOPE, COLUMN)))
        if 1 <= k < ITERS - 1:
            totals.update(one.totals)
        _, earlier = gathered(one.block)
        bar_other = swap(one.bar)
        two = run(push, dict(bar=one.bar, **push_own), dict(pushed=member, running=member))
        three = run(
            dual_kernel(k),
            dict(
                flags=flags,
                pushed=two.pushed,
                bar_other=bar_other,
                last=picked(mapped, (Y,)),
                demand=demand,
                pairs=one.pairs,
                **push_other,
                **begin_ins(k, Y),
                **note_ins(k, (Y,)),
            ),
            dict(mapped=member, pairs=tile, **begin_outs(k, Y), **note_outs(k, (Y,))),
        )
        four = run(
            energy_kernel(k),
            dict(
                flags=flags,
                running=two.running,
                arrived=earlier,
                last=picked(mapped, (E, U)),
                build=one.state,
                mapped=one.mapped[U],
                inflow=inflow,
                weight=weight,
                pairs=three.pairs,
                **begin_ins(k, E),
                **note_ins(k, (E, U)),
            ),
            dict(
                mapped=member,
                products=row,
                **(dict(tail=member, block=line) if keeps else {}),
                **begin_outs(k, E),
                **note_outs(k, (E, U)),
            ),
        )
        if 1 <= k < ITERS - 1:
            totals.update(three.totals)
            totals.update(four.totals)
        take(k, one, (X,))
        take(k, three, (Y,))
        take(k, four, (E, U))
        mapped = {X: one.mapped[X], Y: three.mapped, E: four.mapped, U: one.mapped[U]}
        if keeps:
            tail = four.tail
            dual, products = lax.optimization_barrier((mapped[Y], four.products))
            totals_in = send_totals(four.block, products, dual, swap(dual))

    products = four.products + swap(four.products)
    message, arrived = gathered(products)
    out = run(
        last_kernel,
        dict(
            flags=flags,
            message=message,
            arrived=arrived,
            log=log_ins(ITERS - 1),
            mapped=mapped,
            deltas=picked(deltas, (X, Y, E, U)),
        ),
        dict(
            log=tile,
            following={name: line if name == U else shape(own_hours, width) for name in (X, Y, E, U)},
        ),
    )
    final = out.following
    return final[X], final[Y], final[E], final[U].reshape(width)


def solution(mesh):
    hourly = P(("grp", "tm"), "bus")
    return jax.shard_map(
        on_device,
        mesh=mesh,
        in_specs=(
            P("bus", None),
            P("bus"),
            P("bus"),
            hourly,
            hourly,
            P(("grp", "bus")),
            hourly,
            hourly,
            hourly,
            P(("grp", "bus")),
            P("grp"),
            P("grp"),
        ),
        out_specs=(hourly, hourly, hourly, P(("grp", "bus"))),
        check_vma=False,
    )
```

```python
from types import SimpleNamespace as Space

import jax
import jax.numpy as jnp
from jax import lax
from jax.experimental import pallas as pl
from jax.experimental.pallas import tpu as pltpu
from jax.sharding import PartitionSpec as P

ITERS = 9
MEM = 5
LANES = 128
ROWS = 16
LIMIT = 6 * 1024 * 1024
SPAN = 4
CHUNK = 16
X, Y, E, U, SLOPE, COLUMN = range(6)

primal_step = 0.3
dual_step = 0.3
f32 = jnp.float32
bf16 = jnp.bfloat16


def shape(*dims, dtype=f32):
    return jax.ShapeDtypeStruct(dims, dtype)


def run(body, ins, outs):
    in_leaves, in_tree = jax.tree.flatten(ins)
    out_leaves, out_tree = jax.tree.flatten(outs)

    def kernel(*refs):
        given = jax.tree.unflatten(in_tree, refs[: len(in_leaves)])
        made = jax.tree.unflatten(out_tree, refs[len(in_leaves) :])
        body(Space(**given), Space(**made))

    def place(leaf):
        return pl.BlockSpec(memory_space=pltpu.SMEM if leaf.dtype == jnp.int32 else pltpu.VMEM)

    results = pl.pallas_call(
        kernel,
        out_shape=out_leaves,
        in_specs=[place(leaf) for leaf in in_leaves],
        out_specs=[place(leaf) for leaf in out_leaves],
        compiler_params=pltpu.CompilerParams(vmem_limit_bytes=LIMIT),
        name=body.__name__,
    )(*in_leaves)
    return Space(**jax.tree.unflatten(out_tree, results))


def row_iota(rows):
    return lax.broadcasted_iota(jnp.int32, (rows, LANES), 0)


def tail_sum(block):
    rows = block.shape[0]
    at = row_iota(rows)
    step = 1
    while step < rows:
        block = block + jnp.where(at < rows - step, pltpu.roll(block, rows - step, 0), 0.0)
        step *= 2
    return block


def to_tile(block):
    rows = block.shape[0]
    total = block[0:8]
    for i in range(8, rows, 8):
        total = total + block[i : i + 8]
    return total


def halves(value):
    high = value.astype(bf16)
    return high, (value - high.astype(f32)).astype(bf16)


def product(left, high, low):
    left_high, left_low = left
    rows = left_high.shape[0]
    both = jnp.dot(
        jnp.concatenate([left_high, left_low], axis=0), high, preferred_element_type=f32
    )
    rest = jnp.dot(left_high, low, preferred_element_type=f32)
    return both[:rows] + (both[rows:] + rest)


def running_sum(parts):
    rows = parts[0].shape[0]
    at = lax.broadcasted_iota(jnp.int32, (rows, rows), 0)
    ones = (at >= lax.broadcasted_iota(jnp.int32, (rows, rows), 1)).astype(f32).astype(bf16)
    high, low = (jnp.dot(ones, part, preferred_element_type=f32) for part in parts)
    return high + low


def split_matrix(matrix, column, turns):
    rows = matrix.shape[0]
    width = rows
    step = min(256, rows)
    places = {
        False: (shape(rows, width, dtype=bf16), pl.BlockSpec((step, width), lambda i, b: (i, 0))),
        True: (shape(width, rows, dtype=bf16), pl.BlockSpec((width, step), lambda i, b: (0, i))),
    }

    def split(_, source, *parts):
        for index, turned in enumerate(turns):
            value = source[...].T if turned else source[...]
            parts[2 * index][...], parts[2 * index + 1][...] = halves(value)

    parts = pl.pallas_call(
        split,
        out_shape=[places[turned][0] for turned in turns for _ in range(2)],
        grid_spec=pltpu.PrefetchScalarGridSpec(
            num_scalar_prefetch=1,
            grid=(rows // step,),
            in_specs=[pl.BlockSpec((step, width), lambda i, b: (i, b[0]))],
            out_specs=[places[turned][1] for turned in turns for _ in range(2)],
        ),
        compiler_params=pltpu.CompilerParams(vmem_limit_bytes=2 * LIMIT),
    )(column, matrix)
    return [dict(high=parts[2 * i], low=parts[2 * i + 1]) for i in range(len(turns))]


def solve_rows(entries, values):
    size_n = len(values)
    entries = [list(row) for row in entries]
    values = list(values)
    inverses = []
    for p in range(size_n):
        inverse = 1.0 / entries[p][p]
        inverses.append(inverse)
        for i in range(p + 1, size_n):
            factor = entries[i][p] * inverse
            for j in range(p + 1, size_n):
                entries[i][j] = entries[i][j] - factor * entries[p][j]
            values[i] = values[i] - factor * values[p]
    result = [None] * size_n
    for i in range(size_n - 1, -1, -1):
        value = values[i]
        for j in range(i + 1, size_n):
            value = value - entries[i][j] * result[j]
        result[i] = value * inverses[i]
    return result


def columns_at(iteration):
    return list(range(max(1, iteration - MEM + 1), iteration + 1))


def on_device(
    network,
    upper_bound,
    build_cost,
    unit_cost,
    demand,
    inflow,
    primal_start,
    network_start,
    energy_start,
    build_start,
    accepted,
    restarts,
):
    tm_count, bus_count = lax.axis_size("tm"), lax.axis_size("bus")
    tm, bus = lax.axis_index("tm"), lax.axis_index("bus")
    own_hours, width = primal_start.shape
    hours = SPAN * own_hours
    chunks = [slice(at, at + CHUNK) for at in range(0, hours, CHUNK)]
    flags = jnp.concatenate([accepted, restarts, tm.astype(jnp.int32).reshape(1)])
    first_restart, place_tm = accepted.shape[0], 2 * accepted.shape[0]
    member = shape(hours, width)
    line = shape(1, width)
    row = shape(1, LANES)
    tile = shape(ROWS, LANES)
    weights = shape(hours, LANES)
    kind = {X: member, Y: member, E: member, U: line, SLOPE: member, COLUMN: line}

    upper_bound, build_cost, inflow, build_start = (
        value.reshape(1, width) for value in (upper_bound, build_cost, inflow, build_start)
    )

    def swap(value):
        return lax.ppermute(value, "bus", [(i, (i + 1) % bus_count) for i in range(bus_count)])

    def partner(value, distance):
        return lax.ppermute(value, "tm", [(i, i ^ distance) for i in range(tm_count)])

    distances = [SPAN << i for i in range((tm_count // SPAN).bit_length() - 1)]

    def gathered(value):
        arrived = []
        for distance in distances:
            if arrived:
                value = value + arrived[-1]
            arrived.append(partner(value, distance))
        return value, arrived


    def restart_of(ref, iteration):
        return ref[first_restart + iteration - 1].astype(f32)

    def counter_of(ref, iteration):
        count = jnp.float32(1.0)
        for k in range(1, iteration):
            count = (1.0 - restart_of(ref, k)) * count + 1.0
        return count

    def active_of(ref, column, iteration):
        value = jnp.float32(1.0)
        for k in range(column, iteration + 1):
            value = value * (1.0 - restart_of(ref, k))
        return value

    def over_lanes(step, carried=()):
        def one(j, values):
            return step(pl.ds(pl.multiple_of(j * LANES, LANES), LANES), values)

        return lax.fori_loop(0, width // LANES, one, carried)

    def pair_keys(k, with_line):
        if k == 0:
            return []
        count = len(columns_at(k))
        return [
            (line_too, base + j)
            for line_too in ((False, True) if with_line else (False,))
            for base in (0, 8)
            for j in range(count)
        ]

    def over_pairs(k, step, with_line=False):
        keys = pair_keys(k, with_line)

        def one(sl, values):
            pairs = dict(zip(keys, values))
            step(sl, pairs)
            return tuple(pairs[key] for key in keys)

        zeros = tuple(jnp.zeros((1 if key[0] else 8, LANES), f32) for key in keys)
        return dict(zip(keys, over_lanes(one, zeros)))

    def on_diagonal():
        lane = lax.broadcasted_iota(jnp.int32, (ROWS, LANES), 1)
        return lane == row_iota(ROWS)

    def mixing(i, iteration, products, log):
        columns = columns_at(iteration)
        size_n = len(columns)
        spread = jnp.where(on_diagonal(), jnp.broadcast_to(products, (ROWS, LANES)), 0.0)
        newest = jnp.broadcast_to(jnp.sum(spread, axis=1, keepdims=True), (ROWS, LANES))
        summed = dict(zip(columns[:-1], [ref[...] for ref in i.log]))
        summed[iteration] = newest
        log[...] = newest
        active = [active_of(i.flags, k, iteration) for k in columns]

        def entry(a, b):
            a, b = max(a, b), min(a, b)
            at = columns_at(columns[a]).index(columns[b])
            return summed[columns[a]][at : at + 1]

        gram = [[entry(a, b) for b in range(size_n)] for a in range(size_n)]
        trace = gram[0][0] * active[0]
        for a in range(1, size_n):
            trace = trace + gram[a][a] * active[a]
        shift = 0.001 * trace / size_n + 1e-06
        system = [
            [gram[a][b] * (active[a] * active[b]) for b in range(size_n)] for a in range(size_n)
        ]
        for a in range(size_n):
            system[a][a] = system[a][a] + (1.0 - active[a]) + shift
        right = [newest[8 + a : 9 + a] * active[a] for a in range(size_n)]
        mix = solve_rows(system, right)
        accept = i.flags[iteration - 1].astype(f32)
        return [accept * (value * a) for value, a in zip(mix, active)]

    def mixed(mapped, deltas, coefs):
        if not coefs:
            return mapped
        correction = coefs[0] * deltas[0]
        for coef, delta in zip(coefs[1:], deltas[1:]):
            correction = correction + coef * delta
        return mapped - correction

    def restart_parts(ref, k):
        if k == 0:
            return None, None
        return restart_of(ref, k), 1.0 / jnp.full((1, LANES), counter_of(ref, k), f32)

    def begin(i, o, k, at, name, mapped, deltas, coefs, parts):
        following = mixed(mapped, deltas, coefs)
        if k == 0:
            return following
        restart, inverse = parts
        total = i.totals[name][at] + following if k >= 2 else following
        if k < ITERS - 1:
            o.totals[name][at] = (1.0 - restart) * total
        return jnp.where(restart > 0.5, total * inverse, following)

    def note(i, o, k, at, name, mapped, last, state, pairs):
        residual = mapped - state
        if k < ITERS - 1:
            o.resid[name][at] = residual
        if k == 0:
            return
        o.delta[name][at] = mapped - last
        newest = residual - i.resid[name][at]
        o.column[name][at] = newest
        for j, column in enumerate([ref[at] for ref in i.columns[name]] + [newest]):
            for index, other in ((j, newest), (8 + j, residual)):
                term = column * other
                if name != U:
                    term = to_tile(term)
                pairs[name == U, index] += term

    def pair_tile(pairs, scale=1.0):
        rows = []
        for index in range(ROWS):
            total = jnp.zeros((1, LANES), f32)
            if (False, index) in pairs:
                total = jnp.sum(pairs[False, index], axis=0, keepdims=True)
            if (True, index) in pairs:
                total = total + scale * pairs[True, index]
            rows.append(total)
        return jnp.concatenate(rows, axis=0)

    def beyond(ref, arrived, at, backward):
        total = jnp.zeros((1, LANES), f32)
        for distance, piece in zip(distances, arrived):
            first_half = (ref[place_tm] & distance) == 0
            take = first_half if backward else jnp.logical_not(first_half)
            total = total + jnp.where(take, piece[at], 0.0)
        return total

    def pile(i, o):
        for index, own in enumerate(i.own):
            o.out[index * own_hours : (index + 1) * own_hours, :] = own[...]

    def join(i, o):
        place = i.flags[place_tm] % SPAN
        for index, (own, out) in enumerate(zip(i.own, o.out)):
            for distance in range(SPAN):
                rows = pl.ds(pl.multiple_of((place ^ distance) * own_hours, own_hours), own_hours)
                first = index * own_hours
                if distance == 0:
                    out[rows, :] = own[...]
                elif distance < 3:
                    out[rows, :] = i.arrived[distance - 1][first : first + own_hours, :]
                elif index < early:
                    out[rows, :] = i.arrived[2][first : first + own_hours, :]
                else:
                    first = first - early * own_hours
                    out[rows, :] = i.arrived[3][first : first + own_hours, :]


    def first(i, o):
        at = (i.flags[place_tm] // SPAN) * hours + row_iota(hours) + 1
        o.weight[...] = 1.0 / at.astype(f32)

        def step(sl, _):
            total = jnp.zeros((8, LANES), f32)
            for rows in chunks:
                total = total + to_tile(i.energy[rows, sl] * o.weight[rows, :])
            o.block[:, sl] = jnp.sum(total, axis=0, keepdims=True)
            return ()

        over_lanes(step)

    def whole(i, sl):
        return i.message[:, sl] + i.arrived[-1][:, sl] if i.arrived else i.message[:, sl]

    def primal_kernel(k):
        count = len(columns_at(k - 1)) if k >= 2 else 0

        def primal(i, o):
            coefs = []
            if k >= 2:
                products = whole(i, slice(width, None))
                coefs = mixing(i, k - 1, products, o.log)
            for j, coef in enumerate(coefs):
                o.coefs[j : j + 1, :] = coef

            parts = restart_parts(i.flags, k)

            def step(sl, pairs):
                line_at = (slice(None), sl)

                def start(name, at, value):
                    deltas = [ref[at] for ref in i.deltas[name]] if count else []
                    if name in (SLOPE, COLUMN):
                        if k < ITERS - 1:
                            o.mapped[name][at] = value
                        if count:
                            newest = value - i.last_map[name][at]
                            if k < ITERS - 1:
                                o.delta[name][at] = newest
                            deltas.append(newest)
                    return begin(i, o, k, at, name, value, deltas, coefs, parts)

                later = beyond(i.flags, i.arrived, line_at, True)
                column = start(COLUMN, line_at, whole(i, sl))
                build = start(U, line_at, i.mapped[U][line_at])
                next_build = jnp.maximum(
                    build - primal_step * (i.build_cost[line_at] - column), 0.0
                )
                o.state[line_at] = build
                o.mapped[U][line_at] = next_build
                block = jnp.zeros((8, LANES), f32)
                for rows in chunks:
                    at = (rows, sl)
                    slope = i.pulled[at] - later
                    slope = start(SLOPE, at, slope)
                    last = i.mapped[X][at]
                    primal = start(X, at, last)
                    next_primal = jnp.clip(
                        primal - primal_step * (i.unit_cost[at] - slope),
                        0.0,
                        i.upper_bound[line_at],
                    )
                    bar = 2.0 * next_primal - primal
                    o.mapped[X][at] = next_primal
                    o.bar[at] = bar
                    block = block + to_tile(bar)
                    note(i, o, k, at, X, next_primal, last, primal, pairs)
                o.block[line_at] = jnp.sum(block, axis=0, keepdims=True)

            o.pairs[...] = pair_tile(over_pairs(k, step))

        return primal

    def push(i, o):
        bar = halves(i.bar[...])
        o.pushed[...] = product(bar, i.high[...], i.low[...])
        o.running[...] = running_sum(bar)

    def coefs_of(i, k):
        return [i.coefs[j : j + 1, :] for j in range(len(columns_at(k - 1)) if k >= 2 else 0)]

    def deltas_of(i, name, at, coefs):
        return [ref[at] for ref in i.deltas[name]] if coefs else []

    def dual_kernel(k):
        def dual(i, o):
            o.mapped[...] = i.pushed[...] + product(halves(i.bar_other[...]), i.high[...], i.low[...])

            coefs, parts = coefs_of(i, k), restart_parts(i.flags, k)

            def step(sl, pairs):
                for rows in chunks:
                    at = (rows, sl)
                    last = i.last[Y][at]
                    deltas = deltas_of(i, Y, at, coefs)
                    state = begin(i, o, k, at, Y, last, deltas, coefs, parts)
                    mapped = jnp.maximum(state + dual_step * (i.demand[at] - o.mapped[at]), 0.0)
                    o.mapped[at] = mapped
                    note(i, o, k, at, Y, mapped, last, state, pairs)

            o.pairs[...] = i.pairs[...] + pair_tile(over_pairs(k, step))

        return dual

    def energy_kernel(k):
        def energy(i, o):
            own_build = (i.flags[place_tm] < SPAN).astype(f32)
            coefs, parts = coefs_of(i, k), restart_parts(i.flags, k)

            def step(sl, pairs):
                line_at = (slice(None), sl)
                earlier = beyond(i.flags, i.arrived, line_at, False)
                build, next_build = i.build[line_at], i.mapped[line_at]
                bar_build = 2.0 * next_build - build
                note(i, o, k, line_at, U, next_build, i.last[U][line_at], build, pairs)
                total = jnp.zeros((8, LANES), f32)
                for rows in chunks:
                    at = (rows, sl)
                    running = i.running[at] + earlier
                    last = i.last[E][at]
                    deltas = deltas_of(i, E, at, coefs)
                    state = begin(i, o, k, at, E, last, deltas, coefs, parts)
                    slack = (bar_build - running) * i.weight[rows, :]
                    mapped = jnp.maximum(
                        state + dual_step * (-i.inflow[line_at] - slack), 0.0
                    )
                    o.mapped[at] = mapped
                    note(i, o, k, at, E, mapped, last, state, pairs)
                    if k < ITERS - 1:
                        total = total + to_tile(mapped * i.weight[rows, :])
                if k < ITERS - 1:
                    o.block[line_at] = jnp.sum(total, axis=0, keepdims=True)

            pairs = over_pairs(k, step, True)
            if k >= 1:
                lines = i.pairs[...] + pair_tile(pairs, own_build)
                sums = jnp.broadcast_to(jnp.sum(lines, axis=1, keepdims=True), (ROWS, LANES))
                o.products[...] = jnp.sum(
                    jnp.where(on_diagonal(), sums, 0.0), axis=0, keepdims=True
                )
            else:
                o.products[...] = jnp.zeros((1, LANES), f32)

        return energy

    def pull(i, o):
        o.pulled[...] = product(halves(i.dual[...]), i.own[0][...], i.own[1][...])
        o.pulled[...] += product(halves(i.dual_other[...]), i.other[0][...], i.other[1][...])

        def step(sl, _):
            carry = jnp.zeros((1, LANES), f32)
            for rows in reversed(chunks):
                tail = tail_sum(i.energy[rows, sl] * i.weight[rows, :]) + carry
                o.pulled[rows, sl] -= tail
                carry = tail[0:1]
            return ()

        over_lanes(step)

    def last_kernel(i, o):
        place = i.flags[place_tm] % SPAN
        own = pl.ds(pl.multiple_of(place * own_hours, own_hours), own_hours)
        coefs = mixing(i, ITERS - 1, whole(i, slice(None)), o.log)

        def step(sl, _):
            for name in (X, Y, E, U):
                at = (slice(None) if name == U else own, sl)
                deltas = [ref[at] for ref in i.deltas[name]]
                o.following[name][:, sl] = mixed(i.mapped[name][at], deltas, coefs)
            return ()

        over_lanes(step)


    deltas = {name: [] for name in kind}
    columns = {name: [] for name in (X, Y, E, U)}
    totals, last_map, resid, logs = {}, {}, {}, {}

    def send_totals(block, products, dual, dual_other, energy):
        row = block
        if products is not None:
            row = jnp.concatenate([block, products + swap(products)], axis=1)
        row, arrived = gathered(row)
        out = run(
            pull,
            dict(
                dual=dual,
                dual_other=dual_other,
                energy=energy,
                weight=weight,
                own=[pull_own[part] for part in sorted(pull_own)],
                other=[pull_other[part] for part in sorted(pull_other)],
            ),
            dict(pulled=member),
        )
        return dict(message=row, arrived=arrived, pulled=out.pulled)

    def picked(source, names):
        return {name: source[name] for name in names}

    def kinds(*names):
        return picked(kind, names)

    def note_ins(k, names):
        if k == 0:
            return {}
        return dict(
            resid=picked(resid, names),
            columns={name: columns[name][-(MEM - 1) :] for name in names},
        )

    def begin_ins(k, name):
        if k < 2:
            return {}
        return dict(coefs=one.coefs, deltas={name: deltas[name]}, totals={name: totals[name]})

    def begin_outs(k, name):
        return dict(totals=kinds(name)) if 1 <= k < ITERS - 1 else {}

    def note_outs(k, names):
        each = kinds(*names)
        return dict(
            **(dict(resid=each) if k < ITERS - 1 else {}),
            **(dict(delta=each, column=each) if k else {}),
        )

    def take(k, out, names):
        for name in names:
            if k < ITERS - 1:
                resid[name] = out.resid[name]
            if k:
                deltas[name] = (deltas[name] + [out.delta[name]])[-MEM:]
                columns[name] = (columns[name] + [out.column[name]])[-MEM:]

    def log_ins(iteration):
        return [logs[j] for j in columns_at(iteration)[:-1]]

    starts = [primal_start, network_start, energy_start, unit_cost, demand]
    early = 3
    stack = run(pile, dict(own=starts), dict(out=shape(len(starts) * own_hours, width))).out
    near, far = partner(stack, 1), partner(stack, 2)
    place = bus.astype(jnp.int32).reshape(1)
    pull_own, push_own = split_matrix(network, place, (False, True))
    (push_other,) = split_matrix(network, 1 - place, (True,))
    (pull_other,) = split_matrix(swap(network), place, (False,))
    near, far, pull_own, push_own, push_other = lax.optimization_barrier(
        (near, far, pull_own, push_own, push_other)
    )
    across = [partner(near[: early * own_hours], 2), partner(far[early * own_hours :], 1)]
    across, pull_other = lax.optimization_barrier((across, pull_other))
    primal, dual, energy, unit_cost, demand = run(
        join,
        dict(flags=flags, own=starts, arrived=[near, far, *across]),
        dict(out=[member] * len(starts)),
    ).out
    out = run(first, dict(flags=flags, energy=energy), dict(block=line, weight=weights))
    block, weight = out.block, out.weight
    mapped = {X: primal, Y: dual, E: energy, U: build_start}
    totals_in = send_totals(block, None, dual, swap(dual), energy)

    for k in range(ITERS):
        mixes = k >= 2
        keeps = k < ITERS - 1
        ins = dict(
            flags=flags,
            **totals_in,
            mapped=picked(mapped, (X, U)),
            unit_cost=unit_cost,
            upper_bound=upper_bound,
            build_cost=build_cost,
            **note_ins(k, (X,)),
        )
        outs = dict(
            mapped=kinds(SLOPE, COLUMN, X, U) if keeps else kinds(X, U),
            state=line,
            bar=member,
            block=line,
            pairs=tile,
            **note_outs(k, (X,)),
        )
        if mixes:
            ins.update(
                log=log_ins(k - 1),
                last_map=picked(last_map, (SLOPE, COLUMN)),
                totals=picked(totals, (SLOPE, COLUMN, X, U)),
                deltas={
                    SLOPE: deltas[SLOPE][-(MEM - 1) :],
                    COLUMN: deltas[COLUMN][-(MEM - 1) :],
                    X: deltas[X],
                    U: deltas[U],
                },
            )
            outs.update(log=tile, coefs=shape(8, LANES))
            if keeps:
                outs["delta"] = {**outs["delta"], **kinds(SLOPE, COLUMN)}
        if 1 <= k < ITERS - 1:
            outs.update(totals=kinds(SLOPE, COLUMN, X, U))
        one = run(primal_kernel(k), ins, outs)
        if mixes:
            logs[k - 1] = one.log
        if mixes and keeps:
            for name in (SLOPE, COLUMN):
                deltas[name] = (deltas[name] + [one.delta[name]])[-MEM:]
        if keeps:
            last_map.update(picked(one.mapped, (SLOPE, COLUMN)))
        if 1 <= k < ITERS - 1:
            totals.update(one.totals)
        _, earlier = gathered(one.block)
        bar_other = swap(one.bar)
        two = run(push, dict(bar=one.bar, **push_own), dict(pushed=member, running=member))
        three = run(
            dual_kernel(k),
            dict(
                flags=flags,
                pushed=two.pushed,
                bar_other=bar_other,
                last=picked(mapped, (Y,)),
                demand=demand,
                pairs=one.pairs,
                **push_other,
                **begin_ins(k, Y),
                **note_ins(k, (Y,)),
            ),
            dict(mapped=member, pairs=tile, **begin_outs(k, Y), **note_outs(k, (Y,))),
        )
        four = run(
            energy_kernel(k),
            dict(
                flags=flags,
                running=two.running,
                arrived=earlier,
                last=picked(mapped, (E, U)),
                build=one.state,
                mapped=one.mapped[U],
                inflow=inflow,
                weight=weight,
                pairs=three.pairs,
                **begin_ins(k, E),
                **note_ins(k, (E, U)),
            ),
            dict(
                mapped=member,
                products=row,
                **(dict(block=line) if keeps else {}),
                **begin_outs(k, E),
                **note_outs(k, (E, U)),
            ),
        )
        if 1 <= k < ITERS - 1:
            totals.update(three.totals)
            totals.update(four.totals)
        take(k, one, (X,))
        take(k, three, (Y,))
        take(k, four, (E, U))
        mapped = {X: one.mapped[X], Y: three.mapped, E: four.mapped, U: one.mapped[U]}
        if keeps:
            dual, products = lax.optimization_barrier((mapped[Y], four.products))
            totals_in = send_totals(four.block, products, dual, swap(dual), mapped[E])

    products = four.products + swap(four.products)
    message, arrived = gathered(products)
    out = run(
        last_kernel,
        dict(
            flags=flags,
            message=message,
            arrived=arrived,
            log=log_ins(ITERS - 1),
            mapped=mapped,
            deltas=picked(deltas, (X, Y, E, U)),
        ),
        dict(
            log=tile,
            following={name: line if name == U else shape(own_hours, width) for name in (X, Y, E, U)},
        ),
    )
    final = out.following
    return final[X], final[Y], final[E], final[U].reshape(width)


def solution(mesh):
    hourly = P(("grp", "tm"), "bus")
    return jax.shard_map(
        on_device,
        mesh=mesh,
        in_specs=(
            P("bus", None),
            P("bus"),
            P("bus"),
            hourly,
            hourly,
            P(("grp", "bus")),
            hourly,
            hourly,
            hourly,
            P(("grp", "bus")),
            P("grp"),
            P("grp"),
        ),
        out_specs=(hourly, hourly, hourly, P(("grp", "bus"))),
        check_vma=False,
    )
```

```python
from types import SimpleNamespace as Space

import jax
import jax.numpy as jnp
from jax import lax
from jax.experimental import pallas as pl
from jax.experimental.pallas import tpu as pltpu
from jax.sharding import PartitionSpec as P

ITERS = 9
MEM = 5
LANES = 128
ROWS = 16
LIMIT = 6 * 1024 * 1024
SPAN = 4
CHUNK = 16
X, Y, E, U, SLOPE, COLUMN = range(6)

primal_step = 0.3
dual_step = 0.3
f32 = jnp.float32
bf16 = jnp.bfloat16


def shape(*dims, dtype=f32):
    return jax.ShapeDtypeStruct(dims, dtype)


def run(body, ins, outs):
    in_leaves, in_tree = jax.tree.flatten(ins)
    out_leaves, out_tree = jax.tree.flatten(outs)

    def kernel(*refs):
        given = jax.tree.unflatten(in_tree, refs[: len(in_leaves)])
        made = jax.tree.unflatten(out_tree, refs[len(in_leaves) :])
        body(Space(**given), Space(**made))

    def place(leaf):
        return pl.BlockSpec(memory_space=pltpu.SMEM if leaf.dtype == jnp.int32 else pltpu.VMEM)

    results = pl.pallas_call(
        kernel,
        out_shape=out_leaves,
        in_specs=[place(leaf) for leaf in in_leaves],
        out_specs=[place(leaf) for leaf in out_leaves],
        compiler_params=pltpu.CompilerParams(vmem_limit_bytes=LIMIT),
        name=body.__name__,
    )(*in_leaves)
    return Space(**jax.tree.unflatten(out_tree, results))


def row_iota(rows):
    return lax.broadcasted_iota(jnp.int32, (rows, LANES), 0)


def tail_sum(block):
    rows = block.shape[0]
    at = row_iota(rows)
    step = 1
    while step < rows:
        block = block + jnp.where(at < rows - step, pltpu.roll(block, rows - step, 0), 0.0)
        step *= 2
    return block


def to_tile(block):
    rows = block.shape[0]
    total = block[0:8]
    for i in range(8, rows, 8):
        total = total + block[i : i + 8]
    return total


def halves(value):
    high = value.astype(bf16)
    return high, (value - high.astype(f32)).astype(bf16)


def product(left, high, low):
    left_high, left_low = left
    rows = left_high.shape[0]
    both = jnp.dot(
        jnp.concatenate([left_high, left_low], axis=0), high, preferred_element_type=f32
    )
    rest = jnp.dot(left_high, low, preferred_element_type=f32)
    return both[:rows] + (both[rows:] + rest)


def running_sum(parts):
    rows = parts[0].shape[0]
    at = lax.broadcasted_iota(jnp.int32, (rows, rows), 0)
    ones = (at >= lax.broadcasted_iota(jnp.int32, (rows, rows), 1)).astype(f32).astype(bf16)
    high, low = (jnp.dot(ones, part, preferred_element_type=f32) for part in parts)
    return high + low


def split_matrix(matrix, column, turns):
    rows = matrix.shape[0]
    width = rows
    step = min(256, rows)
    places = {
        False: (shape(rows, width, dtype=bf16), pl.BlockSpec((step, width), lambda i, b: (i, 0))),
        True: (shape(width, rows, dtype=bf16), pl.BlockSpec((width, step), lambda i, b: (0, i))),
    }

    def split(_, source, *parts):
        for index, turned in enumerate(turns):
            value = source[...].T if turned else source[...]
            parts[2 * index][...], parts[2 * index + 1][...] = halves(value)

    parts = pl.pallas_call(
        split,
        out_shape=[places[turned][0] for turned in turns for _ in range(2)],
        grid_spec=pltpu.PrefetchScalarGridSpec(
            num_scalar_prefetch=1,
            grid=(rows // step,),
            in_specs=[pl.BlockSpec((step, width), lambda i, b: (i, b[0]))],
            out_specs=[places[turned][1] for turned in turns for _ in range(2)],
        ),
        compiler_params=pltpu.CompilerParams(vmem_limit_bytes=2 * LIMIT),
    )(column, matrix)
    return [dict(high=parts[2 * i], low=parts[2 * i + 1]) for i in range(len(turns))]


def solve_rows(entries, values):
    size_n = len(values)
    entries = [list(row) for row in entries]
    values = list(values)
    inverses = []
    for p in range(size_n):
        inverse = 1.0 / entries[p][p]
        inverses.append(inverse)
        for i in range(p + 1, size_n):
            factor = entries[i][p] * inverse
            for j in range(p + 1, size_n):
                entries[i][j] = entries[i][j] - factor * entries[p][j]
            values[i] = values[i] - factor * values[p]
    result = [None] * size_n
    for i in range(size_n - 1, -1, -1):
        value = values[i]
        for j in range(i + 1, size_n):
            value = value - entries[i][j] * result[j]
        result[i] = value * inverses[i]
    return result


def columns_at(iteration):
    return list(range(max(1, iteration - MEM + 1), iteration + 1))


def on_device(
    network,
    upper_bound,
    build_cost,
    unit_cost,
    demand,
    inflow,
    primal_start,
    network_start,
    energy_start,
    build_start,
    accepted,
    restarts,
):
    tm_count, bus_count = lax.axis_size("tm"), lax.axis_size("bus")
    tm, bus = lax.axis_index("tm"), lax.axis_index("bus")
    own_hours, width = primal_start.shape
    hours = SPAN * own_hours
    chunks = [slice(at, at + CHUNK) for at in range(0, hours, CHUNK)]
    flags = jnp.concatenate([accepted, restarts, tm.astype(jnp.int32).reshape(1)])
    first_restart, place_tm = accepted.shape[0], 2 * accepted.shape[0]
    member = shape(hours, width)
    line = shape(1, width)
    row = shape(1, LANES)
    tile = shape(ROWS, LANES)
    weights = shape(hours, LANES)
    kind = {X: member, Y: member, E: member, U: line, SLOPE: member, COLUMN: line}

    upper_bound, build_cost, inflow, build_start = (
        value.reshape(1, width) for value in (upper_bound, build_cost, inflow, build_start)
    )

    def swap(value):
        return lax.ppermute(value, "bus", [(i, (i + 1) % bus_count) for i in range(bus_count)])

    def partner(value, distance):
        return lax.ppermute(value, "tm", [(i, i ^ distance) for i in range(tm_count)])

    distances = [SPAN << i for i in range((tm_count // SPAN).bit_length() - 1)]

    def gathered(value):
        arrived = []
        for distance in distances:
            if arrived:
                value = value + arrived[-1]
            arrived.append(partner(value, distance))
        return value, arrived


    def restart_of(ref, iteration):
        return ref[first_restart + iteration - 1].astype(f32)

    def counter_of(ref, iteration):
        count = jnp.float32(1.0)
        for k in range(1, iteration):
            count = (1.0 - restart_of(ref, k)) * count + 1.0
        return count

    def active_of(ref, column, iteration):
        value = jnp.float32(1.0)
        for k in range(column, iteration + 1):
            value = value * (1.0 - restart_of(ref, k))
        return value

    def over_lanes(step, carried=()):
        def one(j, values):
            return step(pl.ds(pl.multiple_of(j * LANES, LANES), LANES), values)

        return lax.fori_loop(0, width // LANES, one, carried)

    def pair_keys(k, with_line):
        if k == 0:
            return []
        count = len(columns_at(k))
        return [
            (line_too, base + j)
            for line_too in ((False, True) if with_line else (False,))
            for base in (0, 8)
            for j in range(count)
        ]

    def over_pairs(k, step, with_line=False):
        keys = pair_keys(k, with_line)

        def one(sl, values):
            pairs = dict(zip(keys, values))
            step(sl, pairs)
            return tuple(pairs[key] for key in keys)

        zeros = tuple(jnp.zeros((1 if key[0] else 8, LANES), f32) for key in keys)
        return dict(zip(keys, over_lanes(one, zeros)))

    def on_diagonal():
        lane = lax.broadcasted_iota(jnp.int32, (ROWS, LANES), 1)
        return lane == row_iota(ROWS)

    def mixing(i, iteration, products, log):
        columns = columns_at(iteration)
        size_n = len(columns)
        spread = jnp.where(on_diagonal(), jnp.broadcast_to(products, (ROWS, LANES)), 0.0)
        newest = jnp.broadcast_to(jnp.sum(spread, axis=1, keepdims=True), (ROWS, LANES))
        summed = dict(zip(columns[:-1], [ref[...] for ref in i.log]))
        summed[iteration] = newest
        log[...] = newest
        active = [active_of(i.flags, k, iteration) for k in columns]

        def entry(a, b):
            a, b = max(a, b), min(a, b)
            at = columns_at(columns[a]).index(columns[b])
            return summed[columns[a]][at : at + 1]

        gram = [[entry(a, b) for b in range(size_n)] for a in range(size_n)]
        trace = gram[0][0] * active[0]
        for a in range(1, size_n):
            trace = trace + gram[a][a] * active[a]
        shift = 0.001 * trace / size_n + 1e-06
        system = [
            [gram[a][b] * (active[a] * active[b]) for b in range(size_n)] for a in range(size_n)
        ]
        for a in range(size_n):
            system[a][a] = system[a][a] + (1.0 - active[a]) + shift
        right = [newest[8 + a : 9 + a] * active[a] for a in range(size_n)]
        mix = solve_rows(system, right)
        accept = i.flags[iteration - 1].astype(f32)
        return [accept * (value * a) for value, a in zip(mix, active)]

    def mixed(mapped, deltas, coefs):
        if not coefs:
            return mapped
        correction = coefs[0] * deltas[0]
        for coef, delta in zip(coefs[1:], deltas[1:]):
            correction = correction + coef * delta
        return mapped - correction

    def restart_parts(ref, k):
        if k == 0:
            return None, None
        return restart_of(ref, k), 1.0 / jnp.full((1, LANES), counter_of(ref, k), f32)

    def begin(i, o, k, at, name, mapped, deltas, coefs, parts):
        following = mixed(mapped, deltas, coefs)
        if k == 0:
            return following
        restart, inverse = parts
        total = i.totals[name][at] + following if k >= 2 else following
        if k < ITERS - 1:
            o.totals[name][at] = (1.0 - restart) * total
        return jnp.where(restart > 0.5, total * inverse, following)

    def note(i, o, k, at, name, mapped, last, state, pairs):
        residual = mapped - state
        if k < ITERS - 1:
            o.resid[name][at] = residual
        if k == 0:
            return
        if k < ITERS - 1:
            o.delta[name][at] = mapped - last
        newest = residual - i.resid[name][at]
        if k < ITERS - 1:
            o.column[name][at] = newest
        for j, column in enumerate([ref[at] for ref in i.columns[name]] + [newest]):
            for index, other in ((j, newest), (8 + j, residual)):
                term = column * other
                if name != U:
                    term = to_tile(term)
                pairs[name == U, index] += term

    def pair_tile(pairs, scale=1.0):
        rows = []
        for index in range(ROWS):
            total = jnp.zeros((1, LANES), f32)
            if (False, index) in pairs:
                total = jnp.sum(pairs[False, index], axis=0, keepdims=True)
            if (True, index) in pairs:
                total = total + scale * pairs[True, index]
            rows.append(total)
        return jnp.concatenate(rows, axis=0)

    def beyond(ref, arrived, at, backward):
        total = jnp.zeros((1, LANES), f32)
        for distance, piece in zip(distances, arrived):
            first_half = (ref[place_tm] & distance) == 0
            take = first_half if backward else jnp.logical_not(first_half)
            total = total + jnp.where(take, piece[at], 0.0)
        return total

    def pile(i, o):
        for index, own in enumerate(i.own):
            group = int(index >= early)
            at = (index - group * early) * own_hours
            o.out[group][at : at + own_hours, :] = own[...]

    def join(i, o):
        place = i.flags[place_tm] % SPAN
        for index, out in enumerate(o.out):
            group = int(index >= early)
            at = (index - group * early) * own_hours
            for distance in range(SPAN):
                rows = pl.ds(pl.multiple_of((place ^ distance) * own_hours, own_hours), own_hours)
                out[rows, :] = i.stacks[distance][group][at : at + own_hours, :]


    def first(i, o):
        at = (i.flags[place_tm] // SPAN) * hours + row_iota(hours) + 1
        o.weight[...] = 1.0 / at.astype(f32)

        def step(sl, _):
            total = jnp.zeros((8, LANES), f32)
            for rows in chunks:
                total = total + to_tile(i.energy[rows, sl] * o.weight[rows, :])
            o.block[:, sl] = jnp.sum(total, axis=0, keepdims=True)
            return ()

        over_lanes(step)

    def whole(i, sl):
        return i.message[:, sl] + i.arrived[-1][:, sl] if i.arrived else i.message[:, sl]

    def primal_kernel(k):
        count = len(columns_at(k - 1)) if k >= 2 else 0

        def primal(i, o):
            coefs = []
            if k >= 2:
                products = whole(i, slice(width, None))
                coefs = mixing(i, k - 1, products, o.log)
            for j, coef in enumerate(coefs):
                o.coefs[j : j + 1, :] = coef

            parts = restart_parts(i.flags, k)

            def step(sl, pairs):
                line_at = (slice(None), sl)

                def start(name, at, value):
                    deltas = [ref[at] for ref in i.deltas[name]] if count else []
                    if name in (SLOPE, COLUMN):
                        if k < ITERS - 1:
                            o.mapped[name][at] = value
                        if count:
                            newest = value - i.last_map[name][at]
                            if k < ITERS - 1:
                                o.delta[name][at] = newest
                            deltas.append(newest)
                    return begin(i, o, k, at, name, value, deltas, coefs, parts)

                later = beyond(i.flags, i.arrived, line_at, True)
                column = start(COLUMN, line_at, whole(i, sl))
                build = start(U, line_at, i.mapped[U][line_at])
                next_build = jnp.maximum(
                    build - primal_step * (i.build_cost[line_at] - column), 0.0
                )
                o.state[line_at] = build
                o.mapped[U][line_at] = next_build
                block = jnp.zeros((8, LANES), f32)
                for rows in chunks:
                    at = (rows, sl)
                    slope = i.pulled[at] - later
                    slope = start(SLOPE, at, slope)
                    last = i.mapped[X][at]
                    primal = start(X, at, last)
                    next_primal = jnp.clip(
                        primal - primal_step * (i.unit_cost[at] - slope),
                        0.0,
                        i.upper_bound[line_at],
                    )
                    bar = 2.0 * next_primal - primal
                    o.mapped[X][at] = next_primal
                    o.bar[at] = bar
                    block = block + to_tile(bar)
                    note(i, o, k, at, X, next_primal, last, primal, pairs)
                o.block[line_at] = jnp.sum(block, axis=0, keepdims=True)

            o.pairs[...] = pair_tile(over_pairs(k, step))

        return primal

    def push(i, o):
        bar = halves(i.bar[...])
        o.pushed[...] = product(bar, i.high[...], i.low[...])
        o.running[...] = running_sum(bar)

    def coefs_of(i, k):
        return [i.coefs[j : j + 1, :] for j in range(len(columns_at(k - 1)) if k >= 2 else 0)]

    def deltas_of(i, name, at, coefs):
        return [ref[at] for ref in i.deltas[name]] if coefs else []

    def dual_kernel(k):
        def dual(i, o):
            o.mapped[...] = i.pushed[...] + product(halves(i.bar_other[...]), i.high[...], i.low[...])

            coefs, parts = coefs_of(i, k), restart_parts(i.flags, k)

            def step(sl, pairs):
                for rows in chunks:
                    at = (rows, sl)
                    last = i.last[Y][at]
                    deltas = deltas_of(i, Y, at, coefs)
                    state = begin(i, o, k, at, Y, last, deltas, coefs, parts)
                    mapped = jnp.maximum(state + dual_step * (i.demand[at] - o.mapped[at]), 0.0)
                    o.mapped[at] = mapped
                    note(i, o, k, at, Y, mapped, last, state, pairs)

            o.pairs[...] = i.pairs[...] + pair_tile(over_pairs(k, step))

        return dual

    def energy_kernel(k):
        def energy(i, o):
            own_build = (i.flags[place_tm] < SPAN).astype(f32)
            coefs, parts = coefs_of(i, k), restart_parts(i.flags, k)

            def step(sl, pairs):
                line_at = (slice(None), sl)
                earlier = beyond(i.flags, i.arrived, line_at, False)
                build, next_build = i.build[line_at], i.mapped[line_at]
                bar_build = 2.0 * next_build - build
                note(i, o, k, line_at, U, next_build, i.last[U][line_at], build, pairs)
                total = jnp.zeros((8, LANES), f32)
                for rows in chunks:
                    at = (rows, sl)
                    running = i.running[at] + earlier
                    last = i.last[E][at]
                    deltas = deltas_of(i, E, at, coefs)
                    state = begin(i, o, k, at, E, last, deltas, coefs, parts)
                    slack = (bar_build - running) * i.weight[rows, :]
                    mapped = jnp.maximum(
                        state + dual_step * (-i.inflow[line_at] - slack), 0.0
                    )
                    o.mapped[at] = mapped
                    note(i, o, k, at, E, mapped, last, state, pairs)
                    if k < ITERS - 1:
                        total = total + to_tile(mapped * i.weight[rows, :])
                if k < ITERS - 1:
                    o.block[line_at] = jnp.sum(total, axis=0, keepdims=True)

            pairs = over_pairs(k, step, True)
            if k >= 1:
                lines = i.pairs[...] + pair_tile(pairs, own_build)
                sums = jnp.broadcast_to(jnp.sum(lines, axis=1, keepdims=True), (ROWS, LANES))
                o.products[...] = jnp.sum(
                    jnp.where(on_diagonal(), sums, 0.0), axis=0, keepdims=True
                )
            else:
                o.products[...] = jnp.zeros((1, LANES), f32)

        return energy

    def pull(i, o):
        o.pulled[...] = product(halves(i.dual[...]), i.own[0][...], i.own[1][...])
        o.pulled[...] += product(halves(i.dual_other[...]), i.other[0][...], i.other[1][...])

        def step(sl, _):
            carry = jnp.zeros((1, LANES), f32)
            for rows in reversed(chunks):
                tail = tail_sum(i.energy[rows, sl] * i.weight[rows, :]) + carry
                o.pulled[rows, sl] -= tail
                carry = tail[0:1]
            return ()

        over_lanes(step)

    def last_kernel(i, o):
        place = i.flags[place_tm] % SPAN
        own = pl.ds(pl.multiple_of(place * own_hours, own_hours), own_hours)
        coefs = mixing(i, ITERS - 1, whole(i, slice(None)), o.log)

        def step(sl, _):
            for name in (X, Y, E, U):
                at = (slice(None) if name == U else own, sl)
                mapped = i.mapped[name][at]
                deltas = [ref[at] for ref in i.deltas[name]] + [mapped - i.last[name][at]]
                o.following[name][:, sl] = mixed(mapped, deltas, coefs)
            return ()

        over_lanes(step)


    deltas = {name: [] for name in kind}
    columns = {name: [] for name in (X, Y, E, U)}
    totals, last_map, resid, logs = {}, {}, {}, {}

    def send_totals(block, products, dual, dual_other, energy):
        row = block
        if products is not None:
            row = jnp.concatenate([block, products + swap(products)], axis=1)
        row, arrived = gathered(row)
        out = run(
            pull,
            dict(
                dual=dual,
                dual_other=dual_other,
                energy=energy,
                weight=weight,
                own=[pull_own[part] for part in sorted(pull_own)],
                other=[pull_other[part] for part in sorted(pull_other)],
            ),
            dict(pulled=member),
        )
        return dict(message=row, arrived=arrived, pulled=out.pulled)

    def picked(source, names):
        return {name: source[name] for name in names}

    def kinds(*names):
        return picked(kind, names)

    def note_ins(k, names):
        if k == 0:
            return {}
        return dict(
            resid=picked(resid, names),
            columns={name: columns[name][-(MEM - 1) :] for name in names},
        )

    def begin_ins(k, name):
        if k < 2:
            return {}
        return dict(coefs=one.coefs, deltas={name: deltas[name]}, totals={name: totals[name]})

    def begin_outs(k, name):
        return dict(totals=kinds(name)) if 1 <= k < ITERS - 1 else {}

    def note_outs(k, names):
        each = kinds(*names)
        if k == ITERS - 1:
            return {}
        return dict(resid=each, **(dict(delta=each, column=each) if k else {}))

    def take(k, out, names):
        for name in names:
            resid[name] = out.resid[name]
            if k:
                deltas[name] = (deltas[name] + [out.delta[name]])[-MEM:]
                columns[name] = (columns[name] + [out.column[name]])[-MEM:]

    def log_ins(iteration):
        return [logs[j] for j in columns_at(iteration)[:-1]]

    starts = [primal_start, network_start, energy_start, unit_cost, demand]
    early = 3
    stacks = run(
        pile,
        dict(own=starts),
        dict(out=[shape(count * own_hours, width) for count in (early, len(starts) - early)]),
    ).out
    near = [partner(stack, 1) for stack in stacks]
    far = [partner(stack, 2) for stack in stacks]
    place = bus.astype(jnp.int32).reshape(1)
    pull_own, push_own = split_matrix(network, place, (False, True))
    (push_other,) = split_matrix(network, 1 - place, (True,))
    (pull_other,) = split_matrix(swap(network), place, (False,))
    near, far, pull_own, push_own, push_other = lax.optimization_barrier(
        (near, far, pull_own, push_own, push_other)
    )
    across = [partner(near[0], 2), partner(far[1], 1)]
    across, pull_other = lax.optimization_barrier((across, pull_other))
    primal, dual, energy, unit_cost, demand = run(
        join,
        dict(flags=flags, stacks=[list(stacks), near, far, across]),
        dict(out=[member] * len(starts)),
    ).out
    out = run(first, dict(flags=flags, energy=energy), dict(block=line, weight=weights))
    block, weight = out.block, out.weight
    mapped = {X: primal, Y: dual, E: energy, U: build_start}
    totals_in = send_totals(block, None, dual, swap(dual), energy)

    for k in range(ITERS):
        mixes = k >= 2
        keeps = k < ITERS - 1
        ins = dict(
            flags=flags,
            **totals_in,
            mapped=picked(mapped, (X, U)),
            unit_cost=unit_cost,
            upper_bound=upper_bound,
            build_cost=build_cost,
            **note_ins(k, (X,)),
        )
        outs = dict(
            mapped=kinds(SLOPE, COLUMN, X, U) if keeps else kinds(X, U),
            state=line,
            bar=member,
            block=line,
            pairs=tile,
            **note_outs(k, (X,)),
        )
        if mixes:
            ins.update(
                log=log_ins(k - 1),
                last_map=picked(last_map, (SLOPE, COLUMN)),
                totals=picked(totals, (SLOPE, COLUMN, X, U)),
                deltas={
                    SLOPE: deltas[SLOPE][-(MEM - 1) :],
                    COLUMN: deltas[COLUMN][-(MEM - 1) :],
                    X: deltas[X],
                    U: deltas[U],
                },
            )
            outs.update(log=tile, coefs=shape(8, LANES))
            if keeps:
                outs["delta"] = {**outs["delta"], **kinds(SLOPE, COLUMN)}
        if 1 <= k < ITERS - 1:
            outs.update(totals=kinds(SLOPE, COLUMN, X, U))
        one = run(primal_kernel(k), ins, outs)
        if mixes:
            logs[k - 1] = one.log
        if mixes and keeps:
            for name in (SLOPE, COLUMN):
                deltas[name] = (deltas[name] + [one.delta[name]])[-MEM:]
        if keeps:
            last_map.update(picked(one.mapped, (SLOPE, COLUMN)))
        if 1 <= k < ITERS - 1:
            totals.update(one.totals)
        _, earlier = gathered(one.block)
        bar_other = swap(one.bar)
        two = run(push, dict(bar=one.bar, **push_own), dict(pushed=member, running=member))
        three = run(
            dual_kernel(k),
            dict(
                flags=flags,
                pushed=two.pushed,
                bar_other=bar_other,
                last=picked(mapped, (Y,)),
                demand=demand,
                pairs=one.pairs,
                **push_other,
                **begin_ins(k, Y),
                **note_ins(k, (Y,)),
            ),
            dict(mapped=member, pairs=tile, **begin_outs(k, Y), **note_outs(k, (Y,))),
        )
        four = run(
            energy_kernel(k),
            dict(
                flags=flags,
                running=two.running,
                arrived=earlier,
                last=picked(mapped, (E, U)),
                build=one.state,
                mapped=one.mapped[U],
                inflow=inflow,
                weight=weight,
                pairs=three.pairs,
                **begin_ins(k, E),
                **note_ins(k, (E, U)),
            ),
            dict(
                mapped=member,
                products=row,
                **(dict(block=line) if keeps else {}),
                **begin_outs(k, E),
                **note_outs(k, (E, U)),
            ),
        )
        if 1 <= k < ITERS - 1:
            totals.update(three.totals)
            totals.update(four.totals)
        if keeps:
            take(k, one, (X,))
            take(k, three, (Y,))
            take(k, four, (E, U))
        last = mapped
        mapped = {X: one.mapped[X], Y: three.mapped, E: four.mapped, U: one.mapped[U]}
        if keeps:
            dual, products = lax.optimization_barrier((mapped[Y], four.products))
            totals_in = send_totals(four.block, products, dual, swap(dual), mapped[E])

    products = four.products + swap(four.products)
    message, arrived = gathered(products)
    out = run(
        last_kernel,
        dict(
            flags=flags,
            message=message,
            arrived=arrived,
            log=log_ins(ITERS - 1),
            mapped=mapped,
            last=last,
            deltas={name: deltas[name][-(MEM - 1) :] for name in (X, Y, E, U)},
        ),
        dict(
            log=tile,
            following={name: line if name == U else shape(own_hours, width) for name in (X, Y, E, U)},
        ),
    )
    final = out.following
    return final[X], final[Y], final[E], final[U].reshape(width)


def solution(mesh):
    hourly = P(("grp", "tm"), "bus")
    return jax.shard_map(
        on_device,
        mesh=mesh,
        in_specs=(
            P("bus", None),
            P("bus"),
            P("bus"),
            hourly,
            hourly,
            P(("grp", "bus")),
            hourly,
            hourly,
            hourly,
            P(("grp", "bus")),
            P("grp"),
            P("grp"),
        ),
        out_specs=(hourly, hourly, hourly, P(("grp", "bus"))),
        check_vma=False,
    )
```

```python
from types import SimpleNamespace as Space

import jax
import jax.numpy as jnp
from jax import lax
from jax.experimental import pallas as pl
from jax.experimental.pallas import tpu as pltpu
from jax.sharding import PartitionSpec as P

ITERS = 9
MEM = 5
LANES = 128
ROWS = 16
LIMIT = 6 * 1024 * 1024
SPAN = 4
CHUNK = 16
X, Y, E, U, SLOPE, COLUMN = range(6)

primal_step = 0.3
dual_step = 0.3
f32 = jnp.float32
bf16 = jnp.bfloat16


def shape(*dims, dtype=f32):
    return jax.ShapeDtypeStruct(dims, dtype)


def run(body, ins, outs):
    in_leaves, in_tree = jax.tree.flatten(ins)
    out_leaves, out_tree = jax.tree.flatten(outs)

    def kernel(*refs):
        given = jax.tree.unflatten(in_tree, refs[: len(in_leaves)])
        made = jax.tree.unflatten(out_tree, refs[len(in_leaves) :])
        body(Space(**given), Space(**made))

    def place(leaf):
        return pl.BlockSpec(memory_space=pltpu.SMEM if leaf.dtype == jnp.int32 else pltpu.VMEM)

    results = pl.pallas_call(
        kernel,
        out_shape=out_leaves,
        in_specs=[place(leaf) for leaf in in_leaves],
        out_specs=[place(leaf) for leaf in out_leaves],
        compiler_params=pltpu.CompilerParams(vmem_limit_bytes=LIMIT),
        name=body.__name__,
    )(*in_leaves)
    return Space(**jax.tree.unflatten(out_tree, results))


def row_iota(rows):
    return lax.broadcasted_iota(jnp.int32, (rows, LANES), 0)


def tail_sum(block):
    rows = block.shape[0]
    at = row_iota(rows)
    step = 1
    while step < rows:
        block = block + jnp.where(at < rows - step, pltpu.roll(block, rows - step, 0), 0.0)
        step *= 2
    return block


def to_tile(block):
    rows = block.shape[0]
    total = block[0:8]
    for i in range(8, rows, 8):
        total = total + block[i : i + 8]
    return total


def halves(value):
    high = value.astype(bf16)
    return high, (value - high.astype(f32)).astype(bf16)


def product(left, high, low):
    left_high, left_low = left
    rows = left_high.shape[0]
    both = jnp.dot(
        jnp.concatenate([left_high, left_low], axis=0), high, preferred_element_type=f32
    )
    rest = jnp.dot(left_high, low, preferred_element_type=f32)
    return both[:rows] + (both[rows:] + rest)


def running_sum(parts):
    rows = parts[0].shape[0]
    at = lax.broadcasted_iota(jnp.int32, (rows, rows), 0)
    ones = (at >= lax.broadcasted_iota(jnp.int32, (rows, rows), 1)).astype(f32).astype(bf16)
    high, low = (jnp.dot(ones, part, preferred_element_type=f32) for part in parts)
    return high + low


def split_matrix(matrix, column, turns):
    rows = matrix.shape[0]
    width = rows
    step = min(256, rows)
    places = {
        False: (shape(rows, width, dtype=bf16), pl.BlockSpec((step, width), lambda i, b: (i, 0))),
        True: (shape(width, rows, dtype=bf16), pl.BlockSpec((width, step), lambda i, b: (0, i))),
    }

    def split(_, source, *parts):
        for index, turned in enumerate(turns):
            value = source[...].T if turned else source[...]
            parts[2 * index][...], parts[2 * index + 1][...] = halves(value)

    parts = pl.pallas_call(
        split,
        out_shape=[places[turned][0] for turned in turns for _ in range(2)],
        grid_spec=pltpu.PrefetchScalarGridSpec(
            num_scalar_prefetch=1,
            grid=(rows // step,),
            in_specs=[pl.BlockSpec((step, width), lambda i, b: (i, b[0]))],
            out_specs=[places[turned][1] for turned in turns for _ in range(2)],
        ),
        compiler_params=pltpu.CompilerParams(vmem_limit_bytes=2 * LIMIT),
    )(column, matrix)
    return [dict(high=parts[2 * i], low=parts[2 * i + 1]) for i in range(len(turns))]


def solve_rows(entries, values):
    size_n = len(values)
    entries = [list(row) for row in entries]
    values = list(values)
    inverses = []
    for p in range(size_n):
        inverse = 1.0 / entries[p][p]
        inverses.append(inverse)
        for i in range(p + 1, size_n):
            factor = entries[i][p] * inverse
            for j in range(p + 1, size_n):
                entries[i][j] = entries[i][j] - factor * entries[p][j]
            values[i] = values[i] - factor * values[p]
    result = [None] * size_n
    for i in range(size_n - 1, -1, -1):
        value = values[i]
        for j in range(i + 1, size_n):
            value = value - entries[i][j] * result[j]
        result[i] = value * inverses[i]
    return result


def columns_at(iteration):
    return list(range(max(1, iteration - MEM + 1), iteration + 1))


def on_device(
    network,
    upper_bound,
    build_cost,
    unit_cost,
    demand,
    inflow,
    primal_start,
    network_start,
    energy_start,
    build_start,
    accepted,
    restarts,
):
    tm_count, bus_count = lax.axis_size("tm"), lax.axis_size("bus")
    tm, bus = lax.axis_index("tm"), lax.axis_index("bus")
    own_hours, width = primal_start.shape
    hours = SPAN * own_hours
    chunks = [slice(at, at + CHUNK) for at in range(0, hours, CHUNK)]
    flags = jnp.concatenate([accepted, restarts, tm.astype(jnp.int32).reshape(1)])
    first_restart, place_tm = accepted.shape[0], 2 * accepted.shape[0]
    member = shape(hours, width)
    line = shape(1, width)
    row = shape(1, LANES)
    tile = shape(ROWS, LANES)
    weights = shape(hours, LANES)
    kind = {X: member, Y: member, E: member, U: line, SLOPE: member, COLUMN: line}

    upper_bound, build_cost, inflow, build_start = (
        value.reshape(1, width) for value in (upper_bound, build_cost, inflow, build_start)
    )

    def swap(value):
        return lax.ppermute(value, "bus", [(i, (i + 1) % bus_count) for i in range(bus_count)])

    def partner(value, distance):
        return lax.ppermute(value, "tm", [(i, i ^ distance) for i in range(tm_count)])

    distances = [SPAN << i for i in range((tm_count // SPAN).bit_length() - 1)]

    def gathered(value):
        arrived = []
        for distance in distances:
            if arrived:
                value = value + arrived[-1]
            arrived.append(partner(value, distance))
        return value, arrived


    def restart_of(ref, iteration):
        return ref[first_restart + iteration - 1].astype(f32)

    def counter_of(ref, iteration):
        count = jnp.float32(1.0)
        for k in range(1, iteration):
            count = (1.0 - restart_of(ref, k)) * count + 1.0
        return count

    def active_of(ref, column, iteration):
        value = jnp.float32(1.0)
        for k in range(column, iteration + 1):
            value = value * (1.0 - restart_of(ref, k))
        return value

    def over_lanes(step, carried=()):
        def one(j, values):
            return step(pl.ds(pl.multiple_of(j * LANES, LANES), LANES), values)

        return lax.fori_loop(0, width // LANES, one, carried)

    def pair_keys(k, with_line):
        if k == 0:
            return []
        count = len(columns_at(k))
        return [
            (line_too, base + j)
            for line_too in ((False, True) if with_line else (False,))
            for base in (0, 8)
            for j in range(count)
        ]

    def over_pairs(k, step, with_line=False):
        keys = pair_keys(k, with_line)

        def one(sl, values):
            pairs = dict(zip(keys, values))
            step(sl, pairs)
            return tuple(pairs[key] for key in keys)

        zeros = tuple(jnp.zeros((1 if key[0] else 8, LANES), f32) for key in keys)
        return dict(zip(keys, over_lanes(one, zeros)))

    def on_diagonal():
        lane = lax.broadcasted_iota(jnp.int32, (ROWS, LANES), 1)
        return lane == row_iota(ROWS)

    def mixing(i, iteration, products, log):
        columns = columns_at(iteration)
        size_n = len(columns)
        spread = jnp.where(on_diagonal(), jnp.broadcast_to(products, (ROWS, LANES)), 0.0)
        newest = jnp.broadcast_to(jnp.sum(spread, axis=1, keepdims=True), (ROWS, LANES))
        summed = dict(zip(columns[:-1], [ref[...] for ref in i.log]))
        summed[iteration] = newest
        log[...] = newest
        active = [active_of(i.flags, k, iteration) for k in columns]

        def entry(a, b):
            a, b = max(a, b), min(a, b)
            at = columns_at(columns[a]).index(columns[b])
            return summed[columns[a]][at : at + 1]

        gram = [[entry(a, b) for b in range(size_n)] for a in range(size_n)]
        trace = gram[0][0] * active[0]
        for a in range(1, size_n):
            trace = trace + gram[a][a] * active[a]
        shift = 0.001 * trace / size_n + 1e-06
        system = [
            [gram[a][b] * (active[a] * active[b]) for b in range(size_n)] for a in range(size_n)
        ]
        for a in range(size_n):
            system[a][a] = system[a][a] + (1.0 - active[a]) + shift
        right = [newest[8 + a : 9 + a] * active[a] for a in range(size_n)]
        mix = solve_rows(system, right)
        accept = i.flags[iteration - 1].astype(f32)
        return [accept * (value * a) for value, a in zip(mix, active)]

    def mixed(mapped, deltas, coefs):
        if not coefs:
            return mapped
        correction = coefs[0] * deltas[0]
        for coef, delta in zip(coefs[1:], deltas[1:]):
            correction = correction + coef * delta
        return mapped - correction

    def restart_parts(ref, k):
        if k == 0:
            return None, None
        return restart_of(ref, k), 1.0 / jnp.full((1, LANES), counter_of(ref, k), f32)

    def begin(i, o, k, at, name, mapped, deltas, coefs, parts):
        following = mixed(mapped, deltas, coefs)
        if k == 0:
            return following
        restart, inverse = parts
        total = i.totals[name][at] + following if k >= 2 else following
        if k < ITERS - 1:
            o.totals[name][at] = (1.0 - restart) * total
        return jnp.where(restart > 0.5, total * inverse, following)

    def note(i, o, k, at, name, mapped, last, state, pairs):
        residual = mapped - state
        if k < ITERS - 1:
            o.resid[name][at] = residual
        if k == 0:
            return
        if name == U and k < ITERS - 1:
            o.delta[name][at] = mapped - last
        newest = residual - i.resid[name][at]
        if k < ITERS - 1:
            o.column[name][at] = newest
        for j, column in enumerate([ref[at] for ref in i.columns[name]] + [newest]):
            for index, other in ((j, newest), (8 + j, residual)):
                term = column * other
                if name != U:
                    term = to_tile(term)
                pairs[name == U, index] += term

    def pair_tile(pairs, scale=1.0):
        rows = []
        for index in range(ROWS):
            total = jnp.zeros((1, LANES), f32)
            if (False, index) in pairs:
                total = jnp.sum(pairs[False, index], axis=0, keepdims=True)
            if (True, index) in pairs:
                total = total + scale * pairs[True, index]
            rows.append(total)
        return jnp.concatenate(rows, axis=0)

    def beyond(ref, arrived, at, backward):
        total = jnp.zeros((1, LANES), f32)
        for distance, piece in zip(distances, arrived):
            first_half = (ref[place_tm] & distance) == 0
            take = first_half if backward else jnp.logical_not(first_half)
            total = total + jnp.where(take, piece[at], 0.0)
        return total

    def pile(i, o):
        for index, own in enumerate(i.own):
            o.out[index * own_hours : (index + 1) * own_hours, :] = own[...]

    def join(i, o):
        place = i.flags[place_tm] % SPAN
        for index, out in enumerate(o.out):
            group = int(index >= early)
            at = (index - group * early) * own_hours
            for distance in range(SPAN):
                rows = pl.ds(pl.multiple_of((place ^ distance) * own_hours, own_hours), own_hours)
                out[rows, :] = i.stacks[distance][group][at : at + own_hours, :]


    def first(i, o):
        at = (i.flags[place_tm] // SPAN) * hours + row_iota(hours) + 1
        o.weight[...] = 1.0 / at.astype(f32)

        def step(sl, _):
            total = jnp.zeros((8, LANES), f32)
            for rows in chunks:
                total = total + to_tile(i.energy[rows, sl] * o.weight[rows, :])
            o.block[:, sl] = jnp.sum(total, axis=0, keepdims=True)
            return ()

        over_lanes(step)

    def whole(i, sl):
        return i.message[:, sl] + i.arrived[-1][:, sl] if i.arrived else i.message[:, sl]

    def primal_kernel(k):
        count = len(columns_at(k - 1)) if k >= 2 else 0

        def primal(i, o):
            coefs = []
            if k >= 2:
                products = whole(i, slice(width, None))
                coefs = mixing(i, k - 1, products, o.log)
            for j, coef in enumerate(coefs):
                o.coefs[j : j + 1, :] = coef

            parts = restart_parts(i.flags, k)

            def step(sl, pairs):
                line_at = (slice(None), sl)

                def start(name, at, value):
                    deltas = [ref[at] for ref in i.deltas[name]] if count else []
                    if name in (SLOPE, COLUMN):
                        if k < ITERS - 1:
                            o.mapped[name][at] = value
                        if count:
                            newest = value - i.last_map[name][at]
                            if k < ITERS - 1:
                                o.delta[name][at] = newest
                            deltas.append(newest)
                    return begin(i, o, k, at, name, value, deltas, coefs, parts)

                later = beyond(i.flags, i.arrived, line_at, True)
                column = start(COLUMN, line_at, whole(i, sl))
                build = start(U, line_at, i.mapped[U][line_at])
                next_build = jnp.maximum(
                    build - primal_step * (i.build_cost[line_at] - column), 0.0
                )
                o.state[line_at] = build
                o.mapped[U][line_at] = next_build
                block = jnp.zeros((8, LANES), f32)
                for rows in chunks:
                    at = (rows, sl)
                    slope = i.pulled[at] - later
                    slope = start(SLOPE, at, slope)
                    last = i.mapped[X][at]
                    primal = start(X, at, last)
                    next_primal = jnp.clip(
                        primal - primal_step * (i.unit_cost[at] - slope),
                        0.0,
                        i.upper_bound[line_at],
                    )
                    bar = 2.0 * next_primal - primal
                    o.mapped[X][at] = next_primal
                    o.bar[at] = bar
                    block = block + to_tile(bar)
                    note(i, o, k, at, X, next_primal, last, primal, pairs)
                o.block[line_at] = jnp.sum(block, axis=0, keepdims=True)

            o.pairs[...] = pair_tile(over_pairs(k, step))

        return primal

    def push(i, o):
        bar = halves(i.bar[...])
        o.pushed[...] = product(bar, i.high[...], i.low[...])
        o.running[...] = running_sum(bar)

    def coefs_of(i, k):
        return [i.coefs[j : j + 1, :] for j in range(len(columns_at(k - 1)) if k >= 2 else 0)]

    def deltas_of(i, name, at, coefs):
        return [ref[at] for ref in i.deltas[name]] if coefs else []

    def dual_kernel(k):
        def dual(i, o):
            o.mapped[...] = i.pushed[...] + product(halves(i.bar_other[...]), i.high[...], i.low[...])

            coefs, parts = coefs_of(i, k), restart_parts(i.flags, k)

            def step(sl, pairs):
                for rows in chunks:
                    at = (rows, sl)
                    last = i.last[Y][at]
                    deltas = deltas_of(i, Y, at, coefs)
                    state = begin(i, o, k, at, Y, last, deltas, coefs, parts)
                    mapped = jnp.maximum(state + dual_step * (i.demand[at] - o.mapped[at]), 0.0)
                    o.mapped[at] = mapped
                    note(i, o, k, at, Y, mapped, last, state, pairs)

            o.pairs[...] = i.pairs[...] + pair_tile(over_pairs(k, step))

        return dual

    def energy_kernel(k):
        def energy(i, o):
            own_build = (i.flags[place_tm] < SPAN).astype(f32)
            coefs, parts = coefs_of(i, k), restart_parts(i.flags, k)

            def step(sl, pairs):
                line_at = (slice(None), sl)
                earlier = beyond(i.flags, i.arrived, line_at, False)
                build, next_build = i.build[line_at], i.mapped[line_at]
                bar_build = 2.0 * next_build - build
                note(i, o, k, line_at, U, next_build, i.last[U][line_at], build, pairs)
                total = jnp.zeros((8, LANES), f32)
                for rows in chunks:
                    at = (rows, sl)
                    running = i.running[at] + earlier
                    last = i.last[E][at]
                    deltas = deltas_of(i, E, at, coefs)
                    state = begin(i, o, k, at, E, last, deltas, coefs, parts)
                    slack = (bar_build - running) * i.weight[rows, :]
                    mapped = jnp.maximum(
                        state + dual_step * (-i.inflow[line_at] - slack), 0.0
                    )
                    o.mapped[at] = mapped
                    note(i, o, k, at, E, mapped, last, state, pairs)
                    if k < ITERS - 1:
                        total = total + to_tile(mapped * i.weight[rows, :])
                if k < ITERS - 1:
                    o.block[line_at] = jnp.sum(total, axis=0, keepdims=True)

            pairs = over_pairs(k, step, True)
            if k >= 1:
                lines = i.pairs[...] + pair_tile(pairs, own_build)
                sums = jnp.broadcast_to(jnp.sum(lines, axis=1, keepdims=True), (ROWS, LANES))
                o.products[...] = jnp.sum(
                    jnp.where(on_diagonal(), sums, 0.0), axis=0, keepdims=True
                )
            else:
                o.products[...] = jnp.zeros((1, LANES), f32)

        return energy

    def pull(i, o):
        o.pulled[...] = product(halves(i.dual[...]), i.own[0][...], i.own[1][...])
        o.pulled[...] += product(halves(i.dual_other[...]), i.other[0][...], i.other[1][...])

        def step(sl, _):
            carry = jnp.zeros((1, LANES), f32)
            for rows in reversed(chunks):
                tail = tail_sum(i.energy[rows, sl] * i.weight[rows, :]) + carry
                o.pulled[rows, sl] -= tail
                carry = tail[0:1]
                for name, out in o.delta.items():
                    out[rows, sl] = i.mapped[name][rows, sl] - i.last[name][rows, sl]
            return ()

        over_lanes(step)

    def last_kernel(i, o):
        place = i.flags[place_tm] % SPAN
        own = pl.ds(pl.multiple_of(place * own_hours, own_hours), own_hours)
        coefs = mixing(i, ITERS - 1, whole(i, slice(None)), o.log)

        def step(sl, _):
            for name in (X, Y, E, U):
                at = (slice(None) if name == U else own, sl)
                mapped = i.mapped[name][at]
                deltas = [ref[at] for ref in i.deltas[name]] + [mapped - i.last[name][at]]
                o.following[name][:, sl] = mixed(mapped, deltas, coefs)
            return ()

        over_lanes(step)


    deltas = {name: [] for name in kind}
    columns = {name: [] for name in (X, Y, E, U)}
    totals, last_map, resid, logs = {}, {}, {}, {}

    def send_totals(block, products, dual, dual_other, energy, maps=None):
        row = block
        if products is not None:
            row = jnp.concatenate([block, products + swap(products)], axis=1)
        row, arrived = gathered(row)
        out = run(
            pull,
            dict(
                dual=dual,
                dual_other=dual_other,
                energy=energy,
                weight=weight,
                **(maps or {}),
                own=[pull_own[part] for part in sorted(pull_own)],
                other=[pull_other[part] for part in sorted(pull_other)],
            ),
            dict(pulled=member, delta=kinds(X, Y, E) if maps else {}),
        )
        for name in out.delta:
            deltas[name] = (deltas[name] + [out.delta[name]])[-MEM:]
        return dict(message=row, arrived=arrived, pulled=out.pulled)

    def picked(source, names):
        return {name: source[name] for name in names}

    def kinds(*names):
        return picked(kind, names)

    def note_ins(k, names):
        if k == 0:
            return {}
        return dict(
            resid=picked(resid, names),
            columns={name: columns[name][-(MEM - 1) :] for name in names},
        )

    def begin_ins(k, name):
        if k < 2:
            return {}
        return dict(coefs=one.coefs, deltas={name: deltas[name]}, totals={name: totals[name]})

    def begin_outs(k, name):
        return dict(totals=kinds(name)) if 1 <= k < ITERS - 1 else {}

    def note_outs(k, names):
        each = kinds(*names)
        if k == ITERS - 1:
            return {}
        if k == 0:
            return dict(resid=each)
        return dict(resid=each, delta=kinds(U) if U in names else {}, column=each)

    def take(k, out, names):
        for name in names:
            resid[name] = out.resid[name]
            if k:
                if name == U:
                    deltas[name] = (deltas[name] + [out.delta[name]])[-MEM:]
                columns[name] = (columns[name] + [out.column[name]])[-MEM:]

    def log_ins(iteration):
        return [logs[j] for j in columns_at(iteration)[:-1]]

    starts = [primal_start, network_start, energy_start, unit_cost, demand]
    early = 3
    stacks = [
        run(pile, dict(own=group), dict(out=shape(len(group) * own_hours, width))).out
        for group in (starts[:early], starts[early:])
    ]
    near = [partner(stack, 1) for stack in stacks]
    far = [partner(stack, 2) for stack in stacks]
    place = bus.astype(jnp.int32).reshape(1)
    pull_own, push_own = split_matrix(network, place, (False, True))
    (push_other,) = split_matrix(network, 1 - place, (True,))
    (pull_other,) = split_matrix(swap(network), place, (False,))
    near, far, pull_own, push_own, push_other = lax.optimization_barrier(
        (near, far, pull_own, push_own, push_other)
    )
    across = [partner(near[0], 2), partner(far[1], 1)]
    across, pull_other = lax.optimization_barrier((across, pull_other))
    primal, dual, energy, unit_cost, demand = run(
        join,
        dict(flags=flags, stacks=[stacks, near, far, across]),
        dict(out=[member] * len(starts)),
    ).out
    out = run(first, dict(flags=flags, energy=energy), dict(block=line, weight=weights))
    block, weight = out.block, out.weight
    mapped = {X: primal, Y: dual, E: energy, U: build_start}
    totals_in = send_totals(block, None, dual, swap(dual), energy)

    for k in range(ITERS):
        mixes = k >= 2
        keeps = k < ITERS - 1
        ins = dict(
            flags=flags,
            **totals_in,
            mapped=picked(mapped, (X, U)),
            unit_cost=unit_cost,
            upper_bound=upper_bound,
            build_cost=build_cost,
            **note_ins(k, (X,)),
        )
        outs = dict(
            mapped=kinds(SLOPE, COLUMN, X, U) if keeps else kinds(X, U),
            state=line,
            bar=member,
            block=line,
            pairs=tile,
            **note_outs(k, (X,)),
        )
        if mixes:
            ins.update(
                log=log_ins(k - 1),
                last_map=picked(last_map, (SLOPE, COLUMN)),
                totals=picked(totals, (SLOPE, COLUMN, X, U)),
                deltas={
                    SLOPE: deltas[SLOPE][-(MEM - 1) :],
                    COLUMN: deltas[COLUMN][-(MEM - 1) :],
                    X: deltas[X],
                    U: deltas[U],
                },
            )
            outs.update(log=tile, coefs=shape(8, LANES))
            if keeps:
                outs["delta"] = {**outs["delta"], **kinds(SLOPE, COLUMN)}
        if 1 <= k < ITERS - 1:
            outs.update(totals=kinds(SLOPE, COLUMN, X, U))
        one = run(primal_kernel(k), ins, outs)
        if mixes:
            logs[k - 1] = one.log
        if mixes and keeps:
            for name in (SLOPE, COLUMN):
                deltas[name] = (deltas[name] + [one.delta[name]])[-MEM:]
        if keeps:
            last_map.update(picked(one.mapped, (SLOPE, COLUMN)))
        if 1 <= k < ITERS - 1:
            totals.update(one.totals)
        _, earlier = gathered(one.block)
        bar_other = swap(one.bar)
        two = run(push, dict(bar=one.bar, **push_own), dict(pushed=member, running=member))
        three = run(
            dual_kernel(k),
            dict(
                flags=flags,
                pushed=two.pushed,
                bar_other=bar_other,
                last=picked(mapped, (Y,)),
                demand=demand,
                pairs=one.pairs,
                **push_other,
                **begin_ins(k, Y),
                **note_ins(k, (Y,)),
            ),
            dict(mapped=member, pairs=tile, **begin_outs(k, Y), **note_outs(k, (Y,))),
        )
        four = run(
            energy_kernel(k),
            dict(
                flags=flags,
                running=two.running,
                arrived=earlier,
                last=picked(mapped, (E, U)),
                build=one.state,
                mapped=one.mapped[U],
                inflow=inflow,
                weight=weight,
                pairs=three.pairs,
                **begin_ins(k, E),
                **note_ins(k, (E, U)),
            ),
            dict(
                mapped=member,
                products=row,
                **(dict(block=line) if keeps else {}),
                **begin_outs(k, E),
                **note_outs(k, (E, U)),
            ),
        )
        if 1 <= k < ITERS - 1:
            totals.update(three.totals)
            totals.update(four.totals)
        if keeps:
            take(k, one, (X,))
            take(k, three, (Y,))
            take(k, four, (E, U))
        last = mapped
        mapped = {X: one.mapped[X], Y: three.mapped, E: four.mapped, U: one.mapped[U]}
        if keeps:
            dual, products = lax.optimization_barrier((mapped[Y], four.products))
            maps = None
            if k >= 1:
                maps = dict(mapped=picked(mapped, (X, Y, E)), last=picked(last, (X, Y, E)))
            totals_in = send_totals(four.block, products, dual, swap(dual), mapped[E], maps)

    products = four.products + swap(four.products)
    message, arrived = gathered(products)
    out = run(
        last_kernel,
        dict(
            flags=flags,
            message=message,
            arrived=arrived,
            log=log_ins(ITERS - 1),
            mapped=mapped,
            last=last,
            deltas={name: deltas[name][-(MEM - 1) :] for name in (X, Y, E, U)},
        ),
        dict(
            log=tile,
            following={name: line if name == U else shape(own_hours, width) for name in (X, Y, E, U)},
        ),
    )
    final = out.following
    return final[X], final[Y], final[E], final[U].reshape(width)


def solution(mesh):
    hourly = P(("grp", "tm"), "bus")
    return jax.shard_map(
        on_device,
        mesh=mesh,
        in_specs=(
            P("bus", None),
            P("bus"),
            P("bus"),
            hourly,
            hourly,
            P(("grp", "bus")),
            hourly,
            hourly,
            hourly,
            P(("grp", "bus")),
            P("grp"),
            P("grp"),
        ),
        out_specs=(hourly, hourly, hourly, P(("grp", "bus"))),
        check_vma=False,
    )
```

```python
from types import SimpleNamespace as Space

import jax
import jax.numpy as jnp
from jax import lax
from jax.experimental import pallas as pl
from jax.experimental.pallas import tpu as pltpu
from jax.sharding import PartitionSpec as P

ITERS = 9
MEM = 5
LANES = 128
ROWS = 16
LIMIT = 6 * 1024 * 1024
SPAN = 4
CHUNK = 8
X, Y, E, U, SLOPE, COLUMN = range(6)

primal_step = 0.3
dual_step = 0.3
f32 = jnp.float32
bf16 = jnp.bfloat16


def shape(*dims, dtype=f32):
    return jax.ShapeDtypeStruct(dims, dtype)


def run(body, ins, outs):
    in_leaves, in_tree = jax.tree.flatten(ins)
    out_leaves, out_tree = jax.tree.flatten(outs)

    def kernel(*refs):
        given = jax.tree.unflatten(in_tree, refs[: len(in_leaves)])
        made = jax.tree.unflatten(out_tree, refs[len(in_leaves) :])
        body(Space(**given), Space(**made))

    def place(leaf):
        return pl.BlockSpec(memory_space=pltpu.SMEM if leaf.dtype == jnp.int32 else pltpu.VMEM)

    results = pl.pallas_call(
        kernel,
        out_shape=out_leaves,
        in_specs=[place(leaf) for leaf in in_leaves],
        out_specs=[place(leaf) for leaf in out_leaves],
        compiler_params=pltpu.CompilerParams(vmem_limit_bytes=LIMIT),
        name=body.__name__,
    )(*in_leaves)
    return Space(**jax.tree.unflatten(out_tree, results))


def row_iota(rows):
    return lax.broadcasted_iota(jnp.int32, (rows, LANES), 0)


def tail_sum(block):
    rows = block.shape[0]
    at = row_iota(rows)
    step = 1
    while step < rows:
        block = block + jnp.where(at < rows - step, pltpu.roll(block, rows - step, 0), 0.0)
        step *= 2
    return block


def to_tile(block):
    rows = block.shape[0]
    total = block[0:8]
    for i in range(8, rows, 8):
        total = total + block[i : i + 8]
    return total


def halves(value):
    high = value.astype(bf16)
    return high, (value - high.astype(f32)).astype(bf16)


def product(left, high, low):
    left_high, left_low = left
    rows = left_high.shape[0]
    both = jnp.dot(
        jnp.concatenate([left_high, left_low], axis=0), high, preferred_element_type=f32
    )
    rest = jnp.dot(left_high, low, preferred_element_type=f32)
    return both[:rows] + (both[rows:] + rest)


def running_sum(parts):
    rows = parts[0].shape[0]
    at = lax.broadcasted_iota(jnp.int32, (rows, rows), 0)
    ones = (at >= lax.broadcasted_iota(jnp.int32, (rows, rows), 1)).astype(f32).astype(bf16)
    high, low = (jnp.dot(ones, part, preferred_element_type=f32) for part in parts)
    return high + low


def split_matrix(matrix, column, turns):
    rows = matrix.shape[0]
    width = rows
    step = min(256, rows)
    places = {
        False: (shape(rows, width, dtype=bf16), pl.BlockSpec((step, width), lambda i, b: (i, 0))),
        True: (shape(width, rows, dtype=bf16), pl.BlockSpec((width, step), lambda i, b: (0, i))),
    }

    def split(_, source, *parts):
        for index, turned in enumerate(turns):
            value = source[...].T if turned else source[...]
            parts[2 * index][...], parts[2 * index + 1][...] = halves(value)

    parts = pl.pallas_call(
        split,
        out_shape=[places[turned][0] for turned in turns for _ in range(2)],
        grid_spec=pltpu.PrefetchScalarGridSpec(
            num_scalar_prefetch=1,
            grid=(rows // step,),
            in_specs=[pl.BlockSpec((step, width), lambda i, b: (i, b[0]))],
            out_specs=[places[turned][1] for turned in turns for _ in range(2)],
        ),
        compiler_params=pltpu.CompilerParams(vmem_limit_bytes=2 * LIMIT),
    )(column, matrix)
    return [dict(high=parts[2 * i], low=parts[2 * i + 1]) for i in range(len(turns))]


def solve_rows(entries, values):
    size_n = len(values)
    entries = [list(row) for row in entries]
    values = list(values)
    inverses = []
    for p in range(size_n):
        inverse = 1.0 / entries[p][p]
        inverses.append(inverse)
        for i in range(p + 1, size_n):
            factor = entries[i][p] * inverse
            for j in range(p + 1, size_n):
                entries[i][j] = entries[i][j] - factor * entries[p][j]
            values[i] = values[i] - factor * values[p]
    result = [None] * size_n
    for i in range(size_n - 1, -1, -1):
        value = values[i]
        for j in range(i + 1, size_n):
            value = value - entries[i][j] * result[j]
        result[i] = value * inverses[i]
    return result


def columns_at(iteration):
    return list(range(max(1, iteration - MEM + 1), iteration + 1))


def on_device(
    network,
    upper_bound,
    build_cost,
    unit_cost,
    demand,
    inflow,
    primal_start,
    network_start,
    energy_start,
    build_start,
    accepted,
    restarts,
):
    tm_count, bus_count = lax.axis_size("tm"), lax.axis_size("bus")
    tm, bus = lax.axis_index("tm"), lax.axis_index("bus")
    own_hours, width = primal_start.shape
    hours = SPAN * own_hours
    chunks = [slice(at, at + CHUNK) for at in range(0, hours, CHUNK)]
    flags = jnp.concatenate([accepted, restarts, tm.astype(jnp.int32).reshape(1)])
    first_restart, place_tm = accepted.shape[0], 2 * accepted.shape[0]
    member = shape(hours, width)
    line = shape(1, width)
    row = shape(1, LANES)
    tile = shape(ROWS, LANES)
    weights = shape(hours, LANES)
    kind = {X: member, Y: member, E: member, U: line, SLOPE: member, COLUMN: line}

    upper_bound, build_cost, inflow, build_start = (
        value.reshape(1, width) for value in (upper_bound, build_cost, inflow, build_start)
    )

    def swap(value):
        return lax.ppermute(value, "bus", [(i, (i + 1) % bus_count) for i in range(bus_count)])

    def partner(value, distance):
        return lax.ppermute(value, "tm", [(i, i ^ distance) for i in range(tm_count)])

    distances = [SPAN << i for i in range((tm_count // SPAN).bit_length() - 1)]

    def gathered(value):
        arrived = []
        for distance in distances:
            if arrived:
                value = value + arrived[-1]
            arrived.append(partner(value, distance))
        return value, arrived


    def restart_of(ref, iteration):
        return ref[first_restart + iteration - 1].astype(f32)

    def counter_of(ref, iteration):
        count = jnp.float32(1.0)
        for k in range(1, iteration):
            count = (1.0 - restart_of(ref, k)) * count + 1.0
        return count

    def active_of(ref, column, iteration):
        value = jnp.float32(1.0)
        for k in range(column, iteration + 1):
            value = value * (1.0 - restart_of(ref, k))
        return value

    def over_lanes(step, carried=()):
        def one(j, values):
            return step(pl.ds(pl.multiple_of(j * LANES, LANES), LANES), values)

        return lax.fori_loop(0, width // LANES, one, carried)

    def pair_keys(k, with_line):
        if k == 0:
            return []
        count = len(columns_at(k))
        return [
            (line_too, base + j)
            for line_too in ((False, True) if with_line else (False,))
            for base in (0, 8)
            for j in range(count)
        ]

    def over_pairs(k, step, with_line=False):
        keys = pair_keys(k, with_line)

        def one(sl, values):
            pairs = dict(zip(keys, values))
            step(sl, pairs)
            return tuple(pairs[key] for key in keys)

        zeros = tuple(jnp.zeros((1 if key[0] else 8, LANES), f32) for key in keys)
        return dict(zip(keys, over_lanes(one, zeros)))

    def on_diagonal():
        lane = lax.broadcasted_iota(jnp.int32, (ROWS, LANES), 1)
        return lane == row_iota(ROWS)

    def mixing(i, iteration, products, log):
        columns = columns_at(iteration)
        size_n = len(columns)
        spread = jnp.where(on_diagonal(), jnp.broadcast_to(products, (ROWS, LANES)), 0.0)
        newest = jnp.broadcast_to(jnp.sum(spread, axis=1, keepdims=True), (ROWS, LANES))
        summed = dict(zip(columns[:-1], [ref[...] for ref in i.log]))
        summed[iteration] = newest
        log[...] = newest
        active = [active_of(i.flags, k, iteration) for k in columns]

        def entry(a, b):
            a, b = max(a, b), min(a, b)
            at = columns_at(columns[a]).index(columns[b])
            return summed[columns[a]][at : at + 1]

        gram = [[entry(a, b) for b in range(size_n)] for a in range(size_n)]
        trace = gram[0][0] * active[0]
        for a in range(1, size_n):
            trace = trace + gram[a][a] * active[a]
        shift = 0.001 * trace / size_n + 1e-06
        system = [
            [gram[a][b] * (active[a] * active[b]) for b in range(size_n)] for a in range(size_n)
        ]
        for a in range(size_n):
            system[a][a] = system[a][a] + (1.0 - active[a]) + shift
        right = [newest[8 + a : 9 + a] * active[a] for a in range(size_n)]
        mix = solve_rows(system, right)
        accept = i.flags[iteration - 1].astype(f32)
        return [accept * (value * a) for value, a in zip(mix, active)]

    def mixed(mapped, deltas, coefs):
        if not coefs:
            return mapped
        correction = coefs[0] * deltas[0]
        for coef, delta in zip(coefs[1:], deltas[1:]):
            correction = correction + coef * delta
        return mapped - correction

    def restart_parts(ref, k):
        if k == 0:
            return None, None
        return restart_of(ref, k), 1.0 / jnp.full((1, LANES), counter_of(ref, k), f32)

    def begin(i, o, k, at, name, mapped, deltas, coefs, parts):
        following = mixed(mapped, deltas, coefs)
        if k == 0:
            return following
        restart, inverse = parts
        total = i.totals[name][at] + following if k >= 2 else following
        if k < ITERS - 1:
            o.totals[name][at] = (1.0 - restart) * total
        return jnp.where(restart > 0.5, total * inverse, following)

    def note(i, o, k, at, name, mapped, last, state, pairs):
        residual = mapped - state
        if k < ITERS - 1:
            o.resid[name][at] = residual
        if k == 0:
            return
        if name == U and k < ITERS - 1:
            o.delta[name][at] = mapped - last
        newest = residual - i.resid[name][at]
        if k < ITERS - 1:
            o.column[name][at] = newest
        for j, column in enumerate([ref[at] for ref in i.columns[name]] + [newest]):
            for index, other in ((j, newest), (8 + j, residual)):
                term = column * other
                if name != U:
                    term = to_tile(term)
                pairs[name == U, index] += term

    def pair_tile(pairs, scale=1.0):
        rows = []
        for index in range(ROWS):
            total = jnp.zeros((1, LANES), f32)
            if (False, index) in pairs:
                total = jnp.sum(pairs[False, index], axis=0, keepdims=True)
            if (True, index) in pairs:
                total = total + scale * pairs[True, index]
            rows.append(total)
        return jnp.concatenate(rows, axis=0)

    def beyond(ref, arrived, at, backward):
        total = jnp.zeros((1, LANES), f32)
        for distance, piece in zip(distances, arrived):
            first_half = (ref[place_tm] & distance) == 0
            take = first_half if backward else jnp.logical_not(first_half)
            total = total + jnp.where(take, piece[at], 0.0)
        return total

    def pile(i, o):
        for index, own in enumerate(i.own):
            o.out[index * own_hours : (index + 1) * own_hours, :] = own[...]

    def join(i, o):
        place = i.flags[place_tm] % SPAN
        for index, out in enumerate(o.out):
            group = int(index >= early)
            at = (index - group * early) * own_hours
            for distance in range(SPAN):
                rows = pl.ds(pl.multiple_of((place ^ distance) * own_hours, own_hours), own_hours)
                out[rows, :] = i.stacks[distance][group][at : at + own_hours, :]


    def first(i, o):
        at = (i.flags[place_tm] // SPAN) * hours + row_iota(hours) + 1
        o.weight[...] = 1.0 / at.astype(f32)

        def step(sl, _):
            total = jnp.zeros((8, LANES), f32)
            for rows in chunks:
                total = total + to_tile(i.energy[rows, sl] * o.weight[rows, :])
            o.block[:, sl] = jnp.sum(total, axis=0, keepdims=True)
            return ()

        over_lanes(step)

    def whole(i, sl):
        return i.message[:, sl] + i.arrived[-1][:, sl] if i.arrived else i.message[:, sl]

    def primal_kernel(k):
        count = len(columns_at(k - 1)) if k >= 2 else 0

        def primal(i, o):
            coefs = []
            if k >= 2:
                products = whole(i, slice(width, None))
                coefs = mixing(i, k - 1, products, o.log)
            for j, coef in enumerate(coefs):
                o.coefs[j : j + 1, :] = coef

            parts = restart_parts(i.flags, k)

            def step(sl, pairs):
                line_at = (slice(None), sl)

                def start(name, at, value):
                    deltas = [ref[at] for ref in i.deltas[name]] if count else []
                    if name in (SLOPE, COLUMN):
                        if k < ITERS - 1:
                            o.mapped[name][at] = value
                        if count:
                            newest = value - i.last_map[name][at]
                            if k < ITERS - 1:
                                o.delta[name][at] = newest
                            deltas.append(newest)
                    return begin(i, o, k, at, name, value, deltas, coefs, parts)

                later = beyond(i.flags, i.arrived, line_at, True)
                column = start(COLUMN, line_at, whole(i, sl))
                build = start(U, line_at, i.mapped[U][line_at])
                next_build = jnp.maximum(
                    build - primal_step * (i.build_cost[line_at] - column), 0.0
                )
                o.state[line_at] = build
                o.mapped[U][line_at] = next_build
                block = jnp.zeros((8, LANES), f32)
                for rows in chunks:
                    at = (rows, sl)
                    slope = i.pulled[at] - later
                    slope = start(SLOPE, at, slope)
                    last = i.mapped[X][at]
                    primal = start(X, at, last)
                    next_primal = jnp.clip(
                        primal - primal_step * (i.unit_cost[at] - slope),
                        0.0,
                        i.upper_bound[line_at],
                    )
                    bar = 2.0 * next_primal - primal
                    o.mapped[X][at] = next_primal
                    o.bar[at] = bar
                    block = block + to_tile(bar)
                    note(i, o, k, at, X, next_primal, last, primal, pairs)
                o.block[line_at] = jnp.sum(block, axis=0, keepdims=True)

            o.pairs[...] = pair_tile(over_pairs(k, step))

        return primal

    def push(i, o):
        bar = halves(i.bar[...])
        o.pushed[...] = product(bar, i.high[...], i.low[...])
        o.running[...] = running_sum(bar)

    def coefs_of(i, k):
        return [i.coefs[j : j + 1, :] for j in range(len(columns_at(k - 1)) if k >= 2 else 0)]

    def deltas_of(i, name, at, coefs):
        return [ref[at] for ref in i.deltas[name]] if coefs else []

    def dual_kernel(k):
        def dual(i, o):
            o.mapped[...] = i.pushed[...] + product(halves(i.bar_other[...]), i.high[...], i.low[...])

            coefs, parts = coefs_of(i, k), restart_parts(i.flags, k)

            def step(sl, pairs):
                for rows in chunks:
                    at = (rows, sl)
                    last = i.last[Y][at]
                    deltas = deltas_of(i, Y, at, coefs)
                    state = begin(i, o, k, at, Y, last, deltas, coefs, parts)
                    mapped = jnp.maximum(state + dual_step * (i.demand[at] - o.mapped[at]), 0.0)
                    o.mapped[at] = mapped
                    note(i, o, k, at, Y, mapped, last, state, pairs)

            o.pairs[...] = i.pairs[...] + pair_tile(over_pairs(k, step))

        return dual

    def energy_kernel(k):
        def energy(i, o):
            own_build = (i.flags[place_tm] < SPAN).astype(f32)
            coefs, parts = coefs_of(i, k), restart_parts(i.flags, k)

            def step(sl, pairs):
                line_at = (slice(None), sl)
                earlier = beyond(i.flags, i.arrived, line_at, False)
                build, next_build = i.build[line_at], i.mapped[line_at]
                bar_build = 2.0 * next_build - build
                note(i, o, k, line_at, U, next_build, i.last[U][line_at], build, pairs)
                total = jnp.zeros((8, LANES), f32)
                for rows in chunks:
                    at = (rows, sl)
                    running = i.running[at] + earlier
                    last = i.last[E][at]
                    deltas = deltas_of(i, E, at, coefs)
                    state = begin(i, o, k, at, E, last, deltas, coefs, parts)
                    slack = (bar_build - running) * i.weight[rows, :]
                    mapped = jnp.maximum(
                        state + dual_step * (-i.inflow[line_at] - slack), 0.0
                    )
                    o.mapped[at] = mapped
                    note(i, o, k, at, E, mapped, last, state, pairs)
                    if k < ITERS - 1:
                        total = total + to_tile(mapped * i.weight[rows, :])
                if k < ITERS - 1:
                    o.block[line_at] = jnp.sum(total, axis=0, keepdims=True)

            pairs = over_pairs(k, step, True)
            if k >= 1:
                lines = i.pairs[...] + pair_tile(pairs, own_build)
                sums = jnp.broadcast_to(jnp.sum(lines, axis=1, keepdims=True), (ROWS, LANES))
                o.products[...] = jnp.sum(
                    jnp.where(on_diagonal(), sums, 0.0), axis=0, keepdims=True
                )
            else:
                o.products[...] = jnp.zeros((1, LANES), f32)

        return energy

    def pull(i, o):
        o.pulled[...] = product(halves(i.dual[...]), i.own[0][...], i.own[1][...])
        o.pulled[...] += product(halves(i.dual_other[...]), i.other[0][...], i.other[1][...])

        def step(sl, _):
            carry = jnp.zeros((1, LANES), f32)
            for rows in reversed(chunks):
                tail = tail_sum(i.energy[rows, sl] * i.weight[rows, :]) + carry
                o.pulled[rows, sl] -= tail
                carry = tail[0:1]
                for name, out in o.delta.items():
                    out[rows, sl] = i.mapped[name][rows, sl] - i.last[name][rows, sl]
            return ()

        over_lanes(step)

    def last_kernel(i, o):
        place = i.flags[place_tm] % SPAN
        own = pl.ds(pl.multiple_of(place * own_hours, own_hours), own_hours)
        coefs = mixing(i, ITERS - 1, whole(i, slice(None)), o.log)

        def step(sl, _):
            for name in (X, Y, E, U):
                at = (slice(None) if name == U else own, sl)
                mapped = i.mapped[name][at]
                deltas = [ref[at] for ref in i.deltas[name]] + [mapped - i.last[name][at]]
                o.following[name][:, sl] = mixed(mapped, deltas, coefs)
            return ()

        over_lanes(step)


    deltas = {name: [] for name in kind}
    columns = {name: [] for name in (X, Y, E, U)}
    totals, last_map, resid, logs = {}, {}, {}, {}

    def send_totals(block, products, dual, dual_other, energy, maps=None):
        row = block
        if products is not None:
            row = jnp.concatenate([block, products + swap(products)], axis=1)
        row, arrived = gathered(row)
        out = run(
            pull,
            dict(
                dual=dual,
                dual_other=dual_other,
                energy=energy,
                weight=weight,
                **(maps or {}),
                own=[pull_own[part] for part in sorted(pull_own)],
                other=[pull_other[part] for part in sorted(pull_other)],
            ),
            dict(pulled=member, delta=kinds(X, Y, E) if maps else {}),
        )
        for name in out.delta:
            deltas[name] = (deltas[name] + [out.delta[name]])[-MEM:]
        return dict(message=row, arrived=arrived, pulled=out.pulled)

    def picked(source, names):
        return {name: source[name] for name in names}

    def kinds(*names):
        return picked(kind, names)

    def note_ins(k, names):
        if k == 0:
            return {}
        return dict(
            resid=picked(resid, names),
            columns={name: columns[name][-(MEM - 1) :] for name in names},
        )

    def begin_ins(k, name):
        if k < 2:
            return {}
        return dict(coefs=one.coefs, deltas={name: deltas[name]}, totals={name: totals[name]})

    def begin_outs(k, name):
        return dict(totals=kinds(name)) if 1 <= k < ITERS - 1 else {}

    def note_outs(k, names):
        each = kinds(*names)
        if k == ITERS - 1:
            return {}
        if k == 0:
            return dict(resid=each)
        return dict(resid=each, delta=kinds(U) if U in names else {}, column=each)

    def take(k, out, names):
        for name in names:
            resid[name] = out.resid[name]
            if k:
                if name == U:
                    deltas[name] = (deltas[name] + [out.delta[name]])[-MEM:]
                columns[name] = (columns[name] + [out.column[name]])[-MEM:]

    def log_ins(iteration):
        return [logs[j] for j in columns_at(iteration)[:-1]]

    starts = [primal_start, network_start, energy_start, unit_cost, demand]
    early = 3
    stacks = [
        run(pile, dict(own=group), dict(out=shape(len(group) * own_hours, width))).out
        for group in (starts[:early], starts[early:])
    ]
    near = [partner(stack, 1) for stack in stacks]
    far = [partner(stack, 2) for stack in stacks]
    place = bus.astype(jnp.int32).reshape(1)
    pull_own, push_own = split_matrix(network, place, (False, True))
    (push_other,) = split_matrix(network, 1 - place, (True,))
    (pull_other,) = split_matrix(swap(network), place, (False,))
    near, far, pull_own, push_own, push_other = lax.optimization_barrier(
        (near, far, pull_own, push_own, push_other)
    )
    across = [partner(near[0], 2), partner(far[1], 1)]
    across, pull_other = lax.optimization_barrier((across, pull_other))
    primal, dual, energy, unit_cost, demand = run(
        join,
        dict(flags=flags, stacks=[stacks, near, far, across]),
        dict(out=[member] * len(starts)),
    ).out
    out = run(first, dict(flags=flags, energy=energy), dict(block=line, weight=weights))
    block, weight = out.block, out.weight
    mapped = {X: primal, Y: dual, E: energy, U: build_start}
    totals_in = send_totals(block, None, dual, swap(dual), energy)

    for k in range(ITERS):
        mixes = k >= 2
        keeps = k < ITERS - 1
        ins = dict(
            flags=flags,
            **totals_in,
            mapped=picked(mapped, (X, U)),
            unit_cost=unit_cost,
            upper_bound=upper_bound,
            build_cost=build_cost,
            **note_ins(k, (X,)),
        )
        outs = dict(
            mapped=kinds(SLOPE, COLUMN, X, U) if keeps else kinds(X, U),
            state=line,
            bar=member,
            block=line,
            pairs=tile,
            **note_outs(k, (X,)),
        )
        if mixes:
            ins.update(
                log=log_ins(k - 1),
                last_map=picked(last_map, (SLOPE, COLUMN)),
                totals=picked(totals, (SLOPE, COLUMN, X, U)),
                deltas={
                    SLOPE: deltas[SLOPE][-(MEM - 1) :],
                    COLUMN: deltas[COLUMN][-(MEM - 1) :],
                    X: deltas[X],
                    U: deltas[U],
                },
            )
            outs.update(log=tile, coefs=shape(8, LANES))
            if keeps:
                outs["delta"] = {**outs["delta"], **kinds(SLOPE, COLUMN)}
        if 1 <= k < ITERS - 1:
            outs.update(totals=kinds(SLOPE, COLUMN, X, U))
        one = run(primal_kernel(k), ins, outs)
        if mixes:
            logs[k - 1] = one.log
        if mixes and keeps:
            for name in (SLOPE, COLUMN):
                deltas[name] = (deltas[name] + [one.delta[name]])[-MEM:]
        if keeps:
            last_map.update(picked(one.mapped, (SLOPE, COLUMN)))
        if 1 <= k < ITERS - 1:
            totals.update(one.totals)
        _, earlier = gathered(one.block)
        bar_other = swap(one.bar)
        two = run(push, dict(bar=one.bar, **push_own), dict(pushed=member, running=member))
        three = run(
            dual_kernel(k),
            dict(
                flags=flags,
                pushed=two.pushed,
                bar_other=bar_other,
                last=picked(mapped, (Y,)),
                demand=demand,
                pairs=one.pairs,
                **push_other,
                **begin_ins(k, Y),
                **note_ins(k, (Y,)),
            ),
            dict(mapped=member, pairs=tile, **begin_outs(k, Y), **note_outs(k, (Y,))),
        )
        four = run(
            energy_kernel(k),
            dict(
                flags=flags,
                running=two.running,
                arrived=earlier,
                last=picked(mapped, (E, U)),
                build=one.state,
                mapped=one.mapped[U],
                inflow=inflow,
                weight=weight,
                pairs=three.pairs,
                **begin_ins(k, E),
                **note_ins(k, (E, U)),
            ),
            dict(
                mapped=member,
                products=row,
                **(dict(block=line) if keeps else {}),
                **begin_outs(k, E),
                **note_outs(k, (E, U)),
            ),
        )
        if 1 <= k < ITERS - 1:
            totals.update(three.totals)
            totals.update(four.totals)
        if keeps:
            take(k, one, (X,))
            take(k, three, (Y,))
            take(k, four, (E, U))
        last = mapped
        mapped = {X: one.mapped[X], Y: three.mapped, E: four.mapped, U: one.mapped[U]}
        if keeps:
            dual, products = lax.optimization_barrier((mapped[Y], four.products))
            maps = None
            if k >= 1:
                maps = dict(mapped=picked(mapped, (X, Y, E)), last=picked(last, (X, Y, E)))
            totals_in = send_totals(four.block, products, dual, swap(dual), mapped[E], maps)

    products = four.products + swap(four.products)
    message, arrived = gathered(products)
    out = run(
        last_kernel,
        dict(
            flags=flags,
            message=message,
            arrived=arrived,
            log=log_ins(ITERS - 1),
            mapped=mapped,
            last=last,
            deltas={name: deltas[name][-(MEM - 1) :] for name in (X, Y, E, U)},
        ),
        dict(
            log=tile,
            following={name: line if name == U else shape(own_hours, width) for name in (X, Y, E, U)},
        ),
    )
    final = out.following
    return final[X], final[Y], final[E], final[U].reshape(width)


def solution(mesh):
    hourly = P(("grp", "tm"), "bus")
    return jax.shard_map(
        on_device,
        mesh=mesh,
        in_specs=(
            P("bus", None),
            P("bus"),
            P("bus"),
            hourly,
            hourly,
            P(("grp", "bus")),
            hourly,
            hourly,
            hourly,
            P(("grp", "bus")),
            P("grp"),
            P("grp"),
        ),
        out_specs=(hourly, hourly, hourly, P(("grp", "bus"))),
        check_vma=False,
    )
```
